32 devices in a mesh: dp: 2 (over y), ha: 4 (over x, core), wa: 4 (over z).
Axes of the slice: x: 2, y: 2, z: 4, core: 2. Of those that a mesh axis runs over, the one named last changes fastest.
Arguments:
- latents: bfloat16 [2, 64, 32, 1280], P('dp', 'ha', 'wa'), may hold values from -40 to 40
- norm_gain: float32 [1280], replicated, may hold values from 0.5 to 1.5
- norm_shift: float32 [1280], replicated, may hold values from -3 to 3
- conv_weight: bfloat16 [3, 3, 1280, 640], P(None, None, 'dp'), may hold values from -0.0546875 to 0.0546875
- conv_bias: float32 [640], replicated, may hold values from -3 to 3
- cotangent: bfloat16 [2, 64, 32, 640], P('dp', 'ha', 'wa'), may hold values from -12 to 12
Outputs:
- conv_out: bfloat16 [2, 64, 32, 640], P('dp', 'ha', 'wa')
- grad_latents: bfloat16 [2, 64, 32, 1280], P('dp', 'ha', 'wa')
The draws below stay inside these ranges and needn't reach their ends.
All inputs are finite; a program needn't handle non-finite values.
Results may differ from the reference program's by a relative error of at most 0.0044.
Values may be sent and summed in bfloat16 or wider, within the bound.
No kernel may reach another device: no remote copies, remote signals or barrier semaphores. Data moves between devices by JAX's collectives and lax.ppermute only.
A program may use at most 64 MiB of HBM per device.

```python
import math
import jax
import jax.numpy as jnp
from jax import lax

CIN = 1280
COUT = 640
GROUPS = 32
IMAGES = 2
HEIGHT = 64
WIDTH = 32


def draw_latents(key, part):
    keys = jax.random.split(key, 5)
    base = jax.random.normal(keys[0], (IMAGES, HEIGHT, WIDTH, CIN), jnp.float32)
    hpos = jnp.arange(HEIGHT, dtype=jnp.float32) / HEIGHT
    wpos = jnp.arange(WIDTH, dtype=jnp.float32) / WIDTH
    rowscale = jnp.exp(jax.random.uniform(keys[1], (IMAGES, HEIGHT, 1, 1), jnp.float32, -0.6, 0.6) + math.log(3.0) * hpos[None, :, None, None])
    colscale = jnp.exp(jax.random.uniform(keys[2], (IMAGES, 1, WIDTH, 1), jnp.float32, -0.6, 0.6) + math.log(3.0) * wpos[None, None, :, None])
    chanscale = jnp.exp(jax.random.uniform(keys[3], (1, 1, 1, CIN), jnp.float32, 0.0, math.log(10.0)))
    common = jax.random.uniform(keys[4], (IMAGES, 1, 1, CIN), jnp.float32, 0.5, 1.0)
    value = 0.1 * (base + common) * rowscale * colscale * chanscale
    return jnp.clip(value, -40.0, 40.0).astype(jnp.bfloat16)


def draw_cotangent(key, part):
    keys = jax.random.split(jax.random.fold_in(key, 7), 4)
    hpos = jnp.arange(HEIGHT, dtype=jnp.float32) / HEIGHT
    wpos = jnp.arange(WIDTH, dtype=jnp.float32) / WIDTH
    rowpart = jax.random.uniform(keys[1], (IMAGES, HEIGHT, 1, 1), jnp.float32, -0.3, 0.3) + math.log(3.0) * hpos[None, :, None, None]
    colpart = jax.random.uniform(keys[2], (IMAGES, 1, WIDTH, 1), jnp.float32, -0.3, 0.3) + math.log(3.0) * wpos[None, None, :, None]
    spatial = jnp.exp(rowpart + colpart - math.log(3.0))
    noise = jax.random.normal(keys[0], (IMAGES, HEIGHT, WIDTH, COUT), jnp.float32)
    offset = jax.random.normal(keys[3], (IMAGES, 1, 1, COUT), jnp.float32)
    return jnp.clip((noise + offset) * spatial, -12.0, 12.0).astype(jnp.bfloat16)


def levels(rng, shape, cuts, least, high):
    loudness = 1.0
    for dim, blocks in cuts:
        draws = jax.random.uniform(jax.random.fold_in(jax.random.fold_in(rng, 6), dim), (blocks,), jnp.float32, least / len(cuts), high / len(cuts))
        loudness = loudness * jnp.repeat(jnp.exp(draws), shape[dim] // blocks).reshape((-1,) + (1,) * (len(shape) - 1 - dim))
    return loudness


def normal_values(stream_key, shape, spread, limit, shards=(), held_as=jnp.bfloat16):
    factor_of = levels(stream_key, shape, shards, -0.22, 0.18) if shards else 1.0
    result = jax.random.normal(stream_key, shape, jnp.float32) * spread * factor_of
    return jnp.minimum(jnp.maximum(result, -limit), limit).astype(held_as)


def setup_inputs(seed: int = 0) -> dict:
    arg_keys = jax.random.split(jax.random.key(seed), 7)
    latents = draw_latents(jax.random.fold_in(arg_keys[6], 71), 0)
    norm_gain = jnp.clip(jax.random.uniform(arg_keys[1], (CIN,), jnp.float32, 0.5, 1.5), 0.5, 1.5)
    norm_shift = normal_values(arg_keys[2], (CIN,), 0.5, 3.0, (), jnp.float32)
    conv_weight = normal_values(arg_keys[3], (3, 3, CIN, COUT), (9 * CIN) ** -0.5, 0.0546875, ((2, 2),))
    conv_bias = normal_values(arg_keys[4], (COUT,), 0.5, 3.0, (), jnp.float32)
    cotangent = draw_cotangent(jax.random.fold_in(arg_keys[6], 71), 0)
    return dict(latents=latents, norm_gain=norm_gain, norm_shift=norm_shift, conv_weight=conv_weight, conv_bias=conv_bias, cotangent=cotangent)


def convolve(field, kernel):
    return lax.conv_general_dilated(field.astype(jnp.float32), kernel.astype(jnp.float32), (1, 1), ((1, 1), (1, 1)), dimension_numbers=('NHWC', 'HWIO', 'NHWC'), precision=lax.Precision.HIGHEST)

def reference(latents, norm_gain, norm_shift, conv_weight, conv_bias, cotangent):
    images, height, width, chans = latents.shape
    per_group = chans // GROUPS
    xg = latents.astype(jnp.float32).reshape(images, height, width, GROUPS, per_group)
    group_mean = lax.optimization_barrier(jnp.mean(xg, axis=(1, 2, 4), keepdims=True))
    centered_input = xg - group_mean
    var = lax.optimization_barrier(jnp.mean(centered_input * centered_input, axis=(1, 2, 4), keepdims=True))
    inverse_deviation = lax.rsqrt(var + 1e-05)
    normalized_input = centered_input * inverse_deviation
    group_gains = norm_gain.reshape(GROUPS, per_group)
    group_shifts = norm_shift.reshape(GROUPS, per_group)
    preactivation_value = normalized_input * group_gains + group_shifts
    sig = jax.nn.sigmoid(preactivation_value)
    act = (preactivation_value * sig).astype(jnp.bfloat16).reshape(images, height, width, chans)
    conv_out = (convolve(act, conv_weight) + conv_bias).astype(jnp.bfloat16)
    flipped = jnp.transpose(jnp.flip(conv_weight, (0, 1)), (0, 1, 3, 2))
    grad_act = convolve(cotangent, flipped).reshape(images, height, width, GROUPS, per_group)
    normalized_gradient = grad_act * sig * (1.0 + preactivation_value * (1.0 - sig)) * group_gains
    first_moment = lax.optimization_barrier(jnp.mean(normalized_gradient, axis=(1, 2, 4), keepdims=True))
    second_moment = lax.optimization_barrier(jnp.mean(normalized_gradient * normalized_input, axis=(1, 2, 4), keepdims=True))
    input_gradient = inverse_deviation * (normalized_gradient - first_moment - normalized_input * second_moment)
    return (conv_out, input_gradient.reshape(images, height, width, chans).astype(jnp.bfloat16))
```

```python
import functools

import jax
import jax.numpy as jnp
from jax import lax
from jax.experimental import pallas as pl
from jax.experimental.pallas import tpu as pltpu
from jax.sharding import PartitionSpec as P

GROUPS = 32
EPS = 1e-05
F32 = jnp.float32
BF16 = jnp.bfloat16


def swap(values, axis, partner):
    count = lax.axis_size(axis)
    pairs = [(i, partner(i) % count) for i in range(count)]
    return [lax.ppermute(v, axis, pairs) for v in values]


def near(i):
    return i ^ 1


def across(i):
    return i - 1 if i % 2 == 0 else i + 1


def merged(stats, other, n):
    delta = other[0] - stats[0]
    return jnp.stack([stats[0] + 0.5 * delta, stats[1] + other[1] + (0.5 * n) * delta * delta])


def conv_windows(padded_ref, windows_ref, images, rows, cols):
    chans = windows_ref.shape[3]
    for kx in range(3):
        windows_ref[kx] = padded_ref[:, kx : kx + cols, :].reshape(rows + 2, images * cols, chans).astype(BF16)


def expanded(values, chans):
    groups = values.shape[-1]
    per_group = chans // groups
    chan = lax.broadcasted_iota(jnp.int32, (groups, chans), 1)
    group = lax.broadcasted_iota(jnp.int32, (groups, chans), 0)
    member = ((chan >= group * per_group) & (chan < (group + 1) * per_group)).astype(F32)
    return jnp.dot(values, member, precision=lax.Precision.HIGHEST, preferred_element_type=F32)


def gathered(values, groups):
    chans = values.shape[-1]
    per_group = chans // groups
    chan = lax.broadcasted_iota(jnp.int32, (chans, groups), 0)
    group = lax.broadcasted_iota(jnp.int32, (chans, groups), 1)
    member = ((chan >= group * per_group) & (chan < (group + 1) * per_group)).astype(F32)
    return jnp.dot(values, member, precision=lax.Precision.HIGHEST, preferred_element_type=F32)


def backward_kernel(
    images, rows, cols, count,
    inside_ref, stats_ref, gain_ref, shift_ref, x_ref, cot_ref, w_ref,
    gx_own_ref, gx_other_ref, moments_ref, act_ref,
    padded_ref, pad_cot_ref, windows_ref,
):
    chans = x_ref.shape[2]
    outs = cot_ref.shape[2]
    groups = stats_ref.shape[2]
    pix = rows * images * cols
    pad_cot_ref[:, : cols + 2, :] = cot_ref[...].astype(F32)
    conv_windows(pad_cot_ref, windows_ref, images, rows, cols)
    total = None
    for ky in range(3):
        for kx in range(3):
            window = windows_ref[kx, ky : ky + rows].reshape(pix, outs)
            term = lax.dot_general(
                w_ref[2 - ky, 2 - kx], window, (((1,), (1,)), ((), ())), preferred_element_type=F32
            )
            total = term if total is None else total + term
    grad_act = total.T.reshape(rows, images, cols, chans)
    mean = expanded(stats_ref[0], chans)
    inv = expanded(lax.rsqrt(stats_ref[1] / count + EPS), chans)
    gain = gain_ref[...]
    shift = shift_ref[...]
    xhat = (x_ref[...].astype(F32).reshape(rows + 2, images, cols + 2, chans) - mean[None, :, None, :]) * inv[None, :, None, :]
    z = xhat * gain.reshape(1, 1, 1, chans) + shift.reshape(1, 1, 1, chans)
    sig = jax.nn.sigmoid(z)
    row = lax.broadcasted_iota(jnp.int32, z.shape, 0)
    col = lax.broadcasted_iota(jnp.int32, z.shape, 2)
    keep = (
        ((row > 0) | (inside_ref[0] > 0))
        & ((row < rows + 1) | (inside_ref[1] > 0))
        & ((col > 0) | (inside_ref[2] > 0))
        & ((col < cols + 1) | (inside_ref[3] > 0))
    )
    act = jnp.where(keep, z * sig, 0.0)
    padded_ref[:, : cols + 2, :] = act.reshape((rows + 2) * images, cols + 2, chans)
    conv_windows(padded_ref, act_ref, images, rows, cols)
    slope = sig * (1.0 + z * (1.0 - sig)) * gain.reshape(1, 1, 1, chans)
    padded_ref[:, : cols + 2, :] = slope.reshape((rows + 2) * images, cols + 2, chans)
    slope = padded_ref[images : (rows + 1) * images, 1 : cols + 1, :].reshape(rows, images, cols, chans)
    padded_ref[:, : cols + 2, :] = xhat.reshape((rows + 2) * images, cols + 2, chans)
    xhat = padded_ref[images : (rows + 1) * images, 1 : cols + 1, :].reshape(rows, images, cols, chans)
    gx = grad_act * slope
    gx_own_ref[...] = gx[:, 0]
    for k in range(1, images):
        gx_other_ref[k - 1] = gx[:, k].astype(BF16)
    first = jnp.sum(gx, axis=(0, 2))
    second = jnp.sum(gx * xhat, axis=(0, 2))
    moments_ref[0] = gathered(first, groups)
    moments_ref[1] = gathered(second, groups)


def forward_kernel(images, rows, cols, act_ref, w_ref, own_ref, other_ref):
    chans = act_ref.shape[3]
    outs = w_ref.shape[3]
    pix = rows * images * cols
    total = None
    for ky in range(3):
        for kx in range(3):
            window = act_ref[kx, ky : ky + rows].reshape(pix, chans)
            term = jnp.dot(window, w_ref[ky, kx], preferred_element_type=F32)
            total = term if total is None else total + term
    total = total.reshape(rows, images, cols, outs)
    own_ref[...] = total[:, 0]
    for k in range(1, images):
        other_ref[k - 1] = total[:, k].astype(BF16)


def call(kernel, outs, scratch, name, *operands, smem=0):
    vmem = pl.BlockSpec(memory_space=pltpu.VMEM)
    return pl.pallas_call(
        kernel,
        out_shape=outs,
        in_specs=[pl.BlockSpec(memory_space=pltpu.SMEM)] * smem + [vmem] * (len(operands) - smem),
        out_specs=[vmem] * len(outs),
        scratch_shapes=scratch,
        compiler_params=pltpu.CompilerParams(vmem_limit_bytes=40 * 2**20),
        name=name,
    )(*operands)


def edges_exchanged(axis, first, last, stats, n):
    count = lax.axis_size(axis)
    index = lax.axis_index(axis)
    even = index % 2 == 0
    pick = lambda a, b: [jnp.where(even, x, y) for x, y in zip(a, b)]
    got_near = swap(pick(last, first) + [stats], axis, near)
    stats, n = merged(stats, got_near[-1], n), 2 * n
    got_across = swap(pick(first, last) + ([stats] if count == 4 else []), axis, across)
    if count == 4:
        stats, n = merged(stats, got_across.pop(), n), 2 * n
    else:
        step = 2
        while step < count:
            (other,) = swap([stats], axis, lambda i: i ^ step)
            stats, n = merged(stats, other, n), 2 * n
            step *= 2
    lower = [jnp.where(index > 0, v, jnp.zeros_like(v)) for v in pick(got_across, got_near)]
    upper = [jnp.where(index < count - 1, v, jnp.zeros_like(v)) for v in pick(got_near[:-1], got_across)]
    return lower, upper, stats, n


def summed(value, axis):
    count = lax.axis_size(axis)
    step = 1
    while step < count:
        (other,) = swap([value], axis, lambda i: i ^ step)
        value = value + other
        step *= 2
    return value


def body(latents, norm_gain, norm_shift, conv_weight, conv_bias, cotangent):
    _, rows, cols, cin = latents.shape
    outs = cotangent.shape[3]
    chans = conv_weight.shape[2]
    parts = lax.axis_size("dp")
    me = lax.axis_index("dp")
    groups = GROUPS * chans // cin
    per_group = cin // GROUPS
    tiles = lax.axis_size("ha") * lax.axis_size("wa")
    n_local = rows * cols * per_group
    count = n_local * tiles
    x, cot = latents[0], cotangent[0]

    def to_peer(k):
        return lambda i: i + k

    def shard_of(a, axis, k, size):
        return lax.dynamic_slice_in_dim(a, (me + k) % parts * size, size, axis)

    xg = x.astype(F32).reshape(rows, cols, GROUPS, per_group)
    local_mean = jnp.mean(xg, axis=(0, 1, 3))
    centered = xg - local_mean[None, None, :, None]
    local = jnp.stack([local_mean, jnp.sum(centered * centered, axis=(0, 1, 3))])

    stats = [shard_of(local, 1, 0, groups)]
    x_all, cot_all = [shard_of(x, 2, 0, chans)], [cot]
    x_edges, cot_edges = [], []
    def edges(t):
        return jnp.concatenate([t[:1], t[-1:]], 0), jnp.concatenate([t[:, :1], t[:, -1:]], 1)
    x_edges.append(edges(x_all[0]))
    cot_edges.append(edges(cot))
    for k in range(1, parts):
        mine = shard_of(x, 2, k, chans)
        xr, xc = edges(mine)
        cr, cc = cot_edges[0]
        got = swap([shard_of(local, 1, k, groups), xr, cr, xc, cc, cot, mine], "dp", to_peer(k))
        stats.append(got[0])
        x_edges.append((got[1], got[3]))
        cot_edges.append((got[2], got[4]))
        cot_all.append(got[5])
        x_all.append(got[6])
    stats = jnp.stack(stats, 1)
    stack = lambda e, j, i, axis: jnp.stack([lax.index_in_dim(v[j], i, axis, keepdims=False) for v in e], axis)

    top = [stack(e, 0, 0, 0) for e in (x_edges, cot_edges)]
    bottom = [stack(e, 0, 1, 0) for e in (x_edges, cot_edges)]
    above, below, stats, n = edges_exchanged("ha", top, bottom, stats, n_local)
    cols_of = lambda e, i: jnp.stack([lax.index_in_dim(v[1], i, 1, keepdims=False) for v in e], 1)
    left = [jnp.concatenate([a[None, :, 0], cols_of(e, 0), b[None, :, 0]], 0) for a, b, e in zip(above, below, (x_edges, cot_edges))]
    right = [jnp.concatenate([a[None, :, -1], cols_of(e, 1), b[None, :, -1]], 0) for a, b, e in zip(above, below, (x_edges, cot_edges))]
    before, after, stats, n = edges_exchanged("wa", left, right, stats, n)

    def padded(tiles_, a, b, l, r):
        t = jnp.stack(tiles_, 1)
        t = jnp.concatenate([a[None], t, b[None]], 0)
        t = jnp.concatenate([l[:, :, None], t, r[:, :, None]], 2)
        return t.reshape((rows + 2) * parts, cols + 2, t.shape[3])

    x_pad = padded(x_all, above[0], below[0], before[0], after[0])
    cot_pad = padded(cot_all, above[1], below[1], before[1], after[1])
    at = lambda axis: (lax.axis_index(axis) > 0, lax.axis_index(axis) < lax.axis_size(axis) - 1)
    inside = jnp.stack(at("ha") + at("wa")).astype(jnp.int32)
    gain = shard_of(norm_gain, 0, 0, chans)[None]
    shift = shard_of(norm_shift, 0, 0, chans)[None]
    sds = jax.ShapeDtypeStruct
    gx_own, gx_other, moments, act = call(
        functools.partial(backward_kernel, parts, rows, cols, float(count)),
        [
            sds((rows, cols, chans), F32),
            sds((parts - 1, rows, cols, chans), BF16),
            sds((2, parts, groups), F32),
            sds((3, rows + 2, parts * cols, chans), BF16),
        ],
        [
            pltpu.VMEM(((rows + 2) * parts, cols + 8, chans), F32),
            pltpu.VMEM(((rows + 2) * parts, cols + 8, outs), F32),
            pltpu.VMEM((3, rows + 2, parts * cols, outs), BF16),
        ],
        "conv_backward",
        inside, stats, gain, shift, x_pad, cot_pad, conv_weight,
        smem=1,
    )
    conv_own, conv_other = call(
        functools.partial(forward_kernel, parts, rows, cols),
        [sds((rows, cols, outs), F32), sds((parts - 1, rows, cols, outs), BF16)],
        [],
        "conv_forward",
        act, conv_weight,
    )

    small = jnp.concatenate([moments, stats], 0)
    whole = jnp.zeros((4, GROUPS), F32)
    place = lambda a, v, k, axis, size: lax.dynamic_update_slice_in_dim(a, v, (me + k) % parts * size, axis)
    whole = place(whole, small[:, 0], 0, 1, groups)
    gx = place(jnp.zeros((rows, cols, cin), F32), gx_own, 0, 2, chans)
    conv = conv_own
    for k in range(1, parts):
        got = swap([small[:, k], gx_other[k - 1], conv_other[k - 1]], "dp", to_peer(-k))
        whole = place(whole, got[0], k, 1, groups)
        gx = place(gx, got[1].astype(F32), k, 2, chans)
        conv = conv + got[2].astype(F32)
    conv_out = (conv + conv_bias).astype(BF16)
    sums = summed(summed(whole[:2], "ha"), "wa") / count
    wide = lambda v: jnp.broadcast_to(v[:, None], (GROUPS, per_group)).reshape(cin)
    inv = lax.rsqrt(whole[3] / count + EPS)
    xhat = (x.astype(F32) - wide(whole[2])) * wide(inv)
    grad = wide(inv) * (gx - wide(sums[0]) - xhat * wide(sums[1]))
    return conv_out[None], grad.astype(BF16)[None]


def solution(mesh):
    tile = P("dp", "ha", "wa", None)
    return jax.shard_map(
        body,
        mesh=mesh,
        in_specs=(tile, P(), P(), P(None, None, "dp", None), P(), tile),
        out_specs=(tile, tile),
        check_vma=False,
    )
```

```python
import functools

import jax
import jax.numpy as jnp
from jax import lax
from jax.experimental import pallas as pl
from jax.experimental.pallas import tpu as pltpu
from jax.sharding import PartitionSpec as P

GROUPS = 32
EPS = 1e-05
F32 = jnp.float32
BF16 = jnp.bfloat16

ME, EVEN_H, EVEN_W, UP, DOWN, LEFT, RIGHT = range(7)


def exchange(value, axis, partner, ends=True):
    count = lax.axis_size(axis)
    pairs = [(i, partner(i) % count) for i in range(count)]
    if not ends:
        pairs = [(i, j) for i, j in pairs if abs(i - j) == 1]
    return lax.ppermute(value, axis, pairs)


def near(i):
    return i ^ 1


def across(i):
    return i - 1 if i % 2 == 0 else i + 1


def merged(stats, other, n):
    delta = other[:, :1] - stats[:, :1]
    return jnp.concatenate([stats[:, :1] + 0.5 * delta, stats[:, 1:] + other[:, 1:] + (0.5 * n) * delta * delta], 1)


def packed(strips, stats):
    high = lax.reduce_precision(stats, 8, 7)
    middle = lax.reduce_precision(stats - high, 8, 7)
    low = lax.reduce_precision(stats - high - middle, 8, 7)
    rows = jnp.concatenate([high, middle, low], 1).astype(BF16)
    rows = jnp.pad(rows, ((0, 0), (0, 0), (0, strips.shape[2] - rows.shape[2])))
    return jnp.concatenate([strips, rows], 1)


def unpacked(pack, r, groups):
    rows = pack[:, r : r + 6, :groups].astype(F32)
    return pack[:, :r], rows[:, :2] + rows[:, 2:4] + rows[:, 4:]


def members(groups, chans, dim):
    per_group = chans // groups
    shape = (groups, chans) if dim else (chans, groups)
    chan = lax.broadcasted_iota(jnp.int32, shape, dim)
    group = lax.broadcasted_iota(jnp.int32, shape, 1 - dim)
    return ((chan >= group * per_group) & (chan < (group + 1) * per_group)).astype(F32)


def three_parts(a):
    high = a.astype(BF16)
    rest = a - high.astype(F32)
    middle = rest.astype(BF16)
    return high, middle, (rest - middle.astype(F32)).astype(BF16)


def exact_dot(a, b):
    rows = a.shape[0]
    parts = jnp.concatenate([p.astype(F32) for p in three_parts(a)], 0).astype(BF16)
    sums = jnp.dot(parts, b.astype(BF16), preferred_element_type=F32)
    return sums[:rows] + sums[rows : 2 * rows] + sums[2 * rows :]


def expanded(values, chans):
    return exact_dot(values, members(values.shape[-1], chans, 1))


def gathered(values, groups):
    return exact_dot(values, members(groups, values.shape[-1], 0))


def shard_of(pieces, shard):
    value = pieces[0]
    for i in range(1, len(pieces)):
        value = jnp.where(shard == i, pieces[i], value)
    return value


def first_kernel(parts, groups, info_ref, x_hbm, cot_hbm, *refs):
    out_refs, (x_ref, cot_ref, sems) = refs[:parts], refs[parts:]
    rows, cols, cin = x_ref.shape
    chans = cin // parts
    n = rows * cols * (chans // groups)
    x_copy = pltpu.make_async_copy(x_hbm, x_ref, sems.at[0])
    cot_copy = pltpu.make_async_copy(cot_hbm, cot_ref, sems.at[1])
    x_copy.start()
    cot_copy.start()
    me = info_ref[ME]
    even_h = info_ref[EVEN_H] > 0
    x_copy.wait()
    shards = [x_ref[:, :, s * chans : (s + 1) * chans].astype(F32) for s in range(parts)]
    stats = []
    for x in shards:
        flat = x.reshape(rows * cols, chans)
        mean = gathered(jnp.sum(flat, axis=0, keepdims=True), groups) / n
        centered = flat - expanded(mean, chans)
        squares = gathered(jnp.sum(centered * centered, axis=0, keepdims=True), groups)
        stats.append(jnp.concatenate([p.astype(F32) for p in three_parts(jnp.concatenate([mean, squares], 0))], 0))
    cot_copy.wait()
    ends = lambda t: (jnp.where(even_h, t[rows - 1], t[0]), jnp.where(even_h, t[0], t[rows - 1]))
    cot_ends = ends(cot_ref[...].astype(F32))
    x_ends = [ends(x) for x in shards]
    for k in range(parts):
        shard = lax.rem(me + k, parts)
        out_refs[k][: 2 * cols, :chans] = jnp.concatenate([shard_of([e[i] for e in x_ends], shard) for i in range(2)], 0).astype(BF16)
        out_refs[k][: 2 * cols, chans:] = jnp.concatenate(cot_ends, 0).astype(BF16)
        out_refs[k][2 * cols :, :] = jnp.zeros((8, out_refs[k].shape[1]), BF16)
        out_refs[k][2 * cols : 2 * cols + 6, :groups] = shard_of(stats, shard).astype(BF16)


def second_kernel(parts, info_ref, x_ref, cot_ref, *refs):
    out_refs = refs[parts - 1 :]
    rows, cols, cin = x_ref.shape
    chans = cin // parts
    me = info_ref[ME]
    even_w = info_ref[EVEN_W] > 0

    def ends(t):
        first, last = t[:, 0, :], t[:, cols - 1, :]
        return jnp.concatenate([jnp.where(even_w, last, first), jnp.where(even_w, first, last)], 0).astype(BF16)

    cot_ends = ends(cot_ref[...].astype(F32))
    shards = [x_ref[:, :, s * chans : (s + 1) * chans].astype(F32) for s in range(parts)]
    for k in range(parts):
        tile_ref, ends_ref = out_refs[2 * k : 2 * k + 2]
        x = shard_of(shards, lax.rem(me + k, parts))
        tile_ref[...] = x.astype(BF16)
        ends_ref[:, :chans] = ends(x)
        ends_ref[:, chans:] = cot_ends


def load_kernel(w_hbm, after_ref, w_ref, sem):
    copy = pltpu.make_async_copy(w_hbm, w_ref, sem)
    copy.start()
    copy.wait()


def halos(info_ref, near_h, across_h, near_w, across_w, lanes):
    even_h = info_ref[EVEN_H] > 0
    even_w = info_ref[EVEN_W] > 0
    rows = near_w.shape[1] - 2

    def strips(k):
        a, b = near_h[k, :, lanes].astype(F32), across_h[k, :, lanes].astype(F32)
        above, below = jnp.where(even_h, b, a), jnp.where(even_h, a, b)
        c, d = near_w[k, :, lanes].astype(F32), across_w[k, :, lanes].astype(F32)
        before, after = jnp.where(even_w, d, c), jnp.where(even_w, c, d)

        def ordered(t):
            head, tail = t[0:1], t[rows + 1 : rows + 2]
            return jnp.where(even_h, tail, head), t[1 : rows + 1], jnp.where(even_h, head, tail)

        return above, below, ordered(before), ordered(after)

    return strips


def windows(padded_ref, windows_ref, k_all, cols):
    for kx in range(3):
        view = padded_ref[:, :, kx : kx + cols, :]
        windows_ref[kx] = view.reshape(view.shape[0], k_all * cols, view.shape[3]).astype(BF16)


def backward_kernel(parts, info_ref, *refs):
    tiles, (near_h, across_h, near_w, across_w, w_ref, grad_ref, padded_ref, windows_ref) = refs[:parts], refs[parts:]
    rows, cols, outs = tiles[0].shape
    chans = w_ref.shape[2]
    strips = halos(info_ref, near_h, across_h, near_w, across_w, slice(chans, chans + outs))
    for k in range(parts):
        above, below, before, after = strips(k)
        padded_ref[1 : rows + 1, k, 1 : cols + 1, :] = tiles[k][...].astype(F32)
        padded_ref[0, k, 1 : cols + 1, :] = above
        padded_ref[rows + 1, k, 1 : cols + 1, :] = below
        for at, (top, mid, bottom) in ((0, before), (cols + 1, after)):
            padded_ref[0, k, at : at + 1, :] = top
            padded_ref[1 : rows + 1, k, at, :] = mid
            padded_ref[rows + 1, k, at : at + 1, :] = bottom
    windows(padded_ref, windows_ref, parts, cols)
    total = None
    for ky in range(3):
        for kx in range(3):
            window = windows_ref[kx, ky : ky + rows].reshape(rows * parts * cols, outs)
            term = lax.dot_general(w_ref[2 - ky, 2 - kx], window, (((1,), (1,)), ((), ())), preferred_element_type=F32)
            total = term if total is None else total + term
    grad_ref[...] = total.T.reshape(rows, parts, cols, chans)


def terms_kernel(parts, count, info_ref, *refs):
    tiles = refs[:parts]
    near_h, across_h, near_w, across_w, stats_ref, gain_ref, shift_ref, grad_ref = refs[parts : parts + 8]
    moments_ref, gx_own_ref, gx_other_ref, windows_ref, padded_ref = refs[parts + 8 :]
    rows, cols, _ = tiles[0].shape
    chans = grad_ref.shape[3]
    groups = stats_ref.shape[2]
    lanes = slice(0, chans)
    stats = jnp.concatenate([stats_ref[:, 0], stats_ref[:, 1]], 0)
    strips = halos(info_ref, near_h, across_h, near_w, across_w, lanes)
    wide = expanded(jnp.concatenate([stats[:parts], lax.rsqrt(stats[parts:] / count + EPS)], 0), chans)
    means, invs = wide[:parts], wide[parts:]
    gain, shift = gain_ref[...], shift_ref[...]
    up, down, left, right = (info_ref[i] > 0 for i in (UP, DOWN, LEFT, RIGHT))
    firsts, seconds = [], []
    for k in range(parts):
        mean, inv = means[k : k + 1], invs[k : k + 1]

        def act_of(t, inside):
            z = (t - mean) * inv * gain + shift
            return jnp.where(inside, z * jax.nn.sigmoid(z), 0.0)

        above, below, before, after = strips(k)
        xhat = (tiles[k][...].astype(F32) - mean[None]) * inv[None]
        z = xhat * gain[None] + shift[None]
        sig = jax.nn.sigmoid(z)
        padded_ref[1 : rows + 1, k, 1 : cols + 1, :] = z * sig
        padded_ref[0, k, 1 : cols + 1, :] = act_of(above, up)
        padded_ref[rows + 1, k, 1 : cols + 1, :] = act_of(below, down)
        for at, (top, mid, bottom), side in ((0, before, left), (cols + 1, after, right)):
            padded_ref[0, k, at : at + 1, :] = act_of(top, side & up)
            padded_ref[1 : rows + 1, k, at, :] = act_of(mid, side)
            padded_ref[rows + 1, k, at : at + 1, :] = act_of(bottom, side & down)
        gx = grad_ref[:, k] * sig * (1.0 + z * (1.0 - sig)) * gain[None]
        if k == 0:
            gx_own_ref[...] = gx
        else:
            gx_other_ref[k - 1] = gx.astype(BF16)
        firsts.append(jnp.sum(gx.reshape(rows * cols, chans), axis=0, keepdims=True))
        seconds.append(jnp.sum((gx * xhat).reshape(rows * cols, chans), axis=0, keepdims=True))
    sums = gathered(jnp.concatenate(firsts + seconds, 0), groups)
    moments_ref[0] = sums[:parts]
    moments_ref[1] = sums[parts:]
    moments_ref[2] = stats[:parts]
    moments_ref[3] = stats[parts:]
    windows(padded_ref, windows_ref, parts, cols)


def forward_kernel(parts, info_ref, windows_ref, w_ref, conv_own_ref, conv_other_ref):
    rows, cols, _ = conv_own_ref.shape
    chans, outs = w_ref.shape[2:]
    total = None
    for ky in range(3):
        for kx in range(3):
            window = windows_ref[kx, ky : ky + rows].reshape(rows * parts * cols, chans)
            term = jnp.dot(window, w_ref[ky, kx], preferred_element_type=F32)
            total = term if total is None else total + term
    total = total.reshape(rows, parts, cols, outs)
    conv_own_ref[...] = total[:, 0]
    for k in range(1, parts):
        conv_other_ref[k - 1] = total[:, k].astype(BF16)


def finish_kernel(parts, count, info_ref, x_ref, stats_ref, sums_ref, bias_ref, gx_own_ref, conv_own_ref, *refs):
    gx_refs, conv_refs = refs[: parts - 1], refs[parts - 1 : 2 * parts - 2]
    conv_ref, grad_ref = refs[2 * parts - 2 :]
    cin = x_ref.shape[2]
    chans = cin // parts
    conv = conv_own_ref[...] + bias_ref[...][None]
    for r in conv_refs:
        conv = conv + r[...].astype(F32)
    conv_ref[...] = conv.astype(BF16)
    wide = jnp.concatenate([stats_ref[0:1], lax.rsqrt(stats_ref[1:2] / count + EPS), sums_ref[...] / count], 0)
    wide = expanded(wide, cin)
    mean, inv, first, second = (wide[i : i + 1] for i in range(4))
    me = info_ref[ME]
    for s in range(parts):
        at = slice(s * chans, (s + 1) * chans)
        gx = gx_own_ref[...]
        for k in range(1, parts):
            gx = jnp.where(lax.rem(me + k, parts) == s, gx_refs[k - 1][...].astype(F32), gx)
        xhat = (x_ref[:, :, at].astype(F32) - mean[None, :, at]) * inv[None, :, at]
        grad = inv[None, :, at] * (gx - first[None, :, at] - xhat * second[None, :, at])
        grad_ref[:, :, at] = grad.astype(BF16)


def call(kernel, name, outs, operands, scratch=(), in_hbm=(), limit=28):
    spec = lambda i: pl.BlockSpec(memory_space=pltpu.HBM if i in in_hbm else pltpu.SMEM if i == 0 else pltpu.VMEM)
    return pl.pallas_call(
        kernel,
        out_shape=outs,
        in_specs=[spec(i) for i in range(len(operands))],
        out_specs=[pl.BlockSpec(memory_space=pltpu.VMEM)] * len(outs),
        scratch_shapes=scratch,
        compiler_params=pltpu.CompilerParams(vmem_limit_bytes=limit * 2**20),
        name=name,
    )(*operands)


def tied(value, *others):
    for other in others:
        value = value + 0.0 * other[0, :1, : value.shape[-1]].astype(F32)
    return value


def stats_rounds(axis):
    count = lax.axis_size(axis)
    if count == 4:
        return [near, lambda i: i ^ 2]
    return [functools.partial(lambda step, i: i ^ step, 2**j) for j in range(count.bit_length() - 1)]


def body(latents, norm_gain, norm_shift, conv_weight, conv_bias, cotangent):
    _, rows, cols, cin = latents.shape
    outs = cotangent.shape[3]
    chans = conv_weight.shape[2]
    parts = lax.axis_size("dp")
    me = lax.axis_index("dp")
    groups = GROUPS * chans // cin
    both = chans + outs
    n = rows * cols * (cin // GROUPS)
    count = float(n * lax.axis_size("ha") * lax.axis_size("wa"))
    x, cot = latents[0], cotangent[0]
    sds = jax.ShapeDtypeStruct
    where = [lax.axis_index(a) for a in ("ha", "wa")]
    last = [lax.axis_size(a) - 1 for a in ("ha", "wa")]
    info = jnp.stack(
        [me, where[0] % 2 == 0, where[1] % 2 == 0, where[0] > 0, where[0] < last[0], where[1] > 0, where[1] < last[1]]
    ).astype(jnp.int32)
    gain = lax.dynamic_slice_in_dim(norm_gain, me * chans, chans, 0)[None]
    shift = lax.dynamic_slice_in_dim(norm_shift, me * chans, chans, 0)[None]

    *first, x, cot = call(
        functools.partial(first_kernel, parts, groups),
        "first",
        [sds((2 * cols + 8, both), BF16)] * parts + [sds(x.shape, BF16), sds(cot.shape, BF16)],
        [info, x, cot],
        [pltpu.SemaphoreType.DMA((2,))],
        in_hbm=(1, 2),
        limit=40,
    )
    peers = [[(i, (i + k) % parts) for i in range(parts)] for k in range(1, parts)]
    from_peers = lambda values: [lax.ppermute(v, "dp", pairs) for v, pairs in zip(values, peers)]
    got = from_peers(first[1:])
    ends_h, stats = unpacked(jnp.stack([first[0], *got], 0), 2 * cols, groups)
    second = call(
        functools.partial(second_kernel, parts),
        "second",
        [sds((rows, cols, chans), BF16), sds((2 * rows, both), BF16)] * parts,
        [info, x, cot, *got],
    )
    ends_w = jnp.stack([second[1], *from_peers(second[3::2])], 0)
    cot_tiles = [cot, *from_peers([cot] * (parts - 1))]
    x_tiles = [second[0], *from_peers(second[2::2])]

    def reduced(stats, n, axis, pairings):
        for partner in pairings:
            stats, n = merged(stats, exchange(stats, axis, partner), n), 2 * n
        return stats, n

    rounds_h, rounds_w = stats_rounds("ha"), stats_rounds("wa")
    near_h, other = unpacked(exchange(packed(ends_h[:, :cols], stats), "ha", near), cols, groups)
    stats, n = merged(stats, other, n), 2 * n
    if lax.axis_size("ha") == 4:
        across_h, other = unpacked(exchange(packed(ends_h[:, cols:], tied(stats, near_h)), "ha", across), cols, groups)
        stats, n = merged(stats, other, n), 2 * n
    else:
        across_h = exchange(ends_h[:, cols:], "ha", across)
        stats, n = reduced(stats, n, "ha", rounds_h[1:])
    across_h = jnp.where((where[0] > 0) & (where[0] < last[0]), across_h, jnp.zeros_like(across_h))

    def column(part, end):
        corner = lambda t: jnp.where(end, t[:, cols - 1 :], t[:, :1])
        return jnp.concatenate([corner(near_h), part, corner(across_h)], 1)

    even_w = where[1] % 2 == 0
    pack = packed(column(ends_w[:, :rows], even_w), stats)
    (weight,) = call(
        load_kernel,
        "load",
        [sds(conv_weight.shape, BF16)],
        [conv_weight, stats],
        [pltpu.SemaphoreType.DMA],
        in_hbm=(0,),
        limit=40,
    )
    near_w, other = unpacked(exchange(pack, "wa", near), rows + 2, groups)
    across_w = exchange(column(ends_w[:, rows:], ~even_w), "wa", across, ends=False)
    stats, n = merged(stats, other, n), 2 * n
    stats, n = reduced(tied(stats, weight[0], *cot_tiles[1:]), n, "wa", rounds_w[1:])

    strips = [near_h, across_h, near_w, across_w]
    padded = lambda depth: pltpu.VMEM((rows + 2, parts, cols + 8, depth), F32)
    shifted = (3, rows + 2, parts * cols)
    (grad_act,) = call(
        functools.partial(backward_kernel, parts),
        "conv_backward",
        [sds((rows, parts, cols, chans), F32)],
        [info, *cot_tiles, *strips, weight],
        [padded(outs), pltpu.VMEM((*shifted, outs), BF16)],
    )
    small, gx_own, gx_other, act = call(
        functools.partial(terms_kernel, parts, count),
        "terms",
        [
            sds((4, parts, groups), F32),
            sds((rows, cols, chans), F32),
            sds((parts - 1, rows, cols, chans), BF16),
            sds((*shifted, chans), BF16),
        ],
        [info, *x_tiles, *strips, stats, gain, shift, grad_act],
        [padded(chans)],
    )
    conv_own, conv_other = call(
        functools.partial(forward_kernel, parts),
        "conv_forward",
        [sds((rows, cols, outs), F32), sds((parts - 1, rows, cols, outs), BF16)],
        [info, act, weight],
    )

    place = lambda a, v, k: lax.dynamic_update_slice_in_dim(a, v, (me + k) % parts * groups, 1)
    whole = place(jnp.zeros((4, GROUPS), F32), small[:, 0], 0)
    gx, conv = [], []
    for k in range(1, parts):
        pairs = [(i, (i - k) % parts) for i in range(parts)]
        whole = place(whole, lax.ppermute(small[:, k], "dp", pairs), k)
        gx.append(lax.ppermute(gx_other[k - 1], "dp", pairs))
        conv.append(lax.ppermute(conv_other[k - 1], "dp", pairs))
    sums = whole[:2]
    for axis, pairings in (("ha", rounds_h), ("wa", rounds_w)):
        for partner in pairings:
            sums = sums + exchange(sums, axis, partner)
    conv_out, grad = call(
        functools.partial(finish_kernel, parts, count),
        "finish",
        [sds((rows, cols, outs), BF16), sds((rows, cols, cin), BF16)],
        [info, x, whole[2:], sums, conv_bias[None], gx_own, conv_own, *gx, *conv],
    )
    return conv_out[None], grad[None]


def solution(mesh):
    tile = P("dp", "ha", "wa", None)
    return jax.shard_map(
        body,
        mesh=mesh,
        in_specs=(tile, P(), P(), P(None, None, "dp", None), P(), tile),
        out_specs=(tile, tile),
        check_vma=False,
    )
```

```python
import functools

import jax
import jax.numpy as jnp
from jax import lax
from jax.experimental import pallas as pl
from jax.experimental.pallas import tpu as pltpu
from jax.sharding import PartitionSpec as P

GROUPS = 32
EPS = 1e-05
F32 = jnp.float32
BF16 = jnp.bfloat16

ME, EVEN_H, EVEN_W, UP, DOWN, LEFT, RIGHT = range(7)


def exchange(value, axis, partner, ends=True):
    count = lax.axis_size(axis)
    pairs = [(i, partner(i) % count) for i in range(count)]
    if not ends:
        pairs = [(i, j) for i, j in pairs if abs(i - j) == 1]
    return lax.ppermute(value, axis, pairs)


def near(i):
    return i ^ 1


def across(i):
    return i - 1 if i % 2 == 0 else i + 1


def merged(stats, other, n):
    half = stats.shape[1] // 2
    delta = other[:, :half] - stats[:, :half]
    return jnp.concatenate([stats[:, :half] + 0.5 * delta, stats[:, half:] + other[:, half:] + (0.5 * n) * delta * delta], 1)


def packed(strips, stats):
    high = lax.reduce_precision(stats, 8, 7)
    middle = lax.reduce_precision(stats - high, 8, 7)
    low = lax.reduce_precision(stats - high - middle, 8, 7)
    rows = jnp.concatenate([high, middle, low], 0).astype(BF16)
    rows = jnp.pad(rows, ((0, 0), (0, strips[0].shape[1] - rows.shape[1])))
    return jnp.concatenate([*strips, rows], 0)


def unpacked(pack, r, size):
    rows = pack[r : r + 3, :size].astype(F32)
    return rows[:1] + rows[1:2] + rows[2:]


def members(groups, chans, dim):
    per_group = chans // groups
    shape = (groups, chans) if dim else (chans, groups)
    chan = lax.broadcasted_iota(jnp.int32, shape, dim)
    group = lax.broadcasted_iota(jnp.int32, shape, 1 - dim)
    return ((chan >= group * per_group) & (chan < (group + 1) * per_group)).astype(F32)


def three_parts(a):
    high = a.astype(BF16)
    rest = a - high.astype(F32)
    middle = rest.astype(BF16)
    return high, middle, (rest - middle.astype(F32)).astype(BF16)


def exact_dot(a, b):
    rows = a.shape[0]
    parts = jnp.concatenate([p.astype(F32) for p in three_parts(a)], 0).astype(BF16)
    sums = jnp.dot(parts, b.astype(BF16), preferred_element_type=F32)
    return sums[:rows] + sums[rows : 2 * rows] + sums[2 * rows :]


def expanded(values, chans):
    return exact_dot(values, members(values.shape[-1], chans, 1))


def gathered(values, groups):
    return exact_dot(values, members(groups, values.shape[-1], 0))


def shard_of(pieces, shard):
    value = pieces[0]
    for i in range(1, len(pieces)):
        value = jnp.where(shard == i, pieces[i], value)
    return value


def first_kernel(parts, groups, info_ref, x_hbm, cot_hbm, *refs):
    out_refs, (x_ref, cot_ref, sems) = refs[:parts], refs[parts:]
    rows, cols, cin = x_ref.shape
    chans = cin // parts
    n = rows * cols * (chans // groups)
    x_copy = pltpu.make_async_copy(x_hbm, x_ref, sems.at[0])
    cot_copy = pltpu.make_async_copy(cot_hbm, cot_ref, sems.at[1])
    x_copy.start()
    cot_copy.start()
    me = info_ref[ME]
    even_h = info_ref[EVEN_H] > 0
    x_copy.wait()
    shards = [x_ref[:, :, s * chans : (s + 1) * chans].astype(F32) for s in range(parts)]
    stats = []
    for x in shards:
        flat = x.reshape(rows * cols, chans)
        mean = gathered(jnp.sum(flat, axis=0, keepdims=True), groups) / n
        centered = flat - expanded(mean, chans)
        squares = gathered(jnp.sum(centered * centered, axis=0, keepdims=True), groups)
        stats.append(jnp.concatenate([p.astype(F32) for p in three_parts(jnp.concatenate([mean, squares], 1))], 0))
    cot_copy.wait()
    ends = lambda t: (jnp.where(even_h, t[rows - 1], t[0]), jnp.where(even_h, t[0], t[rows - 1]))
    cot_ends = ends(cot_ref[...].astype(F32))
    x_ends = [ends(x) for x in shards]
    for k in range(parts):
        shard = lax.rem(me + k, parts)
        out_refs[k][: 2 * cols, :chans] = jnp.concatenate([shard_of([e[i] for e in x_ends], shard) for i in range(2)], 0).astype(BF16)
        out_refs[k][: 2 * cols, chans:] = jnp.concatenate(cot_ends, 0).astype(BF16)
        out_refs[k][2 * cols :, :] = jnp.zeros((8, out_refs[k].shape[1]), BF16)
        out_refs[k][2 * cols : 2 * cols + 3, : 2 * groups] = shard_of(stats, shard).astype(BF16)


def columns_kernel(parts, info_ref, x_ref, cot_ref, w_ref, *out_refs):
    rows, cols, cin = x_ref.shape
    chans = cin // parts
    me = info_ref[ME]
    even_w = info_ref[EVEN_W] > 0

    def ends(t):
        first, last = t[:, 0, :], t[:, cols - 1, :]
        return jnp.concatenate([jnp.where(even_w, last, first), jnp.where(even_w, first, last)], 0).astype(BF16)

    cot_ends = ends(cot_ref[...].astype(F32))
    x_ends = ends(x_ref[...].astype(F32)).astype(F32)
    x_ends = [x_ends[:, s * chans : (s + 1) * chans] for s in range(parts)]
    for k in range(parts):
        out_refs[k][:, :chans] = shard_of(x_ends, lax.rem(me + k, parts)).astype(BF16)
        out_refs[k][:, chans:] = cot_ends


def tiles_kernel(parts, info_ref, x_ref, after_ref, *out_refs):
    chans = x_ref.shape[2] // parts
    me = info_ref[ME]
    shards = [x_ref[:, :, s * chans : (s + 1) * chans].astype(F32) for s in range(parts)]
    for k in range(parts):
        out_refs[k][...] = shard_of(shards, lax.rem(me + k, parts)).astype(BF16)


def pack_kernel(parts, rows, cols, info_ref, near_h, across_h, stats_ref, *refs):
    ends, (near_ref, across_ref) = refs[:parts], refs[parts:]
    even_w = info_ref[EVEN_W] > 0
    both = near_ref.shape[1]
    near_rows = near_h[...].astype(F32)
    across_rows = jnp.where((info_ref[UP] > 0) & (info_ref[DOWN] > 0), across_h[...].astype(F32), 0.0)
    columns = [ref[...].astype(F32) for ref in ends]
    stats = jnp.concatenate([p.astype(F32) for p in three_parts(stats_ref[...])], 0)
    stats = jnp.concatenate([stats, jnp.zeros((3, both - stats.shape[1]), F32)], 1)
    for half, ref, pick_last in ((0, near_ref, even_w), (1, across_ref, jnp.logical_not(even_w))):
        corners = []
        for t in (near_rows, across_rows):
            for k in range(parts):
                first, last = t[k * cols : k * cols + 1], t[(k + 1) * cols - 1 : (k + 1) * cols]
                corners.append(jnp.where(pick_last, last, first))
        pieces = [v[half * rows : (half + 1) * rows] for v in columns] + corners + ([stats] if half == 0 else [])
        used = parts * (rows + 2) + (3 if half == 0 else 0)
        if ref.shape[0] > used:
            pieces.append(jnp.zeros((ref.shape[0] - used, both), F32))
        ref[...] = jnp.concatenate(pieces, 0).astype(BF16)


def halos(parts, rows, cols, info_ref, near_h, across_h, near_w, across_w, lanes):
    even_h = info_ref[EVEN_H] > 0
    even_w = info_ref[EVEN_W] > 0
    part = lambda ref, r: ref[:, lanes].astype(F32)[:r]
    a, b = (part(ref, parts * cols) for ref in (near_h, across_h))
    b = jnp.where((info_ref[UP] > 0) & (info_ref[DOWN] > 0), b, 0.0)
    above_all, below_all = jnp.where(even_h, b, a), jnp.where(even_h, a, b)
    c, d = (part(ref, parts * (rows + 2)) for ref in (near_w, across_w))
    before_all, after_all = jnp.where(even_w, d, c), jnp.where(even_w, c, d)

    def strips(k):
        def ordered(t):
            head, tail = t[parts * rows + k :][:1], t[parts * (rows + 1) + k :][:1]
            return jnp.where(even_h, tail, head), t[k * rows : (k + 1) * rows], jnp.where(even_h, head, tail)

        at = slice(k * cols, (k + 1) * cols)
        return above_all[at], below_all[at], ordered(before_all), ordered(after_all)

    return strips


def windows(padded_ref, windows_ref, k_all, cols):
    for kx in range(3):
        view = padded_ref[:, :, kx : kx + cols, :]
        windows_ref[kx] = view.reshape(view.shape[0], k_all * cols, view.shape[3]).astype(BF16)


def backward_kernel(parts, info_ref, *refs):
    tiles, (near_h, across_h, near_w, across_w, w_ref, grad_ref, padded_ref, windows_ref) = refs[:parts], refs[parts:]
    rows, cols, outs = tiles[0].shape
    chans = w_ref.shape[2]
    strips = halos(parts, rows, cols, info_ref, near_h, across_h, near_w, across_w, slice(chans, chans + outs))
    for k in range(parts):
        above, below, before, after = strips(k)
        padded_ref[1 : rows + 1, k, 1 : cols + 1, :] = tiles[k][...].astype(F32)
        padded_ref[0, k, 1 : cols + 1, :] = above
        padded_ref[rows + 1, k, 1 : cols + 1, :] = below
        for at, (top, mid, bottom) in ((0, before), (cols + 1, after)):
            padded_ref[0, k, at : at + 1, :] = top
            padded_ref[1 : rows + 1, k, at, :] = mid
            padded_ref[rows + 1, k, at : at + 1, :] = bottom
    windows(padded_ref, windows_ref, parts, cols)
    total = None
    for ky in range(3):
        for kx in range(3):
            window = windows_ref[kx, ky : ky + rows].reshape(rows * parts * cols, outs)
            term = lax.dot_general(w_ref[2 - ky, 2 - kx], window, (((1,), (1,)), ((), ())), preferred_element_type=F32)
            total = term if total is None else total + term
    grad_ref[...] = total.T.reshape(rows, parts, cols, chans)


def terms_kernel(parts, count, info_ref, *refs):
    tiles = refs[:parts]
    near_h, across_h, near_w, across_w, stats_ref, gain_ref, shift_ref, grad_ref = refs[parts : parts + 8]
    moments_refs, (gx_own_ref, gx_other_ref, padded_ref) = refs[parts + 8 : -3], refs[-3:]
    rows, cols, _ = tiles[0].shape
    chans = grad_ref.shape[3]
    groups = stats_ref.shape[1] // (2 * parts)
    stats = jnp.concatenate([stats_ref[:, i * groups : (i + 1) * groups] for i in range(2 * parts)], 0)
    strips = halos(parts, rows, cols, info_ref, near_h, across_h, near_w, across_w, slice(0, chans))
    wide = expanded(jnp.concatenate([stats[:parts], lax.rsqrt(stats[parts:] / count + EPS)], 0), chans)
    means, invs = wide[:parts], wide[parts:]
    mine = lambda ref: shard_of([ref[s * chans : (s + 1) * chans].reshape(1, chans) for s in range(parts)], info_ref[ME])
    gain, shift = mine(gain_ref), mine(shift_ref)
    up, down, left, right = (info_ref[i] > 0 for i in (UP, DOWN, LEFT, RIGHT))
    firsts, seconds = [], []
    for k in range(parts):
        mean, inv = means[k : k + 1], invs[k : k + 1]

        def act_of(t, inside):
            z = (t - mean) * inv * gain + shift
            return jnp.where(inside, z * jax.nn.sigmoid(z), 0.0)

        above, below, before, after = strips(k)
        xhat = (tiles[k][...].astype(F32) - mean[None]) * inv[None]
        z = xhat * gain[None] + shift[None]
        sig = jax.nn.sigmoid(z)
        padded_ref[1 : rows + 1, k, 1 : cols + 1, :] = z * sig
        padded_ref[0, k, 1 : cols + 1, :] = act_of(above, up)
        padded_ref[rows + 1, k, 1 : cols + 1, :] = act_of(below, down)
        for at, (top, mid, bottom), side in ((0, before, left), (cols + 1, after, right)):
            padded_ref[0, k, at : at + 1, :] = act_of(top, side & up)
            padded_ref[1 : rows + 1, k, at, :] = act_of(mid, side)
            padded_ref[rows + 1, k, at : at + 1, :] = act_of(bottom, side & down)
        gx = grad_ref[:, k] * sig * (1.0 + z * (1.0 - sig)) * gain[None]
        if k == 0:
            gx_own_ref[...] = gx
        else:
            gx_other_ref[k - 1] = gx.astype(BF16)
        firsts.append(jnp.sum(gx.reshape(rows * cols, chans), axis=0, keepdims=True))
        seconds.append(jnp.sum((gx * xhat).reshape(rows * cols, chans), axis=0, keepdims=True))
    sums = gathered(jnp.concatenate(firsts + seconds, 0), groups)
    for k, ref in enumerate(moments_refs):
        ref[...] = jnp.concatenate([v[k : k + 1] for v in (sums[:parts], sums[parts:], stats[:parts], stats[parts:])], 0)


def forward_kernel(parts, padded_ref, w_ref, conv_own_ref, conv_other_ref, windows_ref):
    rows, cols, outs = conv_own_ref.shape
    chans = windows_ref.shape[3]
    windows(padded_ref, windows_ref, parts, cols)
    total = None
    for ky in range(3):
        for kx in range(3):
            window = windows_ref[kx, ky : ky + rows].reshape(rows * parts * cols, chans)
            term = jnp.dot(window, w_ref[ky, kx], preferred_element_type=F32)
            total = term if total is None else total + term
    total = total.reshape(rows, parts, cols, outs)
    conv_own_ref[...] = total[:, 0]
    for k in range(1, parts):
        conv_other_ref[k - 1] = total[:, k].astype(BF16)


def finish_kernel(parts, count, info_ref, x_ref, small_ref, sums_ref, bias_ref, gx_own_ref, conv_own_ref, *refs):
    gx_refs, conv_refs = refs[: parts - 1], refs[parts - 1 : 2 * parts - 2]
    conv_ref, grad_ref = refs[2 * parts - 2 :]
    cin = x_ref.shape[2]
    chans = cin // parts
    conv = conv_own_ref[...] + bias_ref[...].reshape(1, 1, -1)
    for r in conv_refs:
        conv = conv + r[...].astype(F32)
    conv_ref[...] = conv.astype(BF16)
    wide = []
    for k in range(parts):
        stats = small_ref[k]
        wide.append(jnp.concatenate([stats[2:3], lax.rsqrt(stats[3:4] / count + EPS), sums_ref[k] / count], 0))
    wide = expanded(jnp.concatenate(wide, 0), chans)
    gx_all = [gx_own_ref[...]] + [r[...].astype(F32) for r in gx_refs]
    for s in range(parts):
        at = slice(s * chans, (s + 1) * chans)
        k = lax.rem(s - info_ref[ME] + parts, parts)
        mean, inv, first, second = (shard_of([wide[4 * j + i : 4 * j + i + 1] for j in range(parts)], k)[None] for i in range(4))
        xhat = (x_ref[:, :, at].astype(F32) - mean) * inv
        grad_ref[:, :, at] = (inv * (shard_of(gx_all, k) - first - xhat * second)).astype(BF16)


def call(kernel, name, outs, operands, scratch=(), in_hbm=(), limit=28, scalars=True, cost=None):
    spec = lambda i: pl.BlockSpec(memory_space=pltpu.HBM if i in in_hbm else pltpu.SMEM if scalars and i == 0 else pltpu.VMEM)
    return pl.pallas_call(
        kernel,
        out_shape=outs,
        in_specs=[spec(i) for i in range(len(operands))],
        out_specs=[pl.BlockSpec(memory_space=pltpu.VMEM)] * len(outs),
        scratch_shapes=scratch,
        compiler_params=pltpu.CompilerParams(vmem_limit_bytes=limit * 2**20),
        cost_estimate=cost,
        name=name,
    )(*operands)


def tied(value, *others):
    for other in others:
        value = value + 0.0 * other[0, :1, : value.shape[-1]].astype(F32)
    return value


def stats_rounds(axis):
    count = lax.axis_size(axis)
    if count == 4:
        return [near, lambda i: i ^ 2]
    return [functools.partial(lambda step, i: i ^ step, 2**j) for j in range(count.bit_length() - 1)]


def body(latents, norm_gain, norm_shift, conv_weight, conv_bias, cotangent):
    _, rows, cols, cin = latents.shape
    outs = cotangent.shape[3]
    chans = conv_weight.shape[2]
    parts = lax.axis_size("dp")
    me = lax.axis_index("dp")
    groups = GROUPS * chans // cin
    both = chans + outs
    n = rows * cols * (cin // GROUPS)
    count = float(n * lax.axis_size("ha") * lax.axis_size("wa"))
    x, cot = latents[0], cotangent[0]
    sds = jax.ShapeDtypeStruct
    where = [lax.axis_index(a) for a in ("ha", "wa")]
    last = [lax.axis_size(a) - 1 for a in ("ha", "wa")]
    info = jnp.stack(
        [me, where[0] % 2 == 0, where[1] % 2 == 0, where[0] > 0, where[0] < last[0], where[1] > 0, where[1] < last[1]]
    ).astype(jnp.int32)

    *first, x, cot = call(
        functools.partial(first_kernel, parts, groups),
        "first",
        [sds((2 * cols + 8, both), BF16)] * parts + [sds(x.shape, BF16), sds(cot.shape, BF16)],
        [info, x, cot],
        [pltpu.SemaphoreType.DMA((2,))],
        in_hbm=(1, 2),
        limit=40,
        cost=pl.CostEstimate(flops=10**10, bytes_accessed=1, transcendentals=0),
    )
    peers = [[(i, (i + k) % parts) for i in range(parts)] for k in range(1, parts)]
    from_peers = lambda values: [lax.ppermute(v, "dp", pairs) for v, pairs in zip(values, peers)]
    got = from_peers(first[1:])
    ends_h = [first[0], *got]
    local = [unpacked(v, 2 * cols, 2 * groups) for v in ends_h]
    stats = jnp.concatenate([v[:, :groups] for v in local] + [v[:, groups:] for v in local], 1)
    size = stats.shape[1]
    ends_w = call(
        functools.partial(columns_kernel, parts),
        "columns",
        [sds((2 * rows, both), BF16)] * parts,
        [info, x, cot, conv_weight],
    )
    ends_w = [ends_w[0], *from_peers([v + (0.0 * got[0][:1]).astype(BF16) for v in ends_w[1:]])]

    def reduced(stats, n, axis, pairings):
        for partner in pairings:
            stats, n = merged(stats, exchange(stats, axis, partner), n), 2 * n
        return stats, n

    rounds_h, rounds_w = stats_rounds("ha"), stats_rounds("wa")
    near_h = exchange(packed([v[:cols] for v in ends_h], stats), "ha", near)
    stats, n = merged(stats, unpacked(near_h, parts * cols, size), n), 2 * n
    x_tiles = call(
        functools.partial(tiles_kernel, parts),
        "tiles",
        [sds((rows, cols, chans), BF16)] * parts,
        [info, x, near_h],
    )
    cot_tiles = [cot, *from_peers([cotangent[0]] * (parts - 1))]
    x_tiles = [x_tiles[0], *from_peers(x_tiles[1:])]

    strips = [v[cols : 2 * cols] for v in ends_h]
    if lax.axis_size("ha") == 4:
        across_h = exchange(packed(strips, stats), "ha", across)
        stats, n = merged(stats, unpacked(across_h, parts * cols, size), n), 2 * n
    else:
        across_h = exchange(jnp.concatenate(strips, 0), "ha", across)
        stats, n = reduced(stats, n, "ha", rounds_h[1:])
    used = parts * (rows + 2)
    near_w, across_w = call(
        functools.partial(pack_kernel, parts, rows, cols),
        "pack",
        [sds((-(-(used + 3) // 8) * 8, both), BF16), sds((used, both), BF16)],
        [info, near_h, across_h, stats, *ends_w],
    )
    near_w = exchange(near_w, "wa", near)
    across_w = exchange(across_w, "wa", across, ends=False)
    stats, n = merged(stats, unpacked(near_w, used, size), n), 2 * n
    stats, n = reduced(stats, n, "wa", rounds_w[1:])

    strips = [near_h, across_h, near_w, across_w]
    padded = lambda depth: pltpu.VMEM((rows + 2, parts, cols + 8, depth), F32)
    shifted = (3, rows + 2, parts * cols)
    (grad_act,) = call(
        functools.partial(backward_kernel, parts),
        "conv_backward",
        [sds((rows, parts, cols, chans), F32)],
        [info, *cot_tiles, *strips, conv_weight],
        [padded(outs), pltpu.VMEM((*shifted, outs), BF16)],
    )
    *small, gx_own, gx_other, act = call(
        functools.partial(terms_kernel, parts, count),
        "terms",
        [
            *[sds((4, groups), F32)] * parts,
            sds((rows, cols, chans), F32),
            sds((parts - 1, rows, cols, chans), BF16),
            sds((rows + 2, parts, cols + 8, chans), F32),
        ],
        [info, *x_tiles, *strips, stats, norm_gain, norm_shift, grad_act],
    )

    to_owners = lambda values: [lax.ppermute(v, "dp", [(j, i) for i, j in pairs]) for v, pairs in zip(values, peers)]
    small = jnp.stack([small[0], *to_owners(small[1:])], 0)
    gx = to_owners([gx_other[k] for k in range(parts - 1)])
    conv_own, conv_other = call(
        functools.partial(forward_kernel, parts),
        "conv_forward",
        [sds((rows, cols, outs), F32), sds((parts - 1, rows, cols, outs), BF16)],
        [act, conv_weight],
        [pltpu.VMEM((*shifted, chans), BF16)],
        scalars=False,
    )
    conv = to_owners([conv_other[k] for k in range(parts - 1)])
    sums = tied(small[:, :2], conv_own)
    for axis, pairings in (("ha", rounds_h), ("wa", rounds_w)):
        for partner in pairings:
            sums = sums + exchange(sums, axis, partner)
    conv_out, grad = call(
        functools.partial(finish_kernel, parts, count),
        "finish",
        [sds((rows, cols, outs), BF16), sds((rows, cols, cin), BF16)],
        [info, x, small, sums, conv_bias, gx_own, conv_own, *gx, *conv],
    )
    return conv_out[None], grad[None]


def solution(mesh):
    tile = P("dp", "ha", "wa", None)
    return jax.shard_map(
        body,
        mesh=mesh,
        in_specs=(tile, P(), P(), P(None, None, "dp", None), P(), tile),
        out_specs=(tile, tile),
        check_vma=False,
    )
```

```python
import functools

import jax
import jax.numpy as jnp
from jax import lax
from jax.experimental import pallas as pl
from jax.experimental.pallas import tpu as pltpu
from jax.sharding import PartitionSpec as P

GROUPS = 32
EPS = 1e-05
F32 = jnp.float32
BF16 = jnp.bfloat16

ME, EVEN_H, EVEN_W, UP, DOWN, LEFT, RIGHT = range(7)


def exchange(value, axis, partner, ends=True):
    count = lax.axis_size(axis)
    pairs = [(i, partner(i) % count) for i in range(count)]
    if not ends:
        pairs = [(i, j) for i, j in pairs if abs(i - j) == 1]
    return lax.ppermute(value, axis, pairs)


def near(i):
    return i ^ 1


def across(i):
    return i - 1 if i % 2 == 0 else i + 1


def merged(stats, other, n):
    half = stats.shape[1] // 2
    delta = other[:, :half] - stats[:, :half]
    return jnp.concatenate([stats[:, :half] + 0.5 * delta, stats[:, half:] + other[:, half:] + (0.5 * n) * delta * delta], 1)


def packed(strips, stats):
    high = lax.reduce_precision(stats, 8, 7)
    middle = lax.reduce_precision(stats - high, 8, 7)
    low = lax.reduce_precision(stats - high - middle, 8, 7)
    rows = jnp.concatenate([high, middle, low], 0).astype(BF16)
    rows = jnp.pad(rows, ((0, 0), (0, strips[0].shape[1] - rows.shape[1])))
    return jnp.concatenate([*strips, rows], 0)


def unpacked(pack, r, size):
    rows = pack[r : r + 3, :size].astype(F32)
    return rows[:1] + rows[1:2] + rows[2:]


def members(groups, chans, dim):
    per_group = chans // groups
    shape = (groups, chans) if dim else (chans, groups)
    chan = lax.broadcasted_iota(jnp.int32, shape, dim)
    group = lax.broadcasted_iota(jnp.int32, shape, 1 - dim)
    return ((chan >= group * per_group) & (chan < (group + 1) * per_group)).astype(F32)


def three_parts(a):
    high = a.astype(BF16)
    rest = a - high.astype(F32)
    middle = rest.astype(BF16)
    return high, middle, (rest - middle.astype(F32)).astype(BF16)


def exact_dot(a, b):
    rows = a.shape[0]
    parts = jnp.concatenate([p.astype(F32) for p in three_parts(a)], 0).astype(BF16)
    sums = jnp.dot(parts, b.astype(BF16), preferred_element_type=F32)
    return sums[:rows] + sums[rows : 2 * rows] + sums[2 * rows :]


def expanded(values, chans):
    return exact_dot(values, members(values.shape[-1], chans, 1))


def gathered(values, groups):
    return exact_dot(values, members(groups, values.shape[-1], 0))


def shard_of(pieces, shard):
    value = pieces[0]
    for i in range(1, len(pieces)):
        value = jnp.where(shard == i, pieces[i], value)
    return value


def first_kernel(parts, groups, info_ref, x_ref, *out_refs):
    rows, cols, cin = x_ref.shape
    chans = cin // parts
    n = rows * cols * (chans // groups)
    me = info_ref[ME]
    even_h = info_ref[EVEN_H] > 0
    shards = [x_ref[:, :, s * chans : (s + 1) * chans].astype(F32) for s in range(parts)]
    stats = []
    for x in shards:
        flat = x.reshape(rows * cols, chans)
        mean = gathered(jnp.sum(flat, axis=0, keepdims=True), groups) / n
        centered = flat - expanded(mean, chans)
        squares = gathered(jnp.sum(centered * centered, axis=0, keepdims=True), groups)
        stats.append(jnp.concatenate([p.astype(F32) for p in three_parts(jnp.concatenate([mean, squares], 1))], 0))
    ends = [jnp.concatenate(row_ends(x, even_h), 0) for x in shards]
    for k, ref in enumerate(out_refs):
        shard = lax.rem(me + k, parts)
        ref[: 2 * cols, :] = shard_of(ends, shard).astype(BF16)
        ref[2 * cols :, :] = jnp.zeros((8, chans), BF16)
        ref[2 * cols : 2 * cols + 3, : 2 * groups] = shard_of(stats, shard).astype(BF16)


def row_ends(t, even_h):
    first, last = t[0], t[t.shape[0] - 1]
    return jnp.where(even_h, last, first), jnp.where(even_h, first, last)


def column_ends(t, even_w):
    first, last = t[:, 0, :], t[:, t.shape[1] - 1, :]
    return jnp.concatenate([jnp.where(even_w, last, first), jnp.where(even_w, first, last)], 0)


def columns_kernel(parts, info_ref, x_ref, w_ref, *out_refs):
    chans = x_ref.shape[2] // parts
    me = info_ref[ME]
    ends = column_ends(x_ref[...].astype(F32), info_ref[EVEN_W] > 0)
    for k in range(parts):
        shard = lax.rem(me + k, parts)
        out_refs[k][...] = shard_of([ends[:, s * chans : (s + 1) * chans] for s in range(parts)], shard).astype(BF16)
        out_refs[parts + k][...] = shard_of([x_ref[:, :, s * chans : (s + 1) * chans].astype(F32) for s in range(parts)], shard).astype(BF16)


def rows_kernel(parts, info_ref, *refs):
    packs, cots, (near_ref, across_ref, stats_ref) = refs[:parts], refs[parts : 2 * parts], refs[2 * parts :]
    rows, cols, outs = cots[0].shape
    chans = packs[0].shape[1]
    groups = stats_ref.shape[1] // (2 * parts)
    even_h = info_ref[EVEN_H] > 0
    packs = [ref[...].astype(F32) for ref in packs]
    cot_ends = [row_ends(ref[...].astype(F32), even_h) for ref in cots]
    local = [v[2 * cols : 2 * cols + 3, : 2 * groups] for v in packs]
    terms = jnp.concatenate([v[:, :groups] for v in local] + [v[:, groups:] for v in local], 1)
    stats_ref[...] = terms[0:1] + terms[1:2] + terms[2:3]
    tail = jnp.concatenate([terms, jnp.zeros((3, chans + outs - terms.shape[1]), F32)], 1)
    for half, ref in enumerate((near_ref, across_ref)):
        strips = [jnp.concatenate([v[half * cols : (half + 1) * cols], c[half]], 1) for v, c in zip(packs, cot_ends)]
        ref[...] = jnp.concatenate(strips + ([tail, jnp.zeros((5, chans + outs), F32)] if half == 0 else []), 0).astype(BF16)


def cot_columns_kernel(parts, info_ref, *refs):
    for cot_ref, ref in zip(refs[:parts], refs[parts + 1 :]):
        ref[...] = column_ends(cot_ref[...].astype(F32), info_ref[EVEN_W] > 0).astype(BF16)


def pack_kernel(parts, rows, cols, info_ref, near_h, across_h, stats_ref, *refs):
    ends, cot_ends, (near_ref, across_ref) = refs[:parts], refs[parts : 2 * parts], refs[2 * parts :]
    even_w = info_ref[EVEN_W] > 0
    both = near_ref.shape[1]
    near_rows = near_h[...].astype(F32)
    across_rows = jnp.where((info_ref[UP] > 0) & (info_ref[DOWN] > 0), across_h[...].astype(F32), 0.0)
    columns = [jnp.concatenate([x[...].astype(F32), c[...].astype(F32)], 1) for x, c in zip(ends, cot_ends)]
    stats = jnp.concatenate([p.astype(F32) for p in three_parts(stats_ref[...])], 0)
    stats = jnp.concatenate([stats, jnp.zeros((3, both - stats.shape[1]), F32)], 1)
    for half, ref, pick_last in ((0, near_ref, even_w), (1, across_ref, jnp.logical_not(even_w))):
        corners = []
        for t in (near_rows, across_rows):
            for k in range(parts):
                first, last = t[k * cols : k * cols + 1], t[(k + 1) * cols - 1 : (k + 1) * cols]
                corners.append(jnp.where(pick_last, last, first))
        pieces = [v[half * rows : (half + 1) * rows] for v in columns] + corners + ([stats] if half == 0 else [])
        used = parts * (rows + 2) + (3 if half == 0 else 0)
        if ref.shape[0] > used:
            pieces.append(jnp.zeros((ref.shape[0] - used, both), F32))
        ref[...] = jnp.concatenate(pieces, 0).astype(BF16)


def halos(parts, rows, cols, info_ref, near_h, across_h, near_w, across_w, lanes):
    even_h = info_ref[EVEN_H] > 0
    even_w = info_ref[EVEN_W] > 0
    part = lambda ref, r: ref[:, lanes].astype(F32)[:r]
    a, b = (part(ref, parts * cols) for ref in (near_h, across_h))
    b = jnp.where((info_ref[UP] > 0) & (info_ref[DOWN] > 0), b, 0.0)
    above_all, below_all = jnp.where(even_h, b, a), jnp.where(even_h, a, b)
    c, d = (part(ref, parts * (rows + 2)) for ref in (near_w, across_w))
    before_all, after_all = jnp.where(even_w, d, c), jnp.where(even_w, c, d)

    def strips(k):
        def ordered(t):
            head, tail = t[parts * rows + k :][:1], t[parts * (rows + 1) + k :][:1]
            return jnp.where(even_h, tail, head), t[k * rows : (k + 1) * rows], jnp.where(even_h, head, tail)

        at = slice(k * cols, (k + 1) * cols)
        return above_all[at], below_all[at], ordered(before_all), ordered(after_all)

    return strips


def windows(padded_ref, windows_ref, k_all, cols):
    for kx in range(3):
        view = padded_ref[:, :, kx : kx + cols, :]
        windows_ref[kx] = view.reshape(view.shape[0], k_all * cols, view.shape[3]).astype(BF16)


def backward_kernel(parts, info_ref, *refs):
    tiles, (near_h, across_h, near_w, across_w, w_ref, grad_ref, padded_ref, windows_ref) = refs[:parts], refs[parts:]
    rows, cols, outs = tiles[0].shape
    chans = w_ref.shape[2]
    strips = halos(parts, rows, cols, info_ref, near_h, across_h, near_w, across_w, slice(chans, chans + outs))
    for k in range(parts):
        above, below, before, after = strips(k)
        padded_ref[1 : rows + 1, k, 1 : cols + 1, :] = tiles[k][...].astype(F32)
        padded_ref[0, k, 1 : cols + 1, :] = above
        padded_ref[rows + 1, k, 1 : cols + 1, :] = below
        for at, (top, mid, bottom) in ((0, before), (cols + 1, after)):
            padded_ref[0, k, at : at + 1, :] = top
            padded_ref[1 : rows + 1, k, at, :] = mid
            padded_ref[rows + 1, k, at : at + 1, :] = bottom
    windows(padded_ref, windows_ref, parts, cols)
    total = None
    for ky in range(3):
        for kx in range(3):
            window = windows_ref[kx, ky : ky + rows].reshape(rows * parts * cols, outs)
            term = lax.dot_general(w_ref[2 - ky, 2 - kx], window, (((1,), (1,)), ((), ())), preferred_element_type=F32)
            total = term if total is None else total + term
    grad_ref[...] = total.T.reshape(rows, parts, cols, chans)


def terms_kernel(parts, count, info_ref, *refs):
    tiles = refs[:parts]
    near_h, across_h, near_w, across_w, stats_ref, gain_ref, shift_ref, grad_ref = refs[parts : parts + 8]
    moments_refs, (gx_own_ref, gx_other_ref, padded_ref) = refs[parts + 8 : -3], refs[-3:]
    rows, cols, _ = tiles[0].shape
    chans = grad_ref.shape[3]
    groups = stats_ref.shape[1] // (2 * parts)
    stats = jnp.concatenate([stats_ref[:, i * groups : (i + 1) * groups] for i in range(2 * parts)], 0)
    strips = halos(parts, rows, cols, info_ref, near_h, across_h, near_w, across_w, slice(0, chans))
    wide = expanded(jnp.concatenate([stats[:parts], lax.rsqrt(stats[parts:] / count + EPS)], 0), chans)
    means, invs = wide[:parts], wide[parts:]
    mine = lambda ref: shard_of([ref[s * chans : (s + 1) * chans].reshape(1, chans) for s in range(parts)], info_ref[ME])
    gain, shift = mine(gain_ref), mine(shift_ref)
    up, down, left, right = (info_ref[i] > 0 for i in (UP, DOWN, LEFT, RIGHT))
    firsts, seconds = [], []
    for k in range(parts):
        mean, inv = means[k : k + 1], invs[k : k + 1]

        def act_of(t, inside):
            z = (t - mean) * inv * gain + shift
            return jnp.where(inside, z * jax.nn.sigmoid(z), 0.0)

        above, below, before, after = strips(k)
        xhat = (tiles[k][...].astype(F32) - mean[None]) * inv[None]
        z = xhat * gain[None] + shift[None]
        sig = jax.nn.sigmoid(z)
        padded_ref[1 : rows + 1, k, 1 : cols + 1, :] = z * sig
        padded_ref[0, k, 1 : cols + 1, :] = act_of(above, up)
        padded_ref[rows + 1, k, 1 : cols + 1, :] = act_of(below, down)
        for at, (top, mid, bottom), side in ((0, before, left), (cols + 1, after, right)):
            padded_ref[0, k, at : at + 1, :] = act_of(top, side & up)
            padded_ref[1 : rows + 1, k, at, :] = act_of(mid, side)
            padded_ref[rows + 1, k, at : at + 1, :] = act_of(bottom, side & down)
        gx = grad_ref[:, k] * sig * (1.0 + z * (1.0 - sig)) * gain[None]
        if k == 0:
            gx_own_ref[...] = gx
        else:
            gx_other_ref[k - 1] = gx.astype(BF16)
        firsts.append(jnp.sum(gx.reshape(rows * cols, chans), axis=0, keepdims=True))
        seconds.append(jnp.sum((gx * xhat).reshape(rows * cols, chans), axis=0, keepdims=True))
    sums = gathered(jnp.concatenate(firsts + seconds, 0), groups)
    for k, ref in enumerate(moments_refs):
        ref[...] = jnp.concatenate([v[k : k + 1] for v in (sums[:parts], sums[parts:], stats[:parts], stats[parts:])], 0)


def forward_kernel(parts, padded_ref, w_ref, conv_own_ref, conv_other_ref, windows_ref):
    rows, cols, outs = conv_own_ref.shape
    chans = windows_ref.shape[3]
    windows(padded_ref, windows_ref, parts, cols)
    total = None
    for ky in range(3):
        for kx in range(3):
            window = windows_ref[kx, ky : ky + rows].reshape(rows * parts * cols, chans)
            term = jnp.dot(window, w_ref[ky, kx], preferred_element_type=F32)
            total = term if total is None else total + term
    total = total.reshape(rows, parts, cols, outs)
    conv_own_ref[...] = total[:, 0]
    for k in range(1, parts):
        conv_other_ref[k - 1] = total[:, k].astype(BF16)


def finish_kernel(parts, count, info_ref, x_ref, small_ref, sums_ref, bias_ref, gx_own_ref, conv_own_ref, *refs):
    gx_refs, conv_refs = refs[: parts - 1], refs[parts - 1 : 2 * parts - 2]
    conv_ref, grad_ref = refs[2 * parts - 2 :]
    cin = x_ref.shape[2]
    chans = cin // parts
    conv = conv_own_ref[...] + bias_ref[...].reshape(1, 1, -1)
    for r in conv_refs:
        conv = conv + r[...].astype(F32)
    conv_ref[...] = conv.astype(BF16)
    wide = []
    for k in range(parts):
        stats = small_ref[k]
        wide.append(jnp.concatenate([stats[2:3], lax.rsqrt(stats[3:4] / count + EPS), sums_ref[k] / count], 0))
    wide = expanded(jnp.concatenate(wide, 0), chans)
    gx_all = [gx_own_ref[...]] + [r[...].astype(F32) for r in gx_refs]
    for s in range(parts):
        at = slice(s * chans, (s + 1) * chans)
        k = lax.rem(s - info_ref[ME] + parts, parts)
        mean, inv, first, second = (shard_of([wide[4 * j + i : 4 * j + i + 1] for j in range(parts)], k)[None] for i in range(4))
        xhat = (x_ref[:, :, at].astype(F32) - mean) * inv
        grad_ref[:, :, at] = (inv * (shard_of(gx_all, k) - first - xhat * second)).astype(BF16)


def call(kernel, name, outs, operands, scratch=(), in_hbm=(), limit=28, scalars=True, cost=None):
    spec = lambda i: pl.BlockSpec(memory_space=pltpu.HBM if i in in_hbm else pltpu.SMEM if scalars and i == 0 else pltpu.VMEM)
    return pl.pallas_call(
        kernel,
        out_shape=outs,
        in_specs=[spec(i) for i in range(len(operands))],
        out_specs=[pl.BlockSpec(memory_space=pltpu.VMEM)] * len(outs),
        scratch_shapes=scratch,
        compiler_params=pltpu.CompilerParams(vmem_limit_bytes=limit * 2**20),
        cost_estimate=cost,
        name=name,
    )(*operands)


def tied(value, *others):
    for other in others:
        value = value + 0.0 * other[0, :1, : value.shape[-1]].astype(F32)
    return value


def stats_rounds(axis):
    count = lax.axis_size(axis)
    if count == 4:
        return [near, lambda i: i ^ 2]
    return [functools.partial(lambda step, i: i ^ step, 2**j) for j in range(count.bit_length() - 1)]


def body(latents, norm_gain, norm_shift, conv_weight, conv_bias, cotangent):
    _, rows, cols, cin = latents.shape
    outs = cotangent.shape[3]
    chans = conv_weight.shape[2]
    parts = lax.axis_size("dp")
    me = lax.axis_index("dp")
    groups = GROUPS * chans // cin
    both = chans + outs
    n = rows * cols * (cin // GROUPS)
    count = float(n * lax.axis_size("ha") * lax.axis_size("wa"))
    x, cot = latents[0], cotangent[0]
    sds = jax.ShapeDtypeStruct
    where = [lax.axis_index(a) for a in ("ha", "wa")]
    last = [lax.axis_size(a) - 1 for a in ("ha", "wa")]
    info = jnp.stack(
        [me, where[0] % 2 == 0, where[1] % 2 == 0, where[0] > 0, where[0] < last[0], where[1] > 0, where[1] < last[1]]
    ).astype(jnp.int32)

    peers = [[(i, (i + k) % parts) for i in range(parts)] for k in range(1, parts)]
    from_peers = lambda values: [lax.ppermute(v, "dp", pairs) for v, pairs in zip(values, peers)]
    cot_tiles = [cot, *from_peers([cot] * (parts - 1))]
    first = call(
        functools.partial(first_kernel, parts, groups),
        "first",
        [sds((2 * cols + 8, chans), BF16)] * parts,
        [info, x],
        cost=pl.CostEstimate(flops=10**10, bytes_accessed=1, transcendentals=0),
    )
    got = from_peers(first[1:])
    columns = call(
        functools.partial(columns_kernel, parts),
        "columns",
        [sds((2 * rows, chans), BF16)] * parts + [sds((rows, cols, chans), BF16)] * parts,
        [info, x, conv_weight],
    )
    zero = (0.0 * got[0][:1]).astype(BF16)
    ends_w = [columns[0], *from_peers([v + zero for v in columns[1:parts]])]
    x_tiles = [columns[parts], *from_peers([v + zero[None] for v in columns[parts + 1 :]])]
    size = 2 * parts * groups
    pack_near, pack_across, stats = call(
        functools.partial(rows_kernel, parts),
        "rows",
        [sds((parts * cols + 8, both), BF16), sds((parts * cols, both), BF16), sds((1, size), F32)],
        [info, first[0], *got, *cot_tiles],
    )

    def reduced(stats, n, axis, pairings):
        for partner in pairings:
            stats, n = merged(stats, exchange(stats, axis, partner), n), 2 * n
        return stats, n

    rounds_h, rounds_w = stats_rounds("ha"), stats_rounds("wa")
    near_h = exchange(pack_near, "ha", near)
    cot_ends_w = call(
        functools.partial(cot_columns_kernel, parts),
        "cot_columns",
        [sds((2 * rows, outs), BF16)] * parts,
        [info, *cot_tiles, stats],
    )
    stats, n = merged(stats, unpacked(near_h, parts * cols, size), n), 2 * n
    if lax.axis_size("ha") == 4:
        across_h = exchange(packed([pack_across], stats), "ha", across)
        stats, n = merged(stats, unpacked(across_h, parts * cols, size), n), 2 * n
    else:
        across_h = exchange(pack_across, "ha", across)
        stats, n = reduced(stats, n, "ha", rounds_h[1:])
    used = parts * (rows + 2)
    near_w, across_w = call(
        functools.partial(pack_kernel, parts, rows, cols),
        "pack",
        [sds((-(-(used + 3) // 8) * 8, both), BF16), sds((used, both), BF16)],
        [info, near_h, across_h, stats, *ends_w, *cot_ends_w],
    )
    near_w = exchange(near_w, "wa", near)
    across_w = exchange(across_w, "wa", across, ends=False)
    stats, n = merged(stats, unpacked(near_w, used, size), n), 2 * n
    stats, n = reduced(stats, n, "wa", rounds_w[1:])

    strips = [near_h, across_h, near_w, across_w]
    padded = lambda depth: pltpu.VMEM((rows + 2, parts, cols + 8, depth), F32)
    shifted = (3, rows + 2, parts * cols)
    (grad_act,) = call(
        functools.partial(backward_kernel, parts),
        "conv_backward",
        [sds((rows, parts, cols, chans), F32)],
        [info, *cot_tiles, *strips, conv_weight],
        [padded(outs), pltpu.VMEM((*shifted, outs), BF16)],
    )
    *small, gx_own, gx_other, act = call(
        functools.partial(terms_kernel, parts, count),
        "terms",
        [
            *[sds((4, groups), F32)] * parts,
            sds((rows, cols, chans), F32),
            sds((parts - 1, rows, cols, chans), BF16),
            sds((rows + 2, parts, cols + 8, chans), F32),
        ],
        [info, *x_tiles, *strips, stats, norm_gain, norm_shift, grad_act],
    )

    to_owners = lambda values: [lax.ppermute(v, "dp", [(j, i) for i, j in pairs]) for v, pairs in zip(values, peers)]
    small = jnp.stack([small[0], *to_owners(small[1:])], 0)
    gx = to_owners([gx_other[k] for k in range(parts - 1)])
    conv_own, conv_other = call(
        functools.partial(forward_kernel, parts),
        "conv_forward",
        [sds((rows, cols, outs), F32), sds((parts - 1, rows, cols, outs), BF16)],
        [act, conv_weight],
        [pltpu.VMEM((*shifted, chans), BF16)],
        scalars=False,
    )
    conv = to_owners([conv_other[k] for k in range(parts - 1)])
    sums = tied(small[:, :2], conv_own)
    for axis, pairings in (("ha", rounds_h), ("wa", rounds_w)):
        for partner in pairings:
            sums = sums + exchange(sums, axis, partner)
    conv_out, grad = call(
        functools.partial(finish_kernel, parts, count),
        "finish",
        [sds((rows, cols, outs), BF16), sds((rows, cols, cin), BF16)],
        [info, x, small, sums, conv_bias, gx_own, conv_own, *gx, *conv],
    )
    return conv_out[None], grad[None]


def solution(mesh):
    tile = P("dp", "ha", "wa", None)
    return jax.shard_map(
        body,
        mesh=mesh,
        in_specs=(tile, P(), P(), P(None, None, "dp", None), P(), tile),
        out_specs=(tile, tile),
        check_vma=False,
    )
```

```python
import functools

import jax
import jax.numpy as jnp
from jax import lax
from jax.experimental import pallas as pl
from jax.experimental.pallas import tpu as pltpu
from jax.sharding import PartitionSpec as P

GROUPS = 32
EPS = 1e-05
F32 = jnp.float32
BF16 = jnp.bfloat16

ME, EVEN_H, EVEN_W, UP, DOWN, LEFT, RIGHT = range(7)


def exchange(value, axis, partner, ends=True):
    count = lax.axis_size(axis)
    pairs = [(i, partner(i) % count) for i in range(count)]
    if not ends:
        pairs = [(i, j) for i, j in pairs if abs(i - j) == 1]
    return lax.ppermute(value, axis, pairs)


def near(i):
    return i ^ 1


def across(i):
    return i - 1 if i % 2 == 0 else i + 1


def merged(stats, other, n):
    half = stats.shape[1] // 2
    delta = other[:, :half] - stats[:, :half]
    return jnp.concatenate([stats[:, :half] + 0.5 * delta, stats[:, half:] + other[:, half:] + (0.5 * n) * delta * delta], 1)


def packed(strips, stats):
    high = lax.reduce_precision(stats, 8, 7)
    middle = lax.reduce_precision(stats - high, 8, 7)
    low = lax.reduce_precision(stats - high - middle, 8, 7)
    rows = jnp.concatenate([high, middle, low], 0).astype(BF16)
    rows = jnp.pad(rows, ((0, 0), (0, strips[0].shape[1] - rows.shape[1])))
    return jnp.concatenate([*strips, rows], 0)


def unpacked(pack, r, size):
    rows = pack[r : r + 3, :size].astype(F32)
    return rows[:1] + rows[1:2] + rows[2:]


def members(groups, chans, dim):
    per_group = chans // groups
    shape = (groups, chans) if dim else (chans, groups)
    chan = lax.broadcasted_iota(jnp.int32, shape, dim)
    group = lax.broadcasted_iota(jnp.int32, shape, 1 - dim)
    return ((chan >= group * per_group) & (chan < (group + 1) * per_group)).astype(F32)


def three_parts(a):
    high = a.astype(BF16)
    rest = a - high.astype(F32)
    middle = rest.astype(BF16)
    return high, middle, (rest - middle.astype(F32)).astype(BF16)


def exact_dot(a, b):
    rows = a.shape[0]
    parts = jnp.concatenate([p.astype(F32) for p in three_parts(a)], 0).astype(BF16)
    sums = jnp.dot(parts, b.astype(BF16), preferred_element_type=F32)
    return sums[:rows] + sums[rows : 2 * rows] + sums[2 * rows :]


def expanded(values, chans):
    return exact_dot(values, members(values.shape[-1], chans, 1))


def gathered(values, groups):
    return exact_dot(values, members(groups, values.shape[-1], 0))


def shard_of(pieces, shard):
    value = pieces[0]
    for i in range(1, len(pieces)):
        value = jnp.where(shard == i, pieces[i], value)
    return value


def first_kernel(parts, groups, info_ref, x_ref, *out_refs):
    rows, cols, cin = x_ref.shape
    chans = cin // parts
    n = rows * cols * (chans // groups)
    me = info_ref[ME]
    even_h = info_ref[EVEN_H] > 0
    shards = [x_ref[:, :, s * chans : (s + 1) * chans].astype(F32) for s in range(parts)]
    stats = []
    for x in shards:
        flat = x.reshape(rows * cols, chans)
        mean = gathered(jnp.sum(flat, axis=0, keepdims=True), groups) / n
        centered = flat - expanded(mean, chans)
        squares = gathered(jnp.sum(centered * centered, axis=0, keepdims=True), groups)
        stats.append(jnp.concatenate([p.astype(F32) for p in three_parts(jnp.concatenate([mean, squares], 1))], 0))
    ends = [jnp.concatenate(row_ends(x, even_h), 0) for x in shards]
    columns = [column_ends(x, info_ref[EVEN_W] > 0) for x in shards]
    for k, ref in enumerate(out_refs):
        shard = lax.rem(me + k, parts)
        ref[: 2 * cols, :] = shard_of(ends, shard).astype(BF16)
        ref[2 * cols : 2 * cols + 8, :] = jnp.zeros((8, chans), BF16)
        ref[2 * cols : 2 * cols + 3, : 2 * groups] = shard_of(stats, shard).astype(BF16)
        ref[2 * cols + 8 :, :] = shard_of(columns, shard).astype(BF16)


def row_ends(t, even_h):
    first, last = t[0], t[t.shape[0] - 1]
    return jnp.where(even_h, last, first), jnp.where(even_h, first, last)


def column_ends(t, even_w):
    first, last = t[:, 0, :], t[:, t.shape[1] - 1, :]
    return jnp.concatenate([jnp.where(even_w, last, first), jnp.where(even_w, first, last)], 0)


def tiles_kernel(parts, info_ref, x_ref, w_ref, *out_refs):
    chans = x_ref.shape[2] // parts
    for k in range(parts):
        shard = lax.rem(info_ref[ME] + k, parts)
        out_refs[k][...] = shard_of([x_ref[:, :, s * chans : (s + 1) * chans].astype(F32) for s in range(parts)], shard).astype(BF16)


def rows_kernel(parts, info_ref, *refs):
    packs, cots, (near_ref, across_ref, stats_ref) = refs[:parts], refs[parts : 2 * parts], refs[2 * parts :]
    rows, cols, outs = cots[0].shape
    chans = packs[0].shape[1]
    groups = stats_ref.shape[1] // (2 * parts)
    even_h = info_ref[EVEN_H] > 0
    packs = [ref[...].astype(F32) for ref in packs]
    cot_ends = [row_ends(ref[...].astype(F32), even_h) for ref in cots]
    local = [v[2 * cols : 2 * cols + 3, : 2 * groups] for v in packs]
    terms = jnp.concatenate([v[:, :groups] for v in local] + [v[:, groups:] for v in local], 1)
    stats_ref[...] = terms[0:1] + terms[1:2] + terms[2:3]
    tail = jnp.concatenate([terms, jnp.zeros((3, chans + outs - terms.shape[1]), F32)], 1)
    for half, ref in enumerate((near_ref, across_ref)):
        strips = [jnp.concatenate([v[half * cols : (half + 1) * cols], c[half]], 1) for v, c in zip(packs, cot_ends)]
        ref[...] = jnp.concatenate(strips + ([tail, jnp.zeros((5, chans + outs), F32)] if half == 0 else []), 0).astype(BF16)


def columns_kernel(parts, info_ref, *refs):
    even_w = info_ref[EVEN_W] > 0
    for pack_ref, cot_ref, ref in zip(refs[:parts], refs[parts : 2 * parts], refs[2 * parts + 1 :]):
        rows, cols, _ = cot_ref.shape
        chans = pack_ref.shape[1]
        ref[:, :chans] = pack_ref[...].astype(F32)[2 * cols + 8 :].astype(BF16)
        ref[:, chans:] = column_ends(cot_ref[...].astype(F32), even_w).astype(BF16)


def pack_kernel(parts, rows, cols, info_ref, near_h, across_h, stats_ref, *refs):
    ends, (near_ref, across_ref) = refs[:parts], refs[parts:]
    even_w = info_ref[EVEN_W] > 0
    both = near_ref.shape[1]
    near_rows = near_h[...].astype(F32)
    across_rows = jnp.where((info_ref[UP] > 0) & (info_ref[DOWN] > 0), across_h[...].astype(F32), 0.0)
    columns = [ref[...].astype(F32) for ref in ends]
    stats = jnp.concatenate([p.astype(F32) for p in three_parts(stats_ref[...])], 0)
    stats = jnp.concatenate([stats, jnp.zeros((3, both - stats.shape[1]), F32)], 1)
    for half, ref, pick_last in ((0, near_ref, even_w), (1, across_ref, jnp.logical_not(even_w))):
        corners = []
        for t in (near_rows, across_rows):
            for k in range(parts):
                first, last = t[k * cols : k * cols + 1], t[(k + 1) * cols - 1 : (k + 1) * cols]
                corners.append(jnp.where(pick_last, last, first))
        pieces = [v[half * rows : (half + 1) * rows] for v in columns] + corners + ([stats] if half == 0 else [])
        used = parts * (rows + 2) + (3 if half == 0 else 0)
        if ref.shape[0] > used:
            pieces.append(jnp.zeros((ref.shape[0] - used, both), F32))
        ref[...] = jnp.concatenate(pieces, 0).astype(BF16)


def halos(parts, rows, cols, info_ref, near_h, across_h, near_w, across_w, lanes):
    even_h = info_ref[EVEN_H] > 0
    even_w = info_ref[EVEN_W] > 0
    part = lambda ref, r: ref[:, lanes].astype(F32)[:r]
    a, b = (part(ref, parts * cols) for ref in (near_h, across_h))
    b = jnp.where((info_ref[UP] > 0) & (info_ref[DOWN] > 0), b, 0.0)
    above_all, below_all = jnp.where(even_h, b, a), jnp.where(even_h, a, b)
    c, d = (part(ref, parts * (rows + 2)) for ref in (near_w, across_w))
    before_all, after_all = jnp.where(even_w, d, c), jnp.where(even_w, c, d)

    def strips(k):
        def ordered(t):
            head, tail = t[parts * rows + k :][:1], t[parts * (rows + 1) + k :][:1]
            return jnp.where(even_h, tail, head), t[k * rows : (k + 1) * rows], jnp.where(even_h, head, tail)

        at = slice(k * cols, (k + 1) * cols)
        return above_all[at], below_all[at], ordered(before_all), ordered(after_all)

    return strips


def windows(padded_ref, windows_ref, k_all, cols):
    for kx in range(3):
        view = padded_ref[:, :, kx : kx + cols, :]
        windows_ref[kx] = view.reshape(view.shape[0], k_all * cols, view.shape[3]).astype(BF16)


def backward_kernel(parts, info_ref, *refs):
    tiles, (near_h, across_h, near_w, across_w, w_ref, *_, grad_ref, padded_ref, windows_ref) = refs[:parts], refs[parts:]
    rows, cols, outs = tiles[0].shape
    chans = w_ref.shape[2]
    strips = halos(parts, rows, cols, info_ref, near_h, across_h, near_w, across_w, slice(chans, chans + outs))
    for k in range(parts):
        above, below, before, after = strips(k)
        padded_ref[1 : rows + 1, k, 1 : cols + 1, :] = tiles[k][...].astype(F32)
        padded_ref[0, k, 1 : cols + 1, :] = above
        padded_ref[rows + 1, k, 1 : cols + 1, :] = below
        for at, (top, mid, bottom) in ((0, before), (cols + 1, after)):
            padded_ref[0, k, at : at + 1, :] = top
            padded_ref[1 : rows + 1, k, at, :] = mid
            padded_ref[rows + 1, k, at : at + 1, :] = bottom
    windows(padded_ref, windows_ref, parts, cols)
    taps = [(ky, kx) for ky in range(3) for kx in range(3)]
    shifted = jnp.concatenate([windows_ref[kx, ky : ky + rows].reshape(rows * parts * cols, outs) for ky, kx in taps], 1)
    weight = jnp.concatenate([w_ref[2 - ky, 2 - kx] for ky, kx in taps], 1)
    total = lax.dot_general(weight, shifted, (((1,), (1,)), ((), ())), preferred_element_type=F32)
    grad_ref[...] = total.T.reshape(rows, parts, cols, chans)


def terms_kernel(parts, count, info_ref, *refs):
    tiles = refs[:parts]
    stats_ref, gain_ref, shift_ref, grad_ref = refs[parts : parts + 4]
    moments_refs, (gx_own_ref, gx_other_ref, padded_ref, scales_ref) = refs[parts + 4 : -4], refs[-4:]
    rows, cols, _ = tiles[0].shape
    chans = grad_ref.shape[3]
    groups = stats_ref.shape[1] // (2 * parts)
    stats = jnp.concatenate([stats_ref[:, i * groups : (i + 1) * groups] for i in range(2 * parts)], 0)
    wide = expanded(jnp.concatenate([stats[:parts], lax.rsqrt(stats[parts:] / count + EPS)], 0), chans)
    means, invs = wide[:parts], wide[parts:]
    mine = lambda ref: shard_of([ref[s * chans : (s + 1) * chans].reshape(1, chans) for s in range(parts)], info_ref[ME])
    gain, shift = mine(gain_ref), mine(shift_ref)
    scales_ref[...] = jnp.concatenate([wide, gain, shift], 0)
    firsts, seconds = [], []
    for k in range(parts):
        mean, inv = means[k : k + 1], invs[k : k + 1]
        xhat = (tiles[k][...].astype(F32) - mean[None]) * inv[None]
        z = xhat * gain[None] + shift[None]
        sig = jax.nn.sigmoid(z)
        padded_ref[:, k, 1 : cols + 1, :] = z * sig
        gx = grad_ref[:, k] * sig * (1.0 + z * (1.0 - sig)) * gain[None]
        if k == 0:
            gx_own_ref[...] = gx
        else:
            gx_other_ref[k - 1] = gx.astype(BF16)
        firsts.append(jnp.sum(gx.reshape(rows * cols, chans), axis=0, keepdims=True))
        seconds.append(jnp.sum((gx * xhat).reshape(rows * cols, chans), axis=0, keepdims=True))
    sums = gathered(jnp.concatenate(firsts + seconds, 0), groups)
    for k, ref in enumerate(moments_refs):
        ref[...] = jnp.concatenate([v[k : k + 1] for v in (sums[:parts], sums[parts:], stats[:parts], stats[parts:])], 0)


def forward_kernel(parts, info_ref, given_ref, scales_ref, near_h, across_h, near_w, across_w, w_ref, conv_own_ref, conv_other_ref, padded_ref, windows_ref):
    rows, cols, outs = conv_own_ref.shape
    chans = windows_ref.shape[3]
    strips = halos(parts, rows, cols, info_ref, near_h, across_h, near_w, across_w, slice(0, chans))
    up, down, left, right = (info_ref[i] > 0 for i in (UP, DOWN, LEFT, RIGHT))
    scales = scales_ref[...]
    gain, shift = scales[2 * parts : 2 * parts + 1], scales[2 * parts + 1 : 2 * parts + 2]
    padded_ref[1 : rows + 1] = given_ref[...]
    for k in range(parts):
        mean, inv = scales[k : k + 1], scales[parts + k : parts + k + 1]

        def act_of(t, inside):
            z = (t - mean) * inv * gain + shift
            return jnp.where(inside, z * jax.nn.sigmoid(z), 0.0)

        above, below, before, after = strips(k)
        padded_ref[0, k, 1 : cols + 1, :] = act_of(above, up)
        padded_ref[rows + 1, k, 1 : cols + 1, :] = act_of(below, down)
        for at, (top, mid, bottom), side in ((0, before, left), (cols + 1, after, right)):
            padded_ref[0, k, at : at + 1, :] = act_of(top, side & up)
            padded_ref[1 : rows + 1, k, at, :] = act_of(mid, side)
            padded_ref[rows + 1, k, at : at + 1, :] = act_of(bottom, side & down)
    windows(padded_ref, windows_ref, parts, cols)
    taps = [(ky, kx) for ky in range(3) for kx in range(3)]
    shifted = jnp.concatenate([windows_ref[kx, ky : ky + rows].reshape(rows * parts * cols, chans) for ky, kx in taps], 1)
    weight = w_ref[...].reshape(9 * chans, outs)
    total = lax.dot_general(weight, shifted, (((0,), (1,)), ((), ())), preferred_element_type=F32).T
    total = total.reshape(rows, parts, cols, outs)
    conv_own_ref[...] = total[:, 0]
    for k in range(1, parts):
        conv_other_ref[k - 1] = total[:, k].astype(BF16)


def finish_kernel(parts, count, info_ref, x_ref, small_ref, sums_ref, bias_ref, gx_own_ref, conv_own_ref, *refs):
    gx_refs, conv_refs = refs[: parts - 1], refs[parts - 1 : 2 * parts - 2]
    conv_out, grad_out, conv_ref, grad_ref, sems = refs[2 * parts - 2 :]
    rows = x_ref.shape[0]
    copies = [pltpu.make_async_copy(conv_ref, conv_out, sems.at[0])]
    cin = x_ref.shape[2]
    chans = cin // parts
    conv = conv_own_ref[...] + bias_ref[...].reshape(1, 1, -1)
    for r in conv_refs:
        conv = conv + r[...].astype(F32)
    conv_ref[...] = conv.astype(BF16)
    copies[0].start()
    wide = []
    for k in range(parts):
        stats = small_ref[k]
        wide.append(jnp.concatenate([stats[2:3], lax.rsqrt(stats[3:4] / count + EPS), sums_ref[k] / count], 0))
    wide = expanded(jnp.concatenate(wide, 0), chans)
    picked = []
    for s in range(parts):
        k = lax.rem(s - info_ref[ME] + parts, parts)
        picked.append([shard_of([wide[4 * j + i : 4 * j + i + 1] for j in range(parts)], k)[None] for i in range(4)])
    half = rows // 2
    for r in range(2):
        at_rows = slice(r * half, (r + 1) * half)
        gx_all = [ref[at_rows].astype(F32) for ref in (gx_own_ref, *gx_refs)]
        for s in range(parts):
            at = slice(s * chans, (s + 1) * chans)
            k = lax.rem(s - info_ref[ME] + parts, parts)
            mean, inv, first, second = picked[s]
            xhat = (x_ref[at_rows, :, at].astype(F32) - mean) * inv
            grad_ref[at_rows, :, at] = (inv * (shard_of(gx_all, k) - first - xhat * second)).astype(BF16)
        copies.append(pltpu.make_async_copy(grad_ref.at[at_rows], grad_out.at[at_rows], sems.at[1 + r]))
        copies[-1].start()
    for copy in copies:
        copy.wait()


def call(kernel, name, outs, operands, scratch=(), in_hbm=(), limit=28, scalars=True, cost=None, outs_in_hbm=False):
    spec = lambda i: pl.BlockSpec(memory_space=pltpu.HBM if i in in_hbm else pltpu.SMEM if scalars and i == 0 else pltpu.VMEM)
    return pl.pallas_call(
        kernel,
        out_shape=outs,
        in_specs=[spec(i) for i in range(len(operands))],
        out_specs=[pl.BlockSpec(memory_space=pl.ANY if outs_in_hbm else pltpu.VMEM)] * len(outs),
        scratch_shapes=scratch,
        compiler_params=pltpu.CompilerParams(vmem_limit_bytes=limit * 2**20),
        cost_estimate=cost,
        name=name,
    )(*operands)


def tied(value, *others):
    for other in others:
        value = value + 0.0 * other[0, :1, : value.shape[-1]].astype(F32)
    return value


def stats_rounds(axis):
    count = lax.axis_size(axis)
    if count == 4:
        return [near, lambda i: i ^ 2]
    return [functools.partial(lambda step, i: i ^ step, 2**j) for j in range(count.bit_length() - 1)]


def body(latents, norm_gain, norm_shift, conv_weight, conv_bias, cotangent):
    _, rows, cols, cin = latents.shape
    outs = cotangent.shape[3]
    chans = conv_weight.shape[2]
    parts = lax.axis_size("dp")
    me = lax.axis_index("dp")
    groups = GROUPS * chans // cin
    both = chans + outs
    n = rows * cols * (cin // GROUPS)
    count = float(n * lax.axis_size("ha") * lax.axis_size("wa"))
    x, cot = latents[0], cotangent[0]
    sds = jax.ShapeDtypeStruct
    where = [lax.axis_index(a) for a in ("ha", "wa")]
    last = [lax.axis_size(a) - 1 for a in ("ha", "wa")]
    info = jnp.stack(
        [me, where[0] % 2 == 0, where[1] % 2 == 0, where[0] > 0, where[0] < last[0], where[1] > 0, where[1] < last[1]]
    ).astype(jnp.int32)

    peers = [[(i, (i + k) % parts) for i in range(parts)] for k in range(1, parts)]
    from_peers = lambda values: [lax.ppermute(v, "dp", pairs) for v, pairs in zip(values, peers)]
    cot_tiles = [cot, *from_peers([cot] * (parts - 1))]
    first = call(
        functools.partial(first_kernel, parts, groups),
        "first",
        [sds((2 * (rows + cols) + 8, chans), BF16)] * parts,
        [info, x],
        cost=pl.CostEstimate(flops=10**10, bytes_accessed=1, transcendentals=0),
    )
    got = from_peers(first[1:])
    tiles = call(
        functools.partial(tiles_kernel, parts),
        "tiles",
        [sds((rows, cols, chans), BF16)] * parts,
        [info, x, conv_weight],
    )
    zero = (0.0 * got[0][:1]).astype(BF16)
    x_tiles = [tiles[0], *from_peers([v + zero[None] for v in tiles[1:]])]
    size = 2 * parts * groups
    pack_near, pack_across, stats = call(
        functools.partial(rows_kernel, parts),
        "rows",
        [sds((parts * cols + 8, both), BF16), sds((parts * cols, both), BF16), sds((1, size), F32)],
        [info, first[0], *got, *cot_tiles],
    )

    def reduced(stats, n, axis, pairings):
        for partner in pairings:
            stats, n = merged(stats, exchange(stats, axis, partner), n), 2 * n
        return stats, n

    rounds_h, rounds_w = stats_rounds("ha"), stats_rounds("wa")
    near_h = exchange(pack_near, "ha", near)
    ends_w = call(
        functools.partial(columns_kernel, parts),
        "columns",
        [sds((2 * rows, both), BF16)] * parts,
        [info, first[0], *got, *cot_tiles, stats],
    )
    stats, n = merged(stats, unpacked(near_h, parts * cols, size), n), 2 * n
    if lax.axis_size("ha") == 4:
        across_h = exchange(packed([pack_across], stats), "ha", across)
        stats, n = merged(stats, unpacked(across_h, parts * cols, size), n), 2 * n
    else:
        across_h = exchange(pack_across, "ha", across)
        stats, n = reduced(stats, n, "ha", rounds_h[1:])
    used = parts * (rows + 2)
    near_w, across_w = call(
        functools.partial(pack_kernel, parts, rows, cols),
        "pack",
        [sds((-(-(used + 3) // 8) * 8, both), BF16), sds((used, both), BF16)],
        [info, near_h, across_h, stats, *ends_w],
    )
    near_w = exchange(near_w, "wa", near)
    across_w = exchange(across_w, "wa", across, ends=False)
    stats, n = merged(stats, unpacked(near_w, used, size), n), 2 * n
    stats, n = reduced(stats, n, "wa", rounds_w[1:])

    strips = [near_h, across_h, near_w, across_w]
    padded = lambda depth: pltpu.VMEM((rows + 2, parts, cols + 8, depth), F32)
    shifted = (3, rows + 2, parts * cols)
    (grad_act,) = call(
        functools.partial(backward_kernel, parts),
        "conv_backward",
        [sds((rows, parts, cols, chans), F32)],
        [info, *cot_tiles, *strips, conv_weight, *x_tiles[1:]],
        [padded(outs), pltpu.VMEM((*shifted, outs), BF16)],
    )
    *small, gx_own, gx_other, act, scales = call(
        functools.partial(terms_kernel, parts, count),
        "terms",
        [
            *[sds((4, groups), F32)] * parts,
            sds((rows, cols, chans), F32),
            sds((parts - 1, rows, cols, chans), BF16),
            sds((rows, parts, cols + 8, chans), F32),
            sds((2 * parts + 2, chans), F32),
        ],
        [info, *x_tiles, stats, norm_gain, norm_shift, grad_act],
    )

    to_owners = lambda values: [lax.ppermute(v, "dp", [(j, i) for i, j in pairs]) for v, pairs in zip(values, peers)]
    small = jnp.stack([small[0], *to_owners(small[1:])], 0)
    gx = to_owners([gx_other[k] for k in range(parts - 1)])
    conv_own, conv_other = call(
        functools.partial(forward_kernel, parts),
        "conv_forward",
        [sds((rows, cols, outs), F32), sds((parts - 1, rows, cols, outs), BF16)],
        [info, act, scales, *strips, conv_weight],
        [padded(chans), pltpu.VMEM((*shifted, chans), BF16)],
    )
    conv = to_owners([conv_other[k] for k in range(parts - 1)])
    sums = tied(small[:, :2], conv_own)
    for axis, pairings in (("ha", rounds_h), ("wa", rounds_w)):
        for partner in pairings:
            sums = sums + exchange(sums, axis, partner)
    conv_out, grad = call(
        functools.partial(finish_kernel, parts, count),
        "finish",
        [sds((rows, cols, outs), BF16), sds((rows, cols, cin), BF16)],
        [info, x, small, sums, conv_bias, gx_own, conv_own, *gx, *conv],
        [pltpu.VMEM((rows, cols, outs), BF16), pltpu.VMEM((rows, cols, cin), BF16), pltpu.SemaphoreType.DMA((3,))],
        outs_in_hbm=True,
    )
    return conv_out[None], grad[None]


def solution(mesh):
    tile = P("dp", "ha", "wa", None)
    return jax.shard_map(
        body,
        mesh=mesh,
        in_specs=(tile, P(), P(), P(None, None, "dp", None), P(), tile),
        out_specs=(tile, tile),
        check_vma=False,
    )
```

```python
import functools

import jax
import jax.numpy as jnp
from jax import lax
from jax.experimental import pallas as pl
from jax.experimental.pallas import tpu as pltpu
from jax.sharding import PartitionSpec as P

GROUPS = 32
EPS = 1e-05
F32 = jnp.float32
BF16 = jnp.bfloat16

ME, EVEN_H, EVEN_W, UP, DOWN, LEFT, RIGHT = range(7)


def exchange(value, axis, partner, ends=True):
    count = lax.axis_size(axis)
    pairs = [(i, partner(i) % count) for i in range(count)]
    if not ends:
        pairs = [(i, j) for i, j in pairs if abs(i - j) == 1]
    return lax.ppermute(value, axis, pairs)


def near(i):
    return i ^ 1


def across(i):
    return i - 1 if i % 2 == 0 else i + 1


def merged(stats, other, n):
    half = stats.shape[1] // 2
    delta = other[:, :half] - stats[:, :half]
    return jnp.concatenate([stats[:, :half] + 0.5 * delta, stats[:, half:] + other[:, half:] + (0.5 * n) * delta * delta], 1)


def packed(strips, stats):
    high = lax.reduce_precision(stats, 8, 7)
    middle = lax.reduce_precision(stats - high, 8, 7)
    low = lax.reduce_precision(stats - high - middle, 8, 7)
    rows = jnp.concatenate([high, middle, low], 0).astype(BF16)
    rows = jnp.pad(rows, ((0, 0), (0, strips[0].shape[1] - rows.shape[1])))
    return jnp.concatenate([*strips, rows], 0)


def unpacked(pack, r, size):
    rows = pack[r : r + 3, :size].astype(F32)
    return rows[:1] + rows[1:2] + rows[2:]


def members(groups, chans, dim):
    per_group = chans // groups
    shape = (groups, chans) if dim else (chans, groups)
    chan = lax.broadcasted_iota(jnp.int32, shape, dim)
    group = lax.broadcasted_iota(jnp.int32, shape, 1 - dim)
    return ((chan >= group * per_group) & (chan < (group + 1) * per_group)).astype(F32)


def three_parts(a):
    high = a.astype(BF16)
    rest = a - high.astype(F32)
    middle = rest.astype(BF16)
    return high, middle, (rest - middle.astype(F32)).astype(BF16)


def exact_dot(a, b):
    rows = a.shape[0]
    parts = jnp.concatenate([p.astype(F32) for p in three_parts(a)], 0).astype(BF16)
    sums = jnp.dot(parts, b.astype(BF16), preferred_element_type=F32)
    return sums[:rows] + sums[rows : 2 * rows] + sums[2 * rows :]


def expanded(values, chans):
    return exact_dot(values, members(values.shape[-1], chans, 1))


def gathered(values, groups):
    return exact_dot(values, members(groups, values.shape[-1], 0))


def shard_of(pieces, shard):
    value = pieces[0]
    for i in range(1, len(pieces)):
        value = jnp.where(shard == i, pieces[i], value)
    return value


def first_kernel(parts, groups, info_ref, x_ref, *out_refs):
    rows, cols, cin = x_ref.shape
    chans = cin // parts
    n = rows * cols * (chans // groups)
    me = info_ref[ME]
    even_h = info_ref[EVEN_H] > 0
    shards = [x_ref[:, :, s * chans : (s + 1) * chans].astype(F32) for s in range(parts)]
    stats = []
    for x in shards:
        flat = x.reshape(rows * cols, chans)
        mean = gathered(jnp.sum(flat, axis=0, keepdims=True), groups) / n
        centered = flat - expanded(mean, chans)
        squares = gathered(jnp.sum(centered * centered, axis=0, keepdims=True), groups)
        stats.append(jnp.concatenate([p.astype(F32) for p in three_parts(jnp.concatenate([mean, squares], 1))], 0))
    ends = [jnp.concatenate(row_ends(x, even_h), 0) for x in shards]
    columns = [column_ends(x, info_ref[EVEN_W] > 0) for x in shards]
    for k, ref in enumerate(out_refs):
        shard = lax.rem(me + k, parts)
        ref[: 2 * cols, :] = shard_of(ends, shard).astype(BF16)
        ref[2 * cols : 2 * cols + 8, :] = jnp.zeros((8, chans), BF16)
        ref[2 * cols : 2 * cols + 3, : 2 * groups] = shard_of(stats, shard).astype(BF16)
        ref[2 * cols + 8 :, :] = shard_of(columns, shard).astype(BF16)


def row_ends(t, even_h):
    first, last = t[0], t[t.shape[0] - 1]
    return jnp.where(even_h, last, first), jnp.where(even_h, first, last)


def column_ends(t, even_w):
    first, last = t[:, 0, :], t[:, t.shape[1] - 1, :]
    return jnp.concatenate([jnp.where(even_w, last, first), jnp.where(even_w, first, last)], 0)


def tiles_kernel(parts, info_ref, x_ref, w_ref, *out_refs):
    chans = x_ref.shape[2] // parts
    for k in range(parts):
        shard = lax.rem(info_ref[ME] + k, parts)
        out_refs[k][...] = shard_of([x_ref[:, :, s * chans : (s + 1) * chans].astype(F32) for s in range(parts)], shard).astype(BF16)


def rows_kernel(parts, info_ref, *refs):
    packs, cots, (near_ref, across_ref, stats_ref) = refs[:parts], refs[parts : 2 * parts], refs[2 * parts :]
    rows, cols, outs = cots[0].shape
    chans = packs[0].shape[1]
    groups = stats_ref.shape[1] // (2 * parts)
    even_h = info_ref[EVEN_H] > 0
    packs = [ref[...].astype(F32) for ref in packs]
    cot_ends = [row_ends(ref[...].astype(F32), even_h) for ref in cots]
    local = [v[2 * cols : 2 * cols + 3, : 2 * groups] for v in packs]
    terms = jnp.concatenate([v[:, :groups] for v in local] + [v[:, groups:] for v in local], 1)
    stats_ref[...] = terms[0:1] + terms[1:2] + terms[2:3]
    tail = jnp.concatenate([terms, jnp.zeros((3, chans + outs - terms.shape[1]), F32)], 1)
    for half, ref in enumerate((near_ref, across_ref)):
        strips = [jnp.concatenate([v[half * cols : (half + 1) * cols], c[half]], 1) for v, c in zip(packs, cot_ends)]
        ref[...] = jnp.concatenate(strips + ([tail, jnp.zeros((5, chans + outs), F32)] if half == 0 else []), 0).astype(BF16)


def columns_kernel(parts, info_ref, *refs):
    even_w = info_ref[EVEN_W] > 0
    for pack_ref, cot_ref, ref in zip(refs[:parts], refs[parts : 2 * parts], refs[2 * parts + 1 :]):
        rows, cols, _ = cot_ref.shape
        chans = pack_ref.shape[1]
        ref[:, :chans] = pack_ref[...].astype(F32)[2 * cols + 8 :].astype(BF16)
        ref[:, chans:] = column_ends(cot_ref[...].astype(F32), even_w).astype(BF16)


def pack_kernel(parts, rows, cols, info_ref, near_h, across_h, stats_ref, *refs):
    ends, (near_ref, across_ref) = refs[:parts], refs[parts:]
    even_w = info_ref[EVEN_W] > 0
    both = near_ref.shape[1]
    near_rows = near_h[...].astype(F32)
    across_rows = jnp.where((info_ref[UP] > 0) & (info_ref[DOWN] > 0), across_h[...].astype(F32), 0.0)
    columns = [ref[...].astype(F32) for ref in ends]
    stats = jnp.concatenate([p.astype(F32) for p in three_parts(stats_ref[...])], 0)
    stats = jnp.concatenate([stats, jnp.zeros((3, both - stats.shape[1]), F32)], 1)
    for half, ref, pick_last in ((0, near_ref, even_w), (1, across_ref, jnp.logical_not(even_w))):
        corners = []
        for t in (near_rows, across_rows):
            for k in range(parts):
                first, last = t[k * cols : k * cols + 1], t[(k + 1) * cols - 1 : (k + 1) * cols]
                corners.append(jnp.where(pick_last, last, first))
        pieces = [v[half * rows : (half + 1) * rows] for v in columns] + corners + ([stats] if half == 0 else [])
        used = parts * (rows + 2) + (3 if half == 0 else 0)
        if ref.shape[0] > used:
            pieces.append(jnp.zeros((ref.shape[0] - used, both), F32))
        ref[...] = jnp.concatenate(pieces, 0).astype(BF16)


def halos(parts, rows, cols, info_ref, near_h, across_h, near_w, across_w, lanes):
    even_h = info_ref[EVEN_H] > 0
    even_w = info_ref[EVEN_W] > 0
    part = lambda ref, r: ref[:, lanes].astype(F32)[:r]
    a, b = (part(ref, parts * cols) for ref in (near_h, across_h))
    b = jnp.where((info_ref[UP] > 0) & (info_ref[DOWN] > 0), b, 0.0)
    above_all, below_all = jnp.where(even_h, b, a), jnp.where(even_h, a, b)
    c, d = (part(ref, parts * (rows + 2)) for ref in (near_w, across_w))
    before_all, after_all = jnp.where(even_w, d, c), jnp.where(even_w, c, d)

    def strips(k):
        def ordered(t):
            head, tail = t[parts * rows + k :][:1], t[parts * (rows + 1) + k :][:1]
            return jnp.where(even_h, tail, head), t[k * rows : (k + 1) * rows], jnp.where(even_h, head, tail)

        at = slice(k * cols, (k + 1) * cols)
        return above_all[at], below_all[at], ordered(before_all), ordered(after_all)

    return strips


def windows(padded_ref, windows_ref, k_all, cols):
    for kx in range(3):
        view = padded_ref[:, :, kx : kx + cols, :]
        windows_ref[kx] = view.reshape(view.shape[0], k_all * cols, view.shape[3]).astype(BF16)


def backward_kernel(parts, info_ref, *refs):
    tiles, (near_h, across_h, near_w, across_w, w_ref, *_, grad_ref, padded_ref, windows_ref) = refs[:parts], refs[parts:]
    rows, cols, outs = tiles[0].shape
    chans = w_ref.shape[2]
    strips = halos(parts, rows, cols, info_ref, near_h, across_h, near_w, across_w, slice(chans, chans + outs))
    for k in range(parts):
        above, below, before, after = strips(k)
        padded_ref[1 : rows + 1, k, 1 : cols + 1, :] = tiles[k][...].astype(F32)
        padded_ref[0, k, 1 : cols + 1, :] = above
        padded_ref[rows + 1, k, 1 : cols + 1, :] = below
        for at, (top, mid, bottom) in ((0, before), (cols + 1, after)):
            padded_ref[0, k, at : at + 1, :] = top
            padded_ref[1 : rows + 1, k, at, :] = mid
            padded_ref[rows + 1, k, at : at + 1, :] = bottom
    windows(padded_ref, windows_ref, parts, cols)
    taps = [(ky, kx) for ky in range(3) for kx in range(3)]
    shifted = jnp.concatenate([windows_ref[kx, ky : ky + rows].reshape(rows * parts * cols, outs) for ky, kx in taps], 1)
    weight = jnp.concatenate([w_ref[2 - ky, 2 - kx] for ky, kx in taps], 1)
    total = lax.dot_general(weight, shifted, (((1,), (1,)), ((), ())), preferred_element_type=F32)
    grad_ref[...] = total.T.reshape(rows, parts, cols, chans)


def terms_kernel(parts, count, info_ref, *refs):
    tiles = refs[:parts]
    stats_ref, gain_ref, shift_ref, grad_ref = refs[parts : parts + 4]
    moments_refs, (gx_own_ref, gx_other_ref, padded_ref, scales_ref) = refs[parts + 4 : -4], refs[-4:]
    rows, cols, _ = tiles[0].shape
    chans = grad_ref.shape[3]
    groups = stats_ref.shape[1] // (2 * parts)
    stats = jnp.concatenate([stats_ref[:, i * groups : (i + 1) * groups] for i in range(2 * parts)], 0)
    wide = expanded(jnp.concatenate([stats[:parts], lax.rsqrt(stats[parts:] / count + EPS)], 0), chans)
    means, invs = wide[:parts], wide[parts:]
    mine = lambda ref: shard_of([ref[s * chans : (s + 1) * chans].reshape(1, chans) for s in range(parts)], info_ref[ME])
    gain, shift = mine(gain_ref), mine(shift_ref)
    scales_ref[...] = jnp.concatenate([wide, gain, shift], 0)
    firsts, seconds = [], []
    for k in range(parts):
        mean, inv = means[k : k + 1], invs[k : k + 1]
        xhat = (tiles[k][...].astype(F32) - mean[None]) * inv[None]
        z = xhat * gain[None] + shift[None]
        sig = jax.nn.sigmoid(z)
        padded_ref[:, k, 1 : cols + 1, :] = z * sig
        gx = grad_ref[:, k] * sig * (1.0 + z * (1.0 - sig)) * gain[None]
        if k == 0:
            gx_own_ref[...] = gx
        else:
            gx_other_ref[k - 1] = gx.astype(BF16)
        firsts.append(jnp.sum(gx.reshape(rows * cols, chans), axis=0, keepdims=True))
        seconds.append(jnp.sum((gx * xhat).reshape(rows * cols, chans), axis=0, keepdims=True))
    sums = gathered(jnp.concatenate(firsts + seconds, 0), groups)
    for k, ref in enumerate(moments_refs):
        ref[...] = jnp.concatenate([v[k : k + 1] for v in (sums[:parts], sums[parts:], stats[:parts], stats[parts:])], 0)


def forward_kernel(parts, info_ref, given_ref, scales_ref, near_h, across_h, near_w, across_w, w_ref, conv_own_ref, conv_other_ref, windows_ref, padded_ref):
    rows, cols, outs = conv_own_ref.shape
    chans = windows_ref.shape[3]
    strips = halos(parts, rows, cols, info_ref, near_h, across_h, near_w, across_w, slice(0, chans))
    up, down, left, right = (info_ref[i] > 0 for i in (UP, DOWN, LEFT, RIGHT))
    scales = scales_ref[...]
    gain, shift = scales[2 * parts : 2 * parts + 1], scales[2 * parts + 1 : 2 * parts + 2]
    padded_ref[1 : rows + 1] = given_ref[...]
    for k in range(parts):
        mean, inv = scales[k : k + 1], scales[parts + k : parts + k + 1]

        def act_of(t, inside):
            z = (t - mean) * inv * gain + shift
            return jnp.where(inside, z * jax.nn.sigmoid(z), 0.0)

        above, below, before, after = strips(k)
        padded_ref[0, k, 1 : cols + 1, :] = act_of(above, up)
        padded_ref[rows + 1, k, 1 : cols + 1, :] = act_of(below, down)
        for at, (top, mid, bottom), side in ((0, before, left), (cols + 1, after, right)):
            padded_ref[0, k, at : at + 1, :] = act_of(top, side & up)
            padded_ref[1 : rows + 1, k, at, :] = act_of(mid, side)
            padded_ref[rows + 1, k, at : at + 1, :] = act_of(bottom, side & down)
    windows(padded_ref, windows_ref, parts, cols)
    convolved(parts, windows_ref, w_ref, slice(0, outs), conv_own_ref, conv_other_ref)


def second_forward_kernel(parts, start, windows_ref, w_ref, after_ref, conv_own_ref, conv_other_ref):
    convolved(parts, windows_ref, w_ref, slice(start, w_ref.shape[3]), conv_own_ref, conv_other_ref)


def convolved(parts, windows_ref, w_ref, lanes, conv_own_ref, conv_other_ref):
    rows, cols, outs = conv_own_ref.shape
    chans = windows_ref.shape[3]
    taps = [(ky, kx) for ky in range(3) for kx in range(3)]
    shifted = jnp.concatenate([windows_ref[kx, ky : ky + rows].reshape(rows * parts * cols, chans) for ky, kx in taps], 1)
    weight = w_ref[:, :, :, lanes].reshape(9 * chans, outs)
    total = lax.dot_general(weight, shifted, (((0,), (1,)), ((), ())), preferred_element_type=F32).T
    total = total.reshape(rows, parts, cols, outs)
    conv_own_ref[...] = total[:, 0]
    for k in range(1, parts):
        conv_other_ref[k - 1] = total[:, k].astype(BF16)


def finish_kernel(parts, count, info_ref, x_ref, small_ref, sums_ref, bias_ref, gx_own_ref, *refs):
    gx_refs, conv_refs = refs[: parts - 1], refs[parts - 1 : 3 * parts - 1]
    conv_out, grad_out, conv_ref, grad_ref, sems = refs[3 * parts - 1 :]
    rows = x_ref.shape[0]
    copies = [pltpu.make_async_copy(conv_ref, conv_out, sems.at[0])]
    cin = x_ref.shape[2]
    chans = cin // parts
    start = 0
    for i in range(2):
        conv = sum(r[...].astype(F32) for r in conv_refs[i::2])
        stop = start + conv.shape[2]
        conv_ref[:, :, start:stop] = (conv + bias_ref[start:stop].reshape(1, 1, -1)).astype(BF16)
        start = stop
    copies[0].start()
    wide = []
    for k in range(parts):
        stats = small_ref[k]
        wide.append(jnp.concatenate([stats[2:3], lax.rsqrt(stats[3:4] / count + EPS), sums_ref[k] / count], 0))
    wide = expanded(jnp.concatenate(wide, 0), chans)
    picked = []
    for s in range(parts):
        k = lax.rem(s - info_ref[ME] + parts, parts)
        picked.append([shard_of([wide[4 * j + i : 4 * j + i + 1] for j in range(parts)], k)[None] for i in range(4)])
    half = rows // 2
    for r in range(2):
        at_rows = slice(r * half, (r + 1) * half)
        gx_all = [ref[at_rows].astype(F32) for ref in (gx_own_ref, *gx_refs)]
        for s in range(parts):
            at = slice(s * chans, (s + 1) * chans)
            k = lax.rem(s - info_ref[ME] + parts, parts)
            mean, inv, first, second = picked[s]
            xhat = (x_ref[at_rows, :, at].astype(F32) - mean) * inv
            grad_ref[at_rows, :, at] = (inv * (shard_of(gx_all, k) - first - xhat * second)).astype(BF16)
        copies.append(pltpu.make_async_copy(grad_ref.at[at_rows], grad_out.at[at_rows], sems.at[1 + r]))
        copies[-1].start()
    for copy in copies:
        copy.wait()


def call(kernel, name, outs, operands, scratch=(), in_hbm=(), limit=28, scalars=True, cost=None, outs_in_hbm=False):
    spec = lambda i: pl.BlockSpec(memory_space=pltpu.HBM if i in in_hbm else pltpu.SMEM if scalars and i == 0 else pltpu.VMEM)
    return pl.pallas_call(
        kernel,
        out_shape=outs,
        in_specs=[spec(i) for i in range(len(operands))],
        out_specs=[pl.BlockSpec(memory_space=pl.ANY if outs_in_hbm else pltpu.VMEM)] * len(outs),
        scratch_shapes=scratch,
        compiler_params=pltpu.CompilerParams(vmem_limit_bytes=limit * 2**20),
        cost_estimate=cost,
        name=name,
    )(*operands)


def tied(value, *others):
    for other in others:
        value = value + 0.0 * other[0, :1, : value.shape[-1]].astype(F32)
    return value


def stats_rounds(axis):
    count = lax.axis_size(axis)
    if count == 4:
        return [near, lambda i: i ^ 2]
    return [functools.partial(lambda step, i: i ^ step, 2**j) for j in range(count.bit_length() - 1)]


def body(latents, norm_gain, norm_shift, conv_weight, conv_bias, cotangent):
    _, rows, cols, cin = latents.shape
    outs = cotangent.shape[3]
    chans = conv_weight.shape[2]
    parts = lax.axis_size("dp")
    me = lax.axis_index("dp")
    groups = GROUPS * chans // cin
    both = chans + outs
    n = rows * cols * (cin // GROUPS)
    count = float(n * lax.axis_size("ha") * lax.axis_size("wa"))
    x, cot = latents[0], cotangent[0]
    sds = jax.ShapeDtypeStruct
    where = [lax.axis_index(a) for a in ("ha", "wa")]
    last = [lax.axis_size(a) - 1 for a in ("ha", "wa")]
    info = jnp.stack(
        [me, where[0] % 2 == 0, where[1] % 2 == 0, where[0] > 0, where[0] < last[0], where[1] > 0, where[1] < last[1]]
    ).astype(jnp.int32)

    peers = [[(i, (i + k) % parts) for i in range(parts)] for k in range(1, parts)]
    from_peers = lambda values: [lax.ppermute(v, "dp", pairs) for v, pairs in zip(values, peers)]
    cot_tiles = [cot, *from_peers([cot] * (parts - 1))]
    first = call(
        functools.partial(first_kernel, parts, groups),
        "first",
        [sds((2 * (rows + cols) + 8, chans), BF16)] * parts,
        [info, x],
        cost=pl.CostEstimate(flops=10**10, bytes_accessed=1, transcendentals=0),
    )
    got = from_peers(first[1:])
    tiles = call(
        functools.partial(tiles_kernel, parts),
        "tiles",
        [sds((rows, cols, chans), BF16)] * parts,
        [info, x, conv_weight],
    )
    zero = (0.0 * got[0][:1]).astype(BF16)
    x_tiles = [tiles[0], *from_peers([v + zero[None] for v in tiles[1:]])]
    size = 2 * parts * groups
    pack_near, pack_across, stats = call(
        functools.partial(rows_kernel, parts),
        "rows",
        [sds((parts * cols + 8, both), BF16), sds((parts * cols, both), BF16), sds((1, size), F32)],
        [info, first[0], *got, *cot_tiles],
    )

    def reduced(stats, n, axis, pairings):
        for partner in pairings:
            stats, n = merged(stats, exchange(stats, axis, partner), n), 2 * n
        return stats, n

    rounds_h, rounds_w = stats_rounds("ha"), stats_rounds("wa")
    near_h = exchange(pack_near, "ha", near)
    ends_w = call(
        functools.partial(columns_kernel, parts),
        "columns",
        [sds((2 * rows, both), BF16)] * parts,
        [info, first[0], *got, *cot_tiles, stats],
    )
    stats, n = merged(stats, unpacked(near_h, parts * cols, size), n), 2 * n
    if lax.axis_size("ha") == 4:
        across_h = exchange(packed([pack_across], stats), "ha", across)
        stats, n = merged(stats, unpacked(across_h, parts * cols, size), n), 2 * n
    else:
        across_h = exchange(pack_across, "ha", across)
        stats, n = reduced(stats, n, "ha", rounds_h[1:])
    used = parts * (rows + 2)
    near_w, across_w = call(
        functools.partial(pack_kernel, parts, rows, cols),
        "pack",
        [sds((-(-(used + 3) // 8) * 8, both), BF16), sds((used, both), BF16)],
        [info, near_h, across_h, stats, *ends_w],
    )
    near_w = exchange(near_w, "wa", near)
    across_w = exchange(across_w, "wa", across, ends=False)
    stats, n = merged(stats, unpacked(near_w, used, size), n), 2 * n
    stats, n = reduced(stats, n, "wa", rounds_w[1:])

    strips = [near_h, across_h, near_w, across_w]
    padded = lambda depth: pltpu.VMEM((rows + 2, parts, cols + 8, depth), F32)
    shifted = (3, rows + 2, parts * cols)
    (grad_act,) = call(
        functools.partial(backward_kernel, parts),
        "conv_backward",
        [sds((rows, parts, cols, chans), F32)],
        [info, *cot_tiles, *strips, conv_weight, *x_tiles[1:]],
        [padded(outs), pltpu.VMEM((*shifted, outs), BF16)],
    )
    *small, gx_own, gx_other, act, scales = call(
        functools.partial(terms_kernel, parts, count),
        "terms",
        [
            *[sds((4, groups), F32)] * parts,
            sds((rows, cols, chans), F32),
            sds((parts - 1, rows, cols, chans), BF16),
            sds((rows, parts, cols + 8, chans), F32),
            sds((2 * parts + 2, chans), F32),
        ],
        [info, *x_tiles, stats, norm_gain, norm_shift, grad_act],
    )

    to_owners = lambda values: [lax.ppermute(v, "dp", [(j, i) for i, j in pairs]) for v, pairs in zip(values, peers)]
    small = jnp.stack([small[0], *to_owners(small[1:])], 0)
    gx = to_owners([gx_other[k] for k in range(parts - 1)])
    start = outs * 3 // 5 // 128 * 128
    parts_of = lambda size: [sds((rows, cols, size), F32), sds((parts - 1, rows, cols, size), BF16)]
    conv_own, conv_other, act_windows = call(
        functools.partial(forward_kernel, parts),
        "conv_forward",
        [*parts_of(start), sds((*shifted, chans), BF16)],
        [info, act, scales, *strips, conv_weight],
        [padded(chans)],
    )
    sums = tied(small[:, :2], conv_own)
    sums = sums + exchange(sums, "ha", rounds_h[0])
    conv_own2, conv_other2 = call(
        functools.partial(second_forward_kernel, parts, start),
        "conv_forward2",
        parts_of(outs - start),
        [act_windows, conv_weight, sums],
        scalars=False,
    )
    conv = [conv_own, conv_own2]
    for k in range(parts - 1):
        back = [(j, i) for i, j in peers[k]]
        conv += [lax.ppermute(v[k], "dp", back) for v in (conv_other, conv_other2)]
    for partner in rounds_h[1:]:
        sums = sums + exchange(sums, "ha", partner)
    sums = tied(sums, conv_own2)
    for partner in rounds_w:
        sums = sums + exchange(sums, "wa", partner)
    conv_out, grad = call(
        functools.partial(finish_kernel, parts, count),
        "finish",
        [sds((rows, cols, outs), BF16), sds((rows, cols, cin), BF16)],
        [info, x, small, sums, conv_bias, gx_own, *gx, *conv],
        [pltpu.VMEM((rows, cols, outs), BF16), pltpu.VMEM((rows, cols, cin), BF16), pltpu.SemaphoreType.DMA((3,))],
        outs_in_hbm=True,
    )
    return conv_out[None], grad[None]


def solution(mesh):
    tile = P("dp", "ha", "wa", None)
    return jax.shard_map(
        body,
        mesh=mesh,
        in_specs=(tile, P(), P(), P(None, None, "dp", None), P(), tile),
        out_specs=(tile, tile),
        check_vma=False,
    )
```

```python
import functools

import jax
import jax.numpy as jnp
from jax import lax
from jax.experimental import pallas as pl
from jax.experimental.pallas import tpu as pltpu
from jax.sharding import PartitionSpec as P

GROUPS = 32
EPS = 1e-05
F32 = jnp.float32
BF16 = jnp.bfloat16

ME, EVEN_H, EVEN_W, UP, DOWN, LEFT, RIGHT = range(7)


def exchange(value, axis, partner, ends=True):
    count = lax.axis_size(axis)
    pairs = [(i, partner(i) % count) for i in range(count)]
    if not ends:
        pairs = [(i, j) for i, j in pairs if abs(i - j) == 1]
    return lax.ppermute(value, axis, pairs)


def near(i):
    return i ^ 1


def across(i):
    return i - 1 if i % 2 == 0 else i + 1


def merged(stats, other, n):
    half = stats.shape[1] // 2
    delta = other[:, :half] - stats[:, :half]
    return jnp.concatenate([stats[:, :half] + 0.5 * delta, stats[:, half:] + other[:, half:] + (0.5 * n) * delta * delta], 1)


def packed(strips, stats):
    high = lax.reduce_precision(stats, 8, 7)
    middle = lax.reduce_precision(stats - high, 8, 7)
    low = lax.reduce_precision(stats - high - middle, 8, 7)
    rows = jnp.concatenate([high, middle, low], 0).astype(BF16)
    rows = jnp.pad(rows, ((0, 0), (0, strips[0].shape[1] - rows.shape[1])))
    return jnp.concatenate([*strips, rows], 0)


def unpacked(pack, r, size):
    rows = pack[r : r + 3, :size].astype(F32)
    return rows[:1] + rows[1:2] + rows[2:]


def members(groups, chans, dim):
    per_group = chans // groups
    shape = (groups, chans) if dim else (chans, groups)
    chan = lax.broadcasted_iota(jnp.int32, shape, dim)
    group = lax.broadcasted_iota(jnp.int32, shape, 1 - dim)
    return ((chan >= group * per_group) & (chan < (group + 1) * per_group)).astype(F32)


def three_parts(a):
    high = a.astype(BF16)
    rest = a - high.astype(F32)
    middle = rest.astype(BF16)
    return high, middle, (rest - middle.astype(F32)).astype(BF16)


def exact_dot(a, b):
    rows = a.shape[0]
    parts = jnp.concatenate([p.astype(F32) for p in three_parts(a)], 0).astype(BF16)
    sums = jnp.dot(parts, b.astype(BF16), preferred_element_type=F32)
    return sums[:rows] + sums[rows : 2 * rows] + sums[2 * rows :]


def expanded(values, chans):
    return exact_dot(values, members(values.shape[-1], chans, 1))


def gathered(values, groups):
    return exact_dot(values, members(groups, values.shape[-1], 0))


def shard_of(pieces, shard):
    value = pieces[0]
    for i in range(1, len(pieces)):
        value = jnp.where(shard == i, pieces[i], value)
    return value


def first_kernel(parts, groups, info_ref, x_ref, *out_refs):
    rows, cols, cin = x_ref.shape
    chans = cin // parts
    n = rows * cols * (chans // groups)
    me = info_ref[ME]
    even_h = info_ref[EVEN_H] > 0
    shards = [x_ref[:, :, s * chans : (s + 1) * chans].astype(F32) for s in range(parts)]
    stats = []
    for x in shards:
        flat = x.reshape(rows * cols, chans)
        mean = gathered(jnp.sum(flat, axis=0, keepdims=True), groups) / n
        centered = flat - expanded(mean, chans)
        squares = gathered(jnp.sum(centered * centered, axis=0, keepdims=True), groups)
        stats.append(jnp.concatenate([p.astype(F32) for p in three_parts(jnp.concatenate([mean, squares], 1))], 0))
    pieces = []
    for x, terms in zip(shards, stats):
        terms = jnp.concatenate([terms, jnp.zeros((3, chans - 2 * groups), F32)], 1)
        pieces.append(jnp.concatenate([*row_ends(x, even_h), terms, jnp.zeros((5, chans), F32), column_ends(x, info_ref[EVEN_W] > 0)], 0))
    for k, ref in enumerate(out_refs):
        ref[...] = shard_of(pieces, lax.rem(me + k, parts)).astype(BF16)


def row_ends(t, even_h):
    first, last = t[0], t[t.shape[0] - 1]
    return jnp.where(even_h, last, first), jnp.where(even_h, first, last)


def column_ends(t, even_w):
    first, last = t[:, 0, :], t[:, t.shape[1] - 1, :]
    return jnp.concatenate([jnp.where(even_w, last, first), jnp.where(even_w, first, last)], 0)


def tiles_kernel(parts, info_ref, x_ref, w_ref, *out_refs):
    chans = x_ref.shape[2] // parts
    for k in range(parts):
        shard = lax.rem(info_ref[ME] + k, parts)
        out_refs[k][...] = shard_of([x_ref[:, :, s * chans : (s + 1) * chans].astype(F32) for s in range(parts)], shard).astype(BF16)


def rows_kernel(parts, info_ref, *refs):
    packs, cots, (near_ref, across_ref, stats_ref) = refs[:parts], refs[parts : 2 * parts], refs[2 * parts :]
    rows, cols, outs = cots[0].shape
    chans = packs[0].shape[1]
    groups = stats_ref.shape[1] // (2 * parts)
    even_h = info_ref[EVEN_H] > 0
    packs = [ref[...].astype(F32) for ref in packs]
    cot_ends = [row_ends(ref[...].astype(F32), even_h) for ref in cots]
    local = [v[2 * cols : 2 * cols + 3, : 2 * groups] for v in packs]
    terms = jnp.concatenate([v[:, :groups] for v in local] + [v[:, groups:] for v in local], 1)
    stats_ref[...] = terms[0:1] + terms[1:2] + terms[2:3]
    tail = jnp.concatenate([terms, jnp.zeros((3, chans + outs - terms.shape[1]), F32)], 1)
    for half, ref in enumerate((near_ref, across_ref)):
        strips = [jnp.concatenate([v[half * cols : (half + 1) * cols], c[half]], 1) for v, c in zip(packs, cot_ends)]
        ref[...] = jnp.concatenate(strips + ([tail, jnp.zeros((5, chans + outs), F32)] if half == 0 else []), 0).astype(BF16)


def columns_kernel(parts, info_ref, *refs):
    even_w = info_ref[EVEN_W] > 0
    for pack_ref, cot_ref, ref in zip(refs[:parts], refs[parts : 2 * parts], refs[2 * parts + 1 :]):
        rows, cols, _ = cot_ref.shape
        chans = pack_ref.shape[1]
        ref[:, :chans] = pack_ref[...].astype(F32)[2 * cols + 8 :].astype(BF16)
        ref[:, chans:] = column_ends(cot_ref[...].astype(F32), even_w).astype(BF16)


def pack_kernel(parts, rows, cols, info_ref, near_h, across_h, stats_ref, *refs):
    ends, (near_ref, across_ref) = refs[:parts], refs[parts:]
    even_w = info_ref[EVEN_W] > 0
    both = near_ref.shape[1]
    near_rows = near_h[...].astype(F32)
    across_rows = jnp.where((info_ref[UP] > 0) & (info_ref[DOWN] > 0), across_h[...].astype(F32), 0.0)
    columns = [ref[...].astype(F32) for ref in ends]
    stats = jnp.concatenate([p.astype(F32) for p in three_parts(stats_ref[...])], 0)
    stats = jnp.concatenate([stats, jnp.zeros((3, both - stats.shape[1]), F32)], 1)
    for half, ref, pick_last in ((0, near_ref, even_w), (1, across_ref, jnp.logical_not(even_w))):
        corners = []
        for t in (near_rows, across_rows):
            for k in range(parts):
                first, last = t[k * cols : k * cols + 1], t[(k + 1) * cols - 1 : (k + 1) * cols]
                corners.append(jnp.where(pick_last, last, first))
        pieces = [v[half * rows : (half + 1) * rows] for v in columns] + corners + ([stats] if half == 0 else [])
        used = parts * (rows + 2) + (3 if half == 0 else 0)
        if ref.shape[0] > used:
            pieces.append(jnp.zeros((ref.shape[0] - used, both), F32))
        ref[...] = jnp.concatenate(pieces, 0).astype(BF16)


def halos(parts, rows, cols, info_ref, near_h, across_h, near_w, across_w, lanes):
    even_h = info_ref[EVEN_H] > 0
    even_w = info_ref[EVEN_W] > 0
    part = lambda ref, r: ref[:, lanes].astype(F32)[:r]
    a, b = (part(ref, parts * cols) for ref in (near_h, across_h))
    b = jnp.where((info_ref[UP] > 0) & (info_ref[DOWN] > 0), b, 0.0)
    above_all, below_all = jnp.where(even_h, b, a), jnp.where(even_h, a, b)
    c, d = (part(ref, parts * (rows + 2)) for ref in (near_w, across_w))
    before_all, after_all = jnp.where(even_w, d, c), jnp.where(even_w, c, d)

    def strips(k):
        def ordered(t):
            head, tail = t[parts * rows + k :][:1], t[parts * (rows + 1) + k :][:1]
            return jnp.where(even_h, tail, head), t[k * rows : (k + 1) * rows], jnp.where(even_h, head, tail)

        at = slice(k * cols, (k + 1) * cols)
        return above_all[at], below_all[at], ordered(before_all), ordered(after_all)

    return strips


def windows(padded_ref, windows_ref, k_all, cols):
    for kx in range(3):
        view = padded_ref[:, :, kx : kx + cols, :]
        windows_ref[kx] = view.reshape(view.shape[0], k_all * cols, view.shape[3]).astype(BF16)


def backward_kernel(parts, info_ref, *refs):
    tiles, (near_h, across_h, near_w, across_w, w_ref, *_, grad_ref, padded_ref, windows_ref) = refs[:parts], refs[parts:]
    rows, cols, outs = tiles[0].shape
    chans = w_ref.shape[2]
    strips = halos(parts, rows, cols, info_ref, near_h, across_h, near_w, across_w, slice(chans, chans + outs))
    for k in range(parts):
        above, below, before, after = strips(k)
        padded_ref[1 : rows + 1, k, 1 : cols + 1, :] = tiles[k][...].astype(F32)
        padded_ref[0, k, 1 : cols + 1, :] = above
        padded_ref[rows + 1, k, 1 : cols + 1, :] = below
        for at, (top, mid, bottom) in ((0, before), (cols + 1, after)):
            padded_ref[0, k, at : at + 1, :] = top
            padded_ref[1 : rows + 1, k, at, :] = mid
            padded_ref[rows + 1, k, at : at + 1, :] = bottom
    windows(padded_ref, windows_ref, parts, cols)
    taps = [(ky, kx) for ky in range(3) for kx in range(3)]
    shifted = jnp.concatenate([windows_ref[kx, ky : ky + rows].reshape(rows * parts * cols, outs) for ky, kx in taps], 1)
    weight = jnp.concatenate([w_ref[2 - ky, 2 - kx] for ky, kx in taps], 1)
    total = lax.dot_general(weight, shifted, (((1,), (1,)), ((), ())), preferred_element_type=F32)
    grad_ref[...] = total.T.reshape(rows, parts, cols, chans)


def terms_kernel(parts, count, info_ref, *refs):
    tiles = refs[:parts]
    stats_ref, gain_ref, shift_ref, grad_ref = refs[parts : parts + 4]
    moments_refs, (gx_own_ref, gx_other_ref, padded_ref, scales_ref) = refs[parts + 4 : -4], refs[-4:]
    rows, cols, _ = tiles[0].shape
    chans = grad_ref.shape[3]
    groups = stats_ref.shape[1] // (2 * parts)
    stats = jnp.concatenate([stats_ref[:, i * groups : (i + 1) * groups] for i in range(2 * parts)], 0)
    wide = expanded(jnp.concatenate([stats[:parts], lax.rsqrt(stats[parts:] / count + EPS)], 0), chans)
    means, invs = wide[:parts], wide[parts:]
    mine = lambda ref: shard_of([ref[s * chans : (s + 1) * chans].reshape(1, chans) for s in range(parts)], info_ref[ME])
    gain, shift = mine(gain_ref), mine(shift_ref)
    scales_ref[...] = jnp.concatenate([wide, gain, shift], 0)
    firsts, seconds = [], []
    for k in range(parts):
        mean, inv = means[k : k + 1], invs[k : k + 1]
        xhat = (tiles[k][...].astype(F32) - mean[None]) * inv[None]
        z = xhat * gain[None] + shift[None]
        sig = jax.nn.sigmoid(z)
        padded_ref[:, k, 1 : cols + 1, :] = z * sig
        gx = grad_ref[:, k] * sig * (1.0 + z * (1.0 - sig)) * gain[None]
        if k == 0:
            gx_own_ref[...] = gx
        else:
            gx_other_ref[k - 1] = gx.astype(BF16)
        firsts.append(jnp.sum(gx.reshape(rows * cols, chans), axis=0, keepdims=True))
        seconds.append(jnp.sum((gx * xhat).reshape(rows * cols, chans), axis=0, keepdims=True))
    sums = gathered(jnp.concatenate(firsts + seconds, 0), groups)
    for k, ref in enumerate(moments_refs):
        ref[...] = jnp.concatenate([v[k : k + 1] for v in (sums[:parts], sums[parts:], stats[:parts], stats[parts:])], 0)


def forward_kernel(parts, info_ref, given_ref, scales_ref, near_h, across_h, near_w, across_w, w_ref, conv_own_ref, conv_other_ref, windows_ref, padded_ref):
    rows, cols, outs = conv_own_ref.shape
    chans = windows_ref.shape[3]
    strips = halos(parts, rows, cols, info_ref, near_h, across_h, near_w, across_w, slice(0, chans))
    up, down, left, right = (info_ref[i] > 0 for i in (UP, DOWN, LEFT, RIGHT))
    scales = scales_ref[...]
    gain, shift = scales[2 * parts : 2 * parts + 1], scales[2 * parts + 1 : 2 * parts + 2]
    padded_ref[1 : rows + 1] = given_ref[...]
    for k in range(parts):
        mean, inv = scales[k : k + 1], scales[parts + k : parts + k + 1]

        def act_of(t, inside):
            z = (t - mean) * inv * gain + shift
            return jnp.where(inside, z * jax.nn.sigmoid(z), 0.0)

        above, below, before, after = strips(k)
        padded_ref[0, k, 1 : cols + 1, :] = act_of(above, up)
        padded_ref[rows + 1, k, 1 : cols + 1, :] = act_of(below, down)
        for at, (top, mid, bottom), side in ((0, before, left), (cols + 1, after, right)):
            padded_ref[0, k, at : at + 1, :] = act_of(top, side & up)
            padded_ref[1 : rows + 1, k, at, :] = act_of(mid, side)
            padded_ref[rows + 1, k, at : at + 1, :] = act_of(bottom, side & down)
    windows(padded_ref, windows_ref, parts, cols)
    convolved(parts, windows_ref, w_ref, slice(0, outs), conv_own_ref, conv_other_ref)


def second_forward_kernel(parts, start, windows_ref, w_ref, after_ref, conv_own_ref, conv_other_ref):
    convolved(parts, windows_ref, w_ref, slice(start, w_ref.shape[3]), conv_own_ref, conv_other_ref)


def convolved(parts, windows_ref, w_ref, lanes, conv_own_ref, conv_other_ref):
    rows, cols, outs = conv_own_ref.shape
    chans = windows_ref.shape[3]
    taps = [(ky, kx) for ky in range(3) for kx in range(3)]
    shifted = jnp.concatenate([windows_ref[kx, ky : ky + rows].reshape(rows * parts * cols, chans) for ky, kx in taps], 1)
    weight = w_ref[:, :, :, lanes].reshape(9 * chans, outs)
    total = lax.dot_general(weight, shifted, (((0,), (1,)), ((), ())), preferred_element_type=F32).T
    total = total.reshape(rows, parts, cols, outs)
    conv_own_ref[...] = total[:, 0]
    for k in range(1, parts):
        conv_other_ref[k - 1] = total[:, k].astype(BF16)


def finish_kernel(parts, count, info_ref, x_ref, small_ref, sums_ref, bias_ref, gx_own_ref, *refs):
    gx_refs, conv_refs = refs[: parts - 1], refs[parts - 1 : 3 * parts - 1]
    conv_ref, grad_ref = refs[3 * parts - 1 :]
    cin = x_ref.shape[2]
    chans = cin // parts
    start = 0
    for i in range(2):
        conv = sum(r[...].astype(F32) for r in conv_refs[i::2])
        stop = start + conv.shape[2]
        conv_ref[:, :, start:stop] = (conv + bias_ref[start:stop].reshape(1, 1, -1)).astype(BF16)
        start = stop
    wide = []
    for k in range(parts):
        stats = small_ref[k]
        wide.append(jnp.concatenate([stats[2:3], lax.rsqrt(stats[3:4] / count + EPS), sums_ref[k] / count], 0))
    wide = expanded(jnp.concatenate(wide, 0), chans)
    gx_all = [ref[...].astype(F32) for ref in (gx_own_ref, *gx_refs)]
    for s in range(parts):
        at = slice(s * chans, (s + 1) * chans)
        k = lax.rem(s - info_ref[ME] + parts, parts)
        mean, inv, first, second = (shard_of([wide[4 * j + i : 4 * j + i + 1] for j in range(parts)], k)[None] for i in range(4))
        xhat = (x_ref[:, :, at].astype(F32) - mean) * inv
        grad_ref[:, :, at] = (inv * (shard_of(gx_all, k) - first - xhat * second)).astype(BF16)


def call(kernel, name, outs, operands, scratch=(), scalars=True, cost=None):
    spec = lambda i: pl.BlockSpec(memory_space=pltpu.SMEM if scalars and i == 0 else pltpu.VMEM)
    return pl.pallas_call(
        kernel,
        out_shape=outs,
        in_specs=[spec(i) for i in range(len(operands))],
        out_specs=[pl.BlockSpec(memory_space=pltpu.VMEM)] * len(outs),
        scratch_shapes=scratch,
        compiler_params=pltpu.CompilerParams(vmem_limit_bytes=28 * 2**20),
        cost_estimate=cost,
        name=name,
    )(*operands)


def tied(value, *others):
    for other in others:
        value = value + 0.0 * other[0, :1, : value.shape[-1]].astype(F32)
    return value


def stats_rounds(axis):
    count = lax.axis_size(axis)
    if count == 4:
        return [near, lambda i: i ^ 2]
    return [functools.partial(lambda step, i: i ^ step, 2**j) for j in range(count.bit_length() - 1)]


def body(latents, norm_gain, norm_shift, conv_weight, conv_bias, cotangent):
    _, rows, cols, cin = latents.shape
    outs = cotangent.shape[3]
    chans = conv_weight.shape[2]
    parts = lax.axis_size("dp")
    me = lax.axis_index("dp")
    groups = GROUPS * chans // cin
    both = chans + outs
    n = rows * cols * (cin // GROUPS)
    count = float(n * lax.axis_size("ha") * lax.axis_size("wa"))
    x, cot = latents[0], cotangent[0]
    sds = jax.ShapeDtypeStruct
    where = [lax.axis_index(a) for a in ("ha", "wa")]
    last = [lax.axis_size(a) - 1 for a in ("ha", "wa")]
    info = jnp.stack(
        [me, where[0] % 2 == 0, where[1] % 2 == 0, where[0] > 0, where[0] < last[0], where[1] > 0, where[1] < last[1]]
    ).astype(jnp.int32)

    peers = [[(i, (i + k) % parts) for i in range(parts)] for k in range(1, parts)]
    from_peers = lambda values: [lax.ppermute(v, "dp", pairs) for v, pairs in zip(values, peers)]
    cot_tiles = [cot, *from_peers([cot] * (parts - 1))]
    first = call(
        functools.partial(first_kernel, parts, groups),
        "first",
        [sds((2 * (rows + cols) + 8, chans), BF16)] * parts,
        [info, x],
        cost=pl.CostEstimate(flops=10**10, bytes_accessed=1, transcendentals=0),
    )
    got = from_peers(first[1:])
    tiles = call(
        functools.partial(tiles_kernel, parts),
        "tiles",
        [sds((rows, cols, chans), BF16)] * parts,
        [info, x, conv_weight],
    )
    zero = (0.0 * got[0][:1]).astype(BF16)
    x_tiles = [tiles[0], *from_peers([v + zero[None] for v in tiles[1:]])]
    size = 2 * parts * groups
    pack_near, pack_across, stats = call(
        functools.partial(rows_kernel, parts),
        "rows",
        [sds((parts * cols + 8, both), BF16), sds((parts * cols, both), BF16), sds((1, size), F32)],
        [info, first[0], *got, *cot_tiles],
    )

    def reduced(stats, n, axis, pairings):
        for partner in pairings:
            stats, n = merged(stats, exchange(stats, axis, partner), n), 2 * n
        return stats, n

    rounds_h, rounds_w = stats_rounds("ha"), stats_rounds("wa")
    near_h = exchange(pack_near, "ha", near)
    ends_w = call(
        functools.partial(columns_kernel, parts),
        "columns",
        [sds((2 * rows, both), BF16)] * parts,
        [info, first[0], *got, *cot_tiles, stats],
    )
    stats, n = merged(stats, unpacked(near_h, parts * cols, size), n), 2 * n
    if lax.axis_size("ha") == 4:
        across_h = exchange(packed([pack_across], stats), "ha", across)
        stats, n = merged(stats, unpacked(across_h, parts * cols, size), n), 2 * n
    else:
        across_h = exchange(pack_across, "ha", across)
        stats, n = reduced(stats, n, "ha", rounds_h[1:])
    used = parts * (rows + 2)
    near_w, across_w = call(
        functools.partial(pack_kernel, parts, rows, cols),
        "pack",
        [sds((-(-(used + 3) // 8) * 8, both), BF16), sds((used, both), BF16)],
        [info, near_h, across_h, stats, *ends_w],
    )
    near_w = exchange(near_w, "wa", near)
    across_w = exchange(across_w, "wa", across, ends=False)
    stats, n = merged(stats, unpacked(near_w, used, size), n), 2 * n
    stats, n = reduced(stats, n, "wa", rounds_w[1:])

    strips = [near_h, across_h, near_w, across_w]
    padded = lambda depth: pltpu.VMEM((rows + 2, parts, cols + 8, depth), F32)
    shifted = (3, rows + 2, parts * cols)
    (grad_act,) = call(
        functools.partial(backward_kernel, parts),
        "conv_backward",
        [sds((rows, parts, cols, chans), F32)],
        [info, *cot_tiles, *strips, conv_weight, *x_tiles[1:]],
        [padded(outs), pltpu.VMEM((*shifted, outs), BF16)],
    )
    *small, gx_own, gx_other, act, scales = call(
        functools.partial(terms_kernel, parts, count),
        "terms",
        [
            *[sds((4, groups), F32)] * parts,
            sds((rows, cols, chans), F32),
            sds((parts - 1, rows, cols, chans), BF16),
            sds((rows, parts, cols + 8, chans), F32),
            sds((2 * parts + 2, chans), F32),
        ],
        [info, *x_tiles, stats, norm_gain, norm_shift, grad_act],
    )

    to_owners = lambda values: [lax.ppermute(v, "dp", [(j, i) for i, j in pairs]) for v, pairs in zip(values, peers)]
    small = jnp.stack([small[0], *to_owners(small[1:])], 0)
    gx = to_owners([gx_other[k] for k in range(parts - 1)])
    start = outs * 3 // 5 // 128 * 128
    parts_of = lambda size: [sds((rows, cols, size), F32), sds((parts - 1, rows, cols, size), BF16)]
    conv_own, conv_other, act_windows = call(
        functools.partial(forward_kernel, parts),
        "conv_forward",
        [*parts_of(start), sds((*shifted, chans), BF16)],
        [info, act, scales, *strips, conv_weight],
        [padded(chans)],
    )
    sums = tied(small[:, :2], conv_own)
    sums = sums + exchange(sums, "ha", rounds_h[0])
    conv_own2, conv_other2 = call(
        functools.partial(second_forward_kernel, parts, start),
        "conv_forward2",
        parts_of(outs - start),
        [act_windows, conv_weight, sums],
        scalars=False,
    )
    conv = [conv_own, conv_own2]
    for k in range(parts - 1):
        back = [(j, i) for i, j in peers[k]]
        conv += [lax.ppermute(v[k], "dp", back) for v in (conv_other, conv_other2)]
    for partner in rounds_h[1:]:
        sums = sums + exchange(sums, "ha", partner)
    sums = tied(sums, conv_own2)
    for partner in rounds_w:
        sums = sums + exchange(sums, "wa", partner)
    conv_out, grad = call(
        functools.partial(finish_kernel, parts, count),
        "finish",
        [sds((rows, cols, outs), BF16), sds((rows, cols, cin), BF16)],
        [info, x, small, sums, conv_bias, gx_own, *gx, *conv],
    )
    return conv_out[None], grad[None]


def solution(mesh):
    tile = P("dp", "ha", "wa", None)
    return jax.shard_map(
        body,
        mesh=mesh,
        in_specs=(tile, P(), P(), P(None, None, "dp", None), P(), tile),
        out_specs=(tile, tile),
        check_vma=False,
    )
```

```python
import functools

import jax
import jax.numpy as jnp
from jax import lax
from jax.experimental import pallas as pl
from jax.experimental.pallas import tpu as pltpu
from jax.sharding import PartitionSpec as P

GROUPS = 32
EPS = 1e-05
F32 = jnp.float32
BF16 = jnp.bfloat16

ME, EVEN_H, EVEN_W, UP, DOWN, LEFT, RIGHT = range(7)


def exchange(value, axis, partner, ends=True):
    count = lax.axis_size(axis)
    pairs = [(i, partner(i) % count) for i in range(count)]
    if not ends:
        pairs = [(i, j) for i, j in pairs if abs(i - j) == 1]
    return lax.ppermute(value, axis, pairs)


def near(i):
    return i ^ 1


def across(i):
    return i - 1 if i % 2 == 0 else i + 1


def merged(stats, other, n):
    half = stats.shape[1] // 2
    delta = other[:, :half] - stats[:, :half]
    return jnp.concatenate([stats[:, :half] + 0.5 * delta, stats[:, half:] + other[:, half:] + (0.5 * n) * delta * delta], 1)


def packed(strips, stats):
    high = lax.reduce_precision(stats, 8, 7)
    middle = lax.reduce_precision(stats - high, 8, 7)
    low = lax.reduce_precision(stats - high - middle, 8, 7)
    rows = jnp.concatenate([high, middle, low], 0).astype(BF16)
    rows = jnp.pad(rows, ((0, 0), (0, strips[0].shape[1] - rows.shape[1])))
    return jnp.concatenate([*strips, rows], 0)


def unpacked(pack, r, size):
    rows = pack[r : r + 3, :size].astype(F32)
    return rows[:1] + rows[1:2] + rows[2:]


def members(groups, chans, dim):
    per_group = chans // groups
    shape = (groups, chans) if dim else (chans, groups)
    chan = lax.broadcasted_iota(jnp.int32, shape, dim)
    group = lax.broadcasted_iota(jnp.int32, shape, 1 - dim)
    return ((chan >= group * per_group) & (chan < (group + 1) * per_group)).astype(F32)


def three_parts(a):
    high = a.astype(BF16)
    rest = a - high.astype(F32)
    middle = rest.astype(BF16)
    return high, middle, (rest - middle.astype(F32)).astype(BF16)


def exact_dot(a, b):
    rows = a.shape[0]
    parts = jnp.concatenate([p.astype(F32) for p in three_parts(a)], 0).astype(BF16)
    sums = jnp.dot(parts, b.astype(BF16), preferred_element_type=F32)
    return sums[:rows] + sums[rows : 2 * rows] + sums[2 * rows :]


def expanded(values, chans):
    return exact_dot(values, members(values.shape[-1], chans, 1))


def gathered(values, groups):
    return exact_dot(values, members(groups, values.shape[-1], 0))


def shard_of(pieces, shard):
    value = pieces[0]
    for i in range(1, len(pieces)):
        value = jnp.where(shard == i, pieces[i], value)
    return value


def first_kernel(parts, groups, info_ref, x_ref, *out_refs):
    rows, cols, cin = x_ref.shape
    chans = cin // parts
    n = rows * cols * (chans // groups)
    me = info_ref[ME]
    even_h = info_ref[EVEN_H] > 0
    shards = [x_ref[:, :, s * chans : (s + 1) * chans].astype(F32) for s in range(parts)]
    stats = []
    for x in shards:
        flat = x.reshape(rows * cols, chans)
        mean = gathered(jnp.sum(flat, axis=0, keepdims=True), groups) / n
        centered = flat - expanded(mean, chans)
        squares = gathered(jnp.sum(centered * centered, axis=0, keepdims=True), groups)
        stats.append(jnp.concatenate([p.astype(F32) for p in three_parts(jnp.concatenate([mean, squares], 1))], 0))
    pieces = []
    for x, terms in zip(shards, stats):
        terms = jnp.concatenate([terms, jnp.zeros((3, chans - 2 * groups), F32)], 1)
        pieces.append(jnp.concatenate([*row_ends(x, even_h), terms, jnp.zeros((5, chans), F32), column_ends(x, info_ref[EVEN_W] > 0)], 0))
    for k, ref in enumerate(out_refs):
        ref[...] = shard_of(pieces, lax.rem(me + k, parts)).astype(BF16)


def row_ends(t, even_h):
    first, last = t[0], t[t.shape[0] - 1]
    return jnp.where(even_h, last, first), jnp.where(even_h, first, last)


def column_ends(t, even_w):
    first, last = t[:, 0, :], t[:, t.shape[1] - 1, :]
    return jnp.concatenate([jnp.where(even_w, last, first), jnp.where(even_w, first, last)], 0)


def tiles_kernel(parts, info_ref, x_ref, w_ref, *out_refs):
    chans = x_ref.shape[2] // parts
    for k in range(parts):
        shard = lax.rem(info_ref[ME] + k, parts)
        out_refs[k][...] = shard_of([x_ref[:, :, s * chans : (s + 1) * chans].astype(F32) for s in range(parts)], shard).astype(BF16)


def rows_kernel(parts, info_ref, *refs):
    packs, cots, (near_ref, across_ref, stats_ref) = refs[:parts], refs[parts : 2 * parts], refs[2 * parts :]
    rows, cols, outs = cots[0].shape
    chans = packs[0].shape[1]
    groups = stats_ref.shape[1] // (2 * parts)
    even_h = info_ref[EVEN_H] > 0
    packs = [ref[...].astype(F32) for ref in packs]
    cot_ends = [row_ends(ref[...].astype(F32), even_h) for ref in cots]
    local = [v[2 * cols : 2 * cols + 3, : 2 * groups] for v in packs]
    terms = jnp.concatenate([v[:, :groups] for v in local] + [v[:, groups:] for v in local], 1)
    stats_ref[...] = terms[0:1] + terms[1:2] + terms[2:3]
    tail = jnp.concatenate([terms, jnp.zeros((3, chans + outs - terms.shape[1]), F32)], 1)
    for half, ref in enumerate((near_ref, across_ref)):
        strips = [jnp.concatenate([v[half * cols : (half + 1) * cols], c[half]], 1) for v, c in zip(packs, cot_ends)]
        ref[...] = jnp.concatenate(strips + ([tail, jnp.zeros((5, chans + outs), F32)] if half == 0 else []), 0).astype(BF16)


def columns_kernel(parts, info_ref, *refs):
    even_w = info_ref[EVEN_W] > 0
    for pack_ref, cot_ref, ref in zip(refs[:parts], refs[parts : 2 * parts], refs[2 * parts + 1 :]):
        rows, cols, _ = cot_ref.shape
        chans = pack_ref.shape[1]
        ref[:, :chans] = pack_ref[...].astype(F32)[2 * cols + 8 :].astype(BF16)
        ref[:, chans:] = column_ends(cot_ref[...].astype(F32), even_w).astype(BF16)


def pack_kernel(parts, rows, cols, info_ref, near_h, across_h, stats_ref, *refs):
    ends, (near_ref, across_ref) = refs[:parts], refs[parts:]
    even_w = info_ref[EVEN_W] > 0
    both = near_ref.shape[1]
    near_rows = near_h[...].astype(F32)
    across_rows = jnp.where((info_ref[UP] > 0) & (info_ref[DOWN] > 0), across_h[...].astype(F32), 0.0)
    stats = jnp.concatenate([p.astype(F32) for p in three_parts(stats_ref[...])], 0)
    stats = jnp.concatenate([stats, jnp.zeros((3, both - stats.shape[1]), F32)], 1)
    for half, ref, pick_last in ((0, near_ref, even_w), (1, across_ref, jnp.logical_not(even_w))):
        corners = []
        for t in (near_rows, across_rows):
            for k in range(parts):
                first, last = t[k * cols : k * cols + 1], t[(k + 1) * cols - 1 : (k + 1) * cols]
                corners.append(jnp.where(pick_last, last, first))
        for k in range(parts):
            ref[k * rows : (k + 1) * rows, :] = ends[k][half * rows : (half + 1) * rows, :]
        pieces = corners + ([stats] if half == 0 else [])
        used = parts * (rows + 2) + (3 if half == 0 else 0)
        if ref.shape[0] > used:
            pieces.append(jnp.zeros((ref.shape[0] - used, both), F32))
        ref[parts * rows :, :] = jnp.concatenate(pieces, 0).astype(BF16)


def halos(parts, rows, cols, info_ref, near_h, across_h, near_w, across_w, lanes):
    even_h = info_ref[EVEN_H] > 0
    even_w = info_ref[EVEN_W] > 0
    part = lambda ref, r: ref[:, lanes].astype(F32)[:r]
    a, b = (part(ref, parts * cols) for ref in (near_h, across_h))
    b = jnp.where((info_ref[UP] > 0) & (info_ref[DOWN] > 0), b, 0.0)
    above_all, below_all = jnp.where(even_h, b, a), jnp.where(even_h, a, b)
    c, d = (part(ref, parts * (rows + 2)) for ref in (near_w, across_w))
    before_all, after_all = jnp.where(even_w, d, c), jnp.where(even_w, c, d)

    def strips(k):
        def ordered(t):
            head, tail = t[parts * rows + k :][:1], t[parts * (rows + 1) + k :][:1]
            return jnp.where(even_h, tail, head), t[k * rows : (k + 1) * rows], jnp.where(even_h, head, tail)

        at = slice(k * cols, (k + 1) * cols)
        return above_all[at], below_all[at], ordered(before_all), ordered(after_all)

    return strips


def windows(padded_ref, windows_ref, k_all, cols):
    for kx in range(3):
        view = padded_ref[:, :, kx : kx + cols, :]
        windows_ref[kx] = view.reshape(view.shape[0], k_all * cols, view.shape[3]).astype(BF16)


def backward_kernel(parts, info_ref, *refs):
    tiles, (near_h, across_h, near_w, across_w, w_ref, *_, grad_ref, padded_ref, windows_ref) = refs[:parts], refs[parts:]
    rows, cols, outs = tiles[0].shape
    chans = w_ref.shape[2]
    strips = halos(parts, rows, cols, info_ref, near_h, across_h, near_w, across_w, slice(chans, chans + outs))
    for k in range(parts):
        above, below, before, after = strips(k)
        padded_ref[1 : rows + 1, k, 1 : cols + 1, :] = tiles[k][...].astype(F32)
        padded_ref[0, k, 1 : cols + 1, :] = above
        padded_ref[rows + 1, k, 1 : cols + 1, :] = below
        for at, (top, mid, bottom) in ((0, before), (cols + 1, after)):
            padded_ref[0, k, at : at + 1, :] = top
            padded_ref[1 : rows + 1, k, at, :] = mid
            padded_ref[rows + 1, k, at : at + 1, :] = bottom
    windows(padded_ref, windows_ref, parts, cols)
    taps = [(ky, kx) for ky in range(3) for kx in range(3)]
    shifted = jnp.concatenate([windows_ref[kx, ky : ky + rows].reshape(rows * parts * cols, outs) for ky, kx in taps], 1)
    weight = jnp.concatenate([w_ref[2 - ky, 2 - kx] for ky, kx in taps], 1)
    total = lax.dot_general(weight, shifted, (((1,), (1,)), ((), ())), preferred_element_type=F32)
    grad_ref[...] = total.T.reshape(rows, parts, cols, chans)


def terms_kernel(parts, count, info_ref, *refs):
    tiles = refs[:parts]
    stats_ref, gain_ref, shift_ref, grad_ref = refs[parts : parts + 4]
    moments_refs, (gx_own_ref, gx_other_ref, padded_ref, scales_ref) = refs[parts + 4 : -4], refs[-4:]
    rows, cols, _ = tiles[0].shape
    chans = grad_ref.shape[3]
    groups = stats_ref.shape[1] // (2 * parts)
    stats = jnp.concatenate([stats_ref[:, i * groups : (i + 1) * groups] for i in range(2 * parts)], 0)
    wide = expanded(jnp.concatenate([stats[:parts], lax.rsqrt(stats[parts:] / count + EPS)], 0), chans)
    means, invs = wide[:parts], wide[parts:]
    mine = lambda ref: shard_of([ref[s * chans : (s + 1) * chans].reshape(1, chans) for s in range(parts)], info_ref[ME])
    gain, shift = mine(gain_ref), mine(shift_ref)
    scales_ref[...] = jnp.concatenate([wide, gain, shift], 0)
    firsts, seconds = [], []
    for k in range(parts):
        mean, inv = means[k : k + 1], invs[k : k + 1]
        xhat = (tiles[k][...].astype(F32) - mean[None]) * inv[None]
        z = xhat * gain[None] + shift[None]
        sig = jax.nn.sigmoid(z)
        padded_ref[:, k, 1 : cols + 1, :] = z * sig
        gx = grad_ref[:, k] * sig * (1.0 + z * (1.0 - sig)) * gain[None]
        if k == 0:
            gx_own_ref[...] = gx
        else:
            gx_other_ref[k - 1] = gx.astype(BF16)
        firsts.append(jnp.sum(gx.reshape(rows * cols, chans), axis=0, keepdims=True))
        seconds.append(jnp.sum((gx * xhat).reshape(rows * cols, chans), axis=0, keepdims=True))
    sums = gathered(jnp.concatenate(firsts + seconds, 0), groups)
    for k, ref in enumerate(moments_refs):
        ref[...] = jnp.concatenate([v[k : k + 1] for v in (sums[:parts], sums[parts:], stats[:parts], stats[parts:])], 0)


def forward_kernel(parts, info_ref, given_ref, scales_ref, near_h, across_h, near_w, across_w, w_ref, conv_own_ref, conv_other_ref, windows_ref, padded_ref):
    rows, cols, outs = conv_own_ref.shape
    chans = windows_ref.shape[3]
    strips = halos(parts, rows, cols, info_ref, near_h, across_h, near_w, across_w, slice(0, chans))
    up, down, left, right = (info_ref[i] > 0 for i in (UP, DOWN, LEFT, RIGHT))
    scales = scales_ref[...]
    gain, shift = scales[2 * parts : 2 * parts + 1], scales[2 * parts + 1 : 2 * parts + 2]
    padded_ref[1 : rows + 1] = given_ref[...]
    for k in range(parts):
        mean, inv = scales[k : k + 1], scales[parts + k : parts + k + 1]

        def act_of(t, inside):
            z = (t - mean) * inv * gain + shift
            return jnp.where(inside, z * jax.nn.sigmoid(z), 0.0)

        above, below, before, after = strips(k)
        padded_ref[0, k, 1 : cols + 1, :] = act_of(above, up)
        padded_ref[rows + 1, k, 1 : cols + 1, :] = act_of(below, down)
        for at, (top, mid, bottom), side in ((0, before, left), (cols + 1, after, right)):
            padded_ref[0, k, at : at + 1, :] = act_of(top, side & up)
            padded_ref[1 : rows + 1, k, at, :] = act_of(mid, side)
            padded_ref[rows + 1, k, at : at + 1, :] = act_of(bottom, side & down)
    windows(padded_ref, windows_ref, parts, cols)
    convolved(parts, windows_ref, w_ref, slice(0, outs), conv_own_ref, conv_other_ref)


def second_forward_kernel(parts, start, windows_ref, w_ref, after_ref, conv_own_ref, conv_other_ref):
    convolved(parts, windows_ref, w_ref, slice(start, w_ref.shape[3]), conv_own_ref, conv_other_ref)


def convolved(parts, windows_ref, w_ref, lanes, conv_own_ref, conv_other_ref):
    rows, cols, outs = conv_own_ref.shape
    chans = windows_ref.shape[3]
    taps = [(ky, kx) for ky in range(3) for kx in range(3)]
    shifted = jnp.concatenate([windows_ref[kx, ky : ky + rows].reshape(rows * parts * cols, chans) for ky, kx in taps], 1)
    weight = w_ref[:, :, :, lanes].reshape(9 * chans, outs)
    total = lax.dot_general(weight, shifted, (((0,), (1,)), ((), ())), preferred_element_type=F32).T
    total = total.reshape(rows, parts, cols, outs)
    conv_own_ref[...] = total[:, 0]
    for k in range(1, parts):
        conv_other_ref[k - 1] = total[:, k].astype(BF16)


def finish_kernel(parts, count, info_ref, x_ref, small_ref, sums_ref, bias_ref, gx_own_ref, *refs):
    gx_refs, conv_refs = refs[: parts - 1], refs[parts - 1 : 3 * parts - 1]
    conv_ref, grad_ref = refs[3 * parts - 1 :]
    cin = x_ref.shape[2]
    chans = cin // parts
    start = 0
    for i in range(2):
        conv = sum(r[...].astype(F32) for r in conv_refs[i::2])
        stop = start + conv.shape[2]
        conv_ref[:, :, start:stop] = (conv + bias_ref[start:stop].reshape(1, 1, -1)).astype(BF16)
        start = stop
    wide = []
    for k in range(parts):
        stats = small_ref[k]
        wide.append(jnp.concatenate([stats[2:3], lax.rsqrt(stats[3:4] / count + EPS), sums_ref[k] / count], 0))
    wide = expanded(jnp.concatenate(wide, 0), chans)
    gx_all = [ref[...].astype(F32) for ref in (gx_own_ref, *gx_refs)]
    for s in range(parts):
        at = slice(s * chans, (s + 1) * chans)
        k = lax.rem(s - info_ref[ME] + parts, parts)
        mean, inv, first, second = (shard_of([wide[4 * j + i : 4 * j + i + 1] for j in range(parts)], k)[None] for i in range(4))
        xhat = (x_ref[:, :, at].astype(F32) - mean) * inv
        grad_ref[:, :, at] = (inv * (shard_of(gx_all, k) - first - xhat * second)).astype(BF16)


def call(kernel, name, outs, operands, scratch=(), scalars=True, cost=None):
    spec = lambda i: pl.BlockSpec(memory_space=pltpu.SMEM if scalars and i == 0 else pltpu.VMEM)
    return pl.pallas_call(
        kernel,
        out_shape=outs,
        in_specs=[spec(i) for i in range(len(operands))],
        out_specs=[pl.BlockSpec(memory_space=pltpu.VMEM)] * len(outs),
        scratch_shapes=scratch,
        compiler_params=pltpu.CompilerParams(vmem_limit_bytes=28 * 2**20),
        cost_estimate=cost,
        name=name,
    )(*operands)


def tied(value, *others):
    for other in others:
        value = value + 0.0 * other[0, :1, : value.shape[-1]].astype(F32)
    return value


def stats_rounds(axis):
    count = lax.axis_size(axis)
    if count == 4:
        return [near, lambda i: i ^ 2]
    return [functools.partial(lambda step, i: i ^ step, 2**j) for j in range(count.bit_length() - 1)]


def body(latents, norm_gain, norm_shift, conv_weight, conv_bias, cotangent):
    _, rows, cols, cin = latents.shape
    outs = cotangent.shape[3]
    chans = conv_weight.shape[2]
    parts = lax.axis_size("dp")
    me = lax.axis_index("dp")
    groups = GROUPS * chans // cin
    both = chans + outs
    n = rows * cols * (cin // GROUPS)
    count = float(n * lax.axis_size("ha") * lax.axis_size("wa"))
    x, cot = latents[0], cotangent[0]
    sds = jax.ShapeDtypeStruct
    where = [lax.axis_index(a) for a in ("ha", "wa")]
    last = [lax.axis_size(a) - 1 for a in ("ha", "wa")]
    info = jnp.stack(
        [me, where[0] % 2 == 0, where[1] % 2 == 0, where[0] > 0, where[0] < last[0], where[1] > 0, where[1] < last[1]]
    ).astype(jnp.int32)

    peers = [[(i, (i + k) % parts) for i in range(parts)] for k in range(1, parts)]
    from_peers = lambda values: [lax.ppermute(v, "dp", pairs) for v, pairs in zip(values, peers)]
    cot_tiles = [cot, *from_peers([cot] * (parts - 1))]
    first = call(
        functools.partial(first_kernel, parts, groups),
        "first",
        [sds((2 * (rows + cols) + 8, chans), BF16)] * parts,
        [info, x],
        cost=pl.CostEstimate(flops=10**10, bytes_accessed=1, transcendentals=0),
    )
    got = from_peers(first[1:])
    tiles = call(
        functools.partial(tiles_kernel, parts),
        "tiles",
        [sds((rows, cols, chans), BF16)] * parts,
        [info, x, conv_weight],
    )
    zero = (0.0 * got[0][:1]).astype(BF16)
    x_tiles = [tiles[0], *from_peers([v + zero[None] for v in tiles[1:]])]
    size = 2 * parts * groups
    pack_near, pack_across, stats = call(
        functools.partial(rows_kernel, parts),
        "rows",
        [sds((parts * cols + 8, both), BF16), sds((parts * cols, both), BF16), sds((1, size), F32)],
        [info, first[0], *got, *cot_tiles],
    )

    def reduced(stats, n, axis, pairings):
        for partner in pairings:
            stats, n = merged(stats, exchange(stats, axis, partner), n), 2 * n
        return stats, n

    rounds_h, rounds_w = stats_rounds("ha"), stats_rounds("wa")
    near_h = exchange(pack_near, "ha", near)
    ends_w = call(
        functools.partial(columns_kernel, parts),
        "columns",
        [sds((2 * rows, both), BF16)] * parts,
        [info, first[0], *got, *cot_tiles, stats],
    )
    stats, n = merged(stats, unpacked(near_h, parts * cols, size), n), 2 * n
    if lax.axis_size("ha") == 4:
        across_h = exchange(packed([pack_across], stats), "ha", across)
        stats, n = merged(stats, unpacked(across_h, parts * cols, size), n), 2 * n
    else:
        across_h = exchange(pack_across, "ha", across)
        stats, n = reduced(stats, n, "ha", rounds_h[1:])
    used = parts * (rows + 2)
    near_w, across_w = call(
        functools.partial(pack_kernel, parts, rows, cols),
        "pack",
        [sds((-(-(used + 3) // 8) * 8, both), BF16), sds((used, both), BF16)],
        [info, near_h, across_h, stats, *ends_w],
    )
    near_w = exchange(near_w, "wa", near)
    across_w = exchange(across_w, "wa", across, ends=False)
    stats, n = merged(stats, unpacked(near_w, used, size), n), 2 * n
    stats, n = reduced(stats, n, "wa", rounds_w[1:])

    strips = [near_h, across_h, near_w, across_w]
    padded = lambda depth: pltpu.VMEM((rows + 2, parts, cols + 8, depth), F32)
    shifted = (3, rows + 2, parts * cols)
    (grad_act,) = call(
        functools.partial(backward_kernel, parts),
        "conv_backward",
        [sds((rows, parts, cols, chans), F32)],
        [info, *cot_tiles, *strips, conv_weight, *x_tiles[1:]],
        [padded(outs), pltpu.VMEM((*shifted, outs), BF16)],
    )
    *small, gx_own, gx_other, act, scales = call(
        functools.partial(terms_kernel, parts, count),
        "terms",
        [
            *[sds((4, groups), F32)] * parts,
            sds((rows, cols, chans), F32),
            sds((parts - 1, rows, cols, chans), BF16),
            sds((rows, parts, cols + 8, chans), F32),
            sds((2 * parts + 2, chans), F32),
        ],
        [info, *x_tiles, stats, norm_gain, norm_shift, grad_act],
    )

    to_owners = lambda values: [lax.ppermute(v, "dp", [(j, i) for i, j in pairs]) for v, pairs in zip(values, peers)]
    small = jnp.stack([small[0], *to_owners(small[1:])], 0)
    gx = to_owners([gx_other[k] for k in range(parts - 1)])
    start = outs * 2 // 5 // 128 * 128
    parts_of = lambda size: [sds((rows, cols, size), F32), sds((parts - 1, rows, cols, size), BF16)]
    conv_own, conv_other, act_windows = call(
        functools.partial(forward_kernel, parts),
        "conv_forward",
        [*parts_of(start), sds((*shifted, chans), BF16)],
        [info, act, scales, *strips, conv_weight],
        [padded(chans)],
    )
    sums = tied(small[:, :2], conv_own)
    sums = sums + exchange(sums, "ha", rounds_h[0])
    conv_own2, conv_other2 = call(
        functools.partial(second_forward_kernel, parts, start),
        "conv_forward2",
        parts_of(outs - start),
        [act_windows, conv_weight, sums],
        scalars=False,
    )
    conv = [conv_own, conv_own2]
    for k in range(parts - 1):
        back = [(j, i) for i, j in peers[k]]
        conv += [lax.ppermute(v[k], "dp", back) for v in (conv_other, conv_other2)]
    for partner in rounds_h[1:]:
        sums = sums + exchange(sums, "ha", partner)
    sums = tied(sums, conv_own2)
    for partner in rounds_w:
        sums = sums + exchange(sums, "wa", partner)
    conv_out, grad = call(
        functools.partial(finish_kernel, parts, count),
        "finish",
        [sds((rows, cols, outs), BF16), sds((rows, cols, cin), BF16)],
        [info, x, small, sums, conv_bias, gx_own, *gx, *conv],
    )
    return conv_out[None], grad[None]


def solution(mesh):
    tile = P("dp", "ha", "wa", None)
    return jax.shard_map(
        body,
        mesh=mesh,
        in_specs=(tile, P(), P(), P(None, None, "dp", None), P(), tile),
        out_specs=(tile, tile),
        check_vma=False,
    )
```

```python
import functools

import jax
import jax.numpy as jnp
from jax import lax
from jax.experimental import pallas as pl
from jax.experimental.pallas import tpu as pltpu
from jax.sharding import PartitionSpec as P

GROUPS = 32
EPS = 1e-05
F32 = jnp.float32
BF16 = jnp.bfloat16

ME, EVEN_H, EVEN_W, UP, DOWN, LEFT, RIGHT = range(7)


def exchange(value, axis, partner, ends=True):
    count = lax.axis_size(axis)
    pairs = [(i, partner(i) % count) for i in range(count)]
    if not ends:
        pairs = [(i, j) for i, j in pairs if abs(i - j) == 1]
    return lax.ppermute(value, axis, pairs)


def near(i):
    return i ^ 1


def across(i):
    return i - 1 if i % 2 == 0 else i + 1


def merged(stats, other, n):
    half = stats.shape[1] // 2
    delta = other[:, :half] - stats[:, :half]
    return jnp.concatenate([stats[:, :half] + 0.5 * delta, stats[:, half:] + other[:, half:] + (0.5 * n) * delta * delta], 1)


def packed(strips, stats):
    high = lax.reduce_precision(stats, 8, 7)
    middle = lax.reduce_precision(stats - high, 8, 7)
    low = lax.reduce_precision(stats - high - middle, 8, 7)
    rows = jnp.concatenate([high, middle, low], 0).astype(BF16)
    rows = jnp.pad(rows, ((0, 0), (0, strips[0].shape[1] - rows.shape[1])))
    return jnp.concatenate([*strips, rows], 0)


def unpacked(pack, r, size):
    rows = pack[r : r + 3, :size].astype(F32)
    return rows[:1] + rows[1:2] + rows[2:]


def members(groups, chans, dim):
    per_group = chans // groups
    shape = (groups, chans) if dim else (chans, groups)
    chan = lax.broadcasted_iota(jnp.int32, shape, dim)
    group = lax.broadcasted_iota(jnp.int32, shape, 1 - dim)
    return ((chan >= group * per_group) & (chan < (group + 1) * per_group)).astype(F32)


def three_parts(a):
    high = a.astype(BF16)
    rest = a - high.astype(F32)
    middle = rest.astype(BF16)
    return high, middle, (rest - middle.astype(F32)).astype(BF16)


def exact_dot(a, b):
    rows = a.shape[0]
    parts = jnp.concatenate([p.astype(F32) for p in three_parts(a)], 0).astype(BF16)
    sums = jnp.dot(parts, b.astype(BF16), preferred_element_type=F32)
    return sums[:rows] + sums[rows : 2 * rows] + sums[2 * rows :]


def expanded(values, chans):
    return exact_dot(values, members(values.shape[-1], chans, 1))


def gathered(values, groups):
    return exact_dot(values, members(groups, values.shape[-1], 0))


def shard_of(pieces, shard):
    value = pieces[0]
    for i in range(1, len(pieces)):
        value = jnp.where(shard == i, pieces[i], value)
    return value


def first_kernel(parts, groups, info_ref, x_ref, *out_refs):
    rows, cols, cin = x_ref.shape
    chans = cin // parts
    n = rows * cols * (chans // groups)
    me = info_ref[ME]
    even_h = info_ref[EVEN_H] > 0
    shards = [x_ref[:, :, s * chans : (s + 1) * chans].astype(F32) for s in range(parts)]
    stats = []
    for x in shards:
        flat = x.reshape(rows * cols, chans)
        mean = gathered(jnp.sum(flat, axis=0, keepdims=True), groups) / n
        centered = flat - expanded(mean, chans)
        squares = gathered(jnp.sum(centered * centered, axis=0, keepdims=True), groups)
        stats.append(jnp.concatenate([p.astype(F32) for p in three_parts(jnp.concatenate([mean, squares], 1))], 0))
    pieces = []
    for x, terms in zip(shards, stats):
        terms = jnp.concatenate([terms, jnp.zeros((3, chans - 2 * groups), F32)], 1)
        pieces.append(jnp.concatenate([*row_ends(x, even_h), terms, jnp.zeros((5, chans), F32), column_ends(x, info_ref[EVEN_W] > 0)], 0))
    for k, ref in enumerate(out_refs):
        ref[...] = shard_of(pieces, lax.rem(me + k, parts)).astype(BF16)


def row_ends(t, even_h):
    first, last = t[0], t[t.shape[0] - 1]
    return jnp.where(even_h, last, first), jnp.where(even_h, first, last)


def column_ends(t, even_w):
    first, last = t[:, 0, :], t[:, t.shape[1] - 1, :]
    return jnp.concatenate([jnp.where(even_w, last, first), jnp.where(even_w, first, last)], 0)


def tiles_kernel(parts, info_ref, x_ref, w_ref, *out_refs):
    chans = x_ref.shape[2] // parts
    for k in range(parts):
        shard = lax.rem(info_ref[ME] + k, parts)
        out_refs[k][...] = shard_of([x_ref[:, :, s * chans : (s + 1) * chans].astype(F32) for s in range(parts)], shard).astype(BF16)


def rows_kernel(parts, info_ref, *refs):
    packs, cots, (near_ref, across_ref, stats_ref) = refs[:parts], refs[parts : 2 * parts], refs[2 * parts :]
    rows, cols, outs = cots[0].shape
    chans = packs[0].shape[1]
    groups = stats_ref.shape[1] // (2 * parts)
    even_h = info_ref[EVEN_H] > 0
    packs = [ref[...].astype(F32) for ref in packs]
    cot_ends = [row_ends(ref[...].astype(F32), even_h) for ref in cots]
    local = [v[2 * cols : 2 * cols + 3, : 2 * groups] for v in packs]
    terms = jnp.concatenate([v[:, :groups] for v in local] + [v[:, groups:] for v in local], 1)
    stats_ref[...] = terms[0:1] + terms[1:2] + terms[2:3]
    tail = jnp.concatenate([terms, jnp.zeros((3, chans + outs - terms.shape[1]), F32)], 1)
    for half, ref in enumerate((near_ref, across_ref)):
        strips = [jnp.concatenate([v[half * cols : (half + 1) * cols], c[half]], 1) for v, c in zip(packs, cot_ends)]
        ref[...] = jnp.concatenate(strips + ([tail, jnp.zeros((5, chans + outs), F32)] if half == 0 else []), 0).astype(BF16)


def columns_kernel(parts, info_ref, *refs):
    even_w = info_ref[EVEN_W] > 0
    for pack_ref, cot_ref, ref in zip(refs[:parts], refs[parts : 2 * parts], refs[2 * parts + 1 :]):
        rows, cols, _ = cot_ref.shape
        chans = pack_ref.shape[1]
        ref[:, :chans] = pack_ref[...].astype(F32)[2 * cols + 8 :].astype(BF16)
        ref[:, chans:] = column_ends(cot_ref[...].astype(F32), even_w).astype(BF16)


def pack_kernel(parts, rows, cols, info_ref, near_h, across_h, stats_ref, *refs):
    ends, (near_ref, across_ref) = refs[:parts], refs[parts:]
    even_w = info_ref[EVEN_W] > 0
    both = near_ref.shape[1]
    near_rows = near_h[...].astype(F32)
    across_rows = jnp.where((info_ref[UP] > 0) & (info_ref[DOWN] > 0), across_h[...].astype(F32), 0.0)
    columns = [ref[...].astype(F32) for ref in ends]
    stats = jnp.concatenate([p.astype(F32) for p in three_parts(stats_ref[...])], 0)
    stats = jnp.concatenate([stats, jnp.zeros((3, both - stats.shape[1]), F32)], 1)
    for half, ref, pick_last in ((0, near_ref, even_w), (1, across_ref, jnp.logical_not(even_w))):
        corners = []
        for t in (near_rows, across_rows):
            for k in range(parts):
                first, last = t[k * cols : k * cols + 1], t[(k + 1) * cols - 1 : (k + 1) * cols]
                corners.append(jnp.where(pick_last, last, first))
        pieces = [v[half * rows : (half + 1) * rows] for v in columns] + corners + ([stats] if half == 0 else [])
        used = parts * (rows + 2) + (3 if half == 0 else 0)
        if ref.shape[0] > used:
            pieces.append(jnp.zeros((ref.shape[0] - used, both), F32))
        ref[...] = jnp.concatenate(pieces, 0).astype(BF16)


def halos(parts, rows, cols, info_ref, near_h, across_h, near_w, across_w, lanes):
    even_h = info_ref[EVEN_H] > 0
    even_w = info_ref[EVEN_W] > 0
    part = lambda ref, r: ref[:, lanes].astype(F32)[:r]
    a, b = (part(ref, parts * cols) for ref in (near_h, across_h))
    b = jnp.where((info_ref[UP] > 0) & (info_ref[DOWN] > 0), b, 0.0)
    above_all, below_all = jnp.where(even_h, b, a), jnp.where(even_h, a, b)
    c, d = (part(ref, parts * (rows + 2)) for ref in (near_w, across_w))
    before_all, after_all = jnp.where(even_w, d, c), jnp.where(even_w, c, d)

    def strips(k):
        def ordered(t):
            head, tail = t[parts * rows + k :][:1], t[parts * (rows + 1) + k :][:1]
            return jnp.where(even_h, tail, head), t[k * rows : (k + 1) * rows], jnp.where(even_h, head, tail)

        at = slice(k * cols, (k + 1) * cols)
        return above_all[at], below_all[at], ordered(before_all), ordered(after_all)

    return strips


def windows(padded_ref, windows_ref, k_all, cols):
    for kx in range(3):
        view = padded_ref[:, :, kx : kx + cols, :]
        windows_ref[kx] = view.reshape(view.shape[0], k_all * cols, view.shape[3]).astype(BF16)


def backward_kernel(parts, info_ref, *refs):
    tiles, (near_h, across_h, near_w, across_w, w_ref, *_, grad_ref, padded_ref, windows_ref) = refs[:parts], refs[parts:]
    rows, cols, outs = tiles[0].shape
    chans = w_ref.shape[2]
    strips = halos(parts, rows, cols, info_ref, near_h, across_h, near_w, across_w, slice(chans, chans + outs))
    for k in range(parts):
        above, below, before, after = strips(k)
        padded_ref[1 : rows + 1, k, 1 : cols + 1, :] = tiles[k][...].astype(F32)
        padded_ref[0, k, 1 : cols + 1, :] = above
        padded_ref[rows + 1, k, 1 : cols + 1, :] = below
        for at, (top, mid, bottom) in ((0, before), (cols + 1, after)):
            padded_ref[0, k, at : at + 1, :] = top
            padded_ref[1 : rows + 1, k, at, :] = mid
            padded_ref[rows + 1, k, at : at + 1, :] = bottom
    windows(padded_ref, windows_ref, parts, cols)
    taps = [(ky, kx) for ky in range(3) for kx in range(3)]
    shifted = jnp.concatenate([windows_ref[kx, ky : ky + rows].reshape(rows * parts * cols, outs) for ky, kx in taps], 1)
    weight = jnp.concatenate([w_ref[2 - ky, 2 - kx] for ky, kx in taps], 1)
    total = lax.dot_general(weight, shifted, (((1,), (1,)), ((), ())), preferred_element_type=F32)
    grad_ref[...] = total.T.reshape(rows, parts, cols, chans)


def terms_kernel(parts, count, info_ref, *refs):
    tiles = refs[:parts]
    stats_ref, gain_ref, shift_ref, grad_ref = refs[parts : parts + 4]
    moments_refs, (gx_own_ref, gx_other_ref, padded_ref, scales_ref) = refs[parts + 4 : -4], refs[-4:]
    rows, cols, _ = tiles[0].shape
    chans = grad_ref.shape[3]
    groups = stats_ref.shape[1] // (2 * parts)
    stats = jnp.concatenate([stats_ref[:, i * groups : (i + 1) * groups] for i in range(2 * parts)], 0)
    wide = expanded(jnp.concatenate([stats[:parts], lax.rsqrt(stats[parts:] / count + EPS)], 0), chans)
    means, invs = wide[:parts], wide[parts:]
    mine = lambda ref: shard_of([ref[s * chans : (s + 1) * chans].reshape(1, chans) for s in range(parts)], info_ref[ME])
    gain, shift = mine(gain_ref), mine(shift_ref)
    scales_ref[...] = jnp.concatenate([wide, gain, shift], 0)
    firsts, seconds = [], []
    for k in range(parts):
        mean, inv = means[k : k + 1], invs[k : k + 1]
        xhat = (tiles[k][...].astype(F32) - mean[None]) * inv[None]
        z = xhat * gain[None] + shift[None]
        sig = jax.nn.sigmoid(z)
        padded_ref[:, k, 1 : cols + 1, :] = z * sig
        gx = grad_ref[:, k] * sig * (1.0 + z * (1.0 - sig)) * gain[None]
        if k == 0:
            gx_own_ref[...] = gx
        else:
            gx_other_ref[k - 1] = gx.astype(BF16)
        firsts.append(jnp.sum(gx.reshape(rows * cols, chans), axis=0, keepdims=True))
        seconds.append(jnp.sum((gx * xhat).reshape(rows * cols, chans), axis=0, keepdims=True))
    sums = gathered(jnp.concatenate(firsts + seconds, 0), groups)
    for k, ref in enumerate(moments_refs):
        ref[...] = jnp.concatenate([v[k : k + 1] for v in (sums[:parts], sums[parts:], stats[:parts], stats[parts:])], 0)


def forward_kernel(parts, info_ref, given_ref, scales_ref, near_h, across_h, near_w, across_w, w_ref, conv_own_ref, conv_other_ref, windows_ref, padded_ref):
    rows, cols, outs = conv_own_ref.shape
    chans = windows_ref.shape[3]
    strips = halos(parts, rows, cols, info_ref, near_h, across_h, near_w, across_w, slice(0, chans))
    up, down, left, right = (info_ref[i] > 0 for i in (UP, DOWN, LEFT, RIGHT))
    scales = scales_ref[...]
    gain, shift = scales[2 * parts : 2 * parts + 1], scales[2 * parts + 1 : 2 * parts + 2]
    padded_ref[1 : rows + 1] = given_ref[...]
    for k in range(parts):
        mean, inv = scales[k : k + 1], scales[parts + k : parts + k + 1]

        def act_of(t, inside):
            z = (t - mean) * inv * gain + shift
            return jnp.where(inside, z * jax.nn.sigmoid(z), 0.0)

        above, below, before, after = strips(k)
        padded_ref[0, k, 1 : cols + 1, :] = act_of(above, up)
        padded_ref[rows + 1, k, 1 : cols + 1, :] = act_of(below, down)
        for at, (top, mid, bottom), side in ((0, before, left), (cols + 1, after, right)):
            padded_ref[0, k, at : at + 1, :] = act_of(top, side & up)
            padded_ref[1 : rows + 1, k, at, :] = act_of(mid, side)
            padded_ref[rows + 1, k, at : at + 1, :] = act_of(bottom, side & down)
    windows(padded_ref, windows_ref, parts, cols)
    convolved(parts, windows_ref, w_ref, slice(0, outs), conv_own_ref, conv_other_ref)


def second_forward_kernel(parts, start, windows_ref, w_ref, after_ref, conv_own_ref, conv_other_ref):
    convolved(parts, windows_ref, w_ref, slice(start, w_ref.shape[3]), conv_own_ref, conv_other_ref)


def convolved(parts, windows_ref, w_ref, lanes, conv_own_ref, conv_other_ref):
    rows, cols, outs = conv_own_ref.shape
    chans = windows_ref.shape[3]
    taps = [(ky, kx) for ky in range(3) for kx in range(3)]
    shifted = jnp.concatenate([windows_ref[kx, ky : ky + rows].reshape(rows * parts * cols, chans) for ky, kx in taps], 1)
    weight = w_ref[:, :, :, lanes].reshape(9 * chans, outs)
    total = lax.dot_general(weight, shifted, (((0,), (1,)), ((), ())), preferred_element_type=F32).T
    total = total.reshape(rows, parts, cols, outs)
    conv_own_ref[...] = total[:, 0]
    for k in range(1, parts):
        conv_other_ref[k - 1] = total[:, k].astype(BF16)


def finish_kernel(parts, count, info_ref, x_ref, small_ref, sums_ref, bias_ref, gx_own_ref, *refs):
    gx_refs, conv_refs = refs[: parts - 1], refs[parts - 1 : 3 * parts - 1]
    conv_ref, grad_ref = refs[3 * parts - 1 :]
    cin = x_ref.shape[2]
    chans = cin // parts
    start = 0
    for i in range(2):
        conv = sum(r[...].astype(F32) for r in conv_refs[i::2])
        stop = start + conv.shape[2]
        conv_ref[:, :, start:stop] = (conv + bias_ref[start:stop].reshape(1, 1, -1)).astype(BF16)
        start = stop
    wide = []
    for k in range(parts):
        stats = small_ref[k]
        wide.append(jnp.concatenate([stats[2:3], lax.rsqrt(stats[3:4] / count + EPS), sums_ref[k] / count], 0))
    wide = expanded(jnp.concatenate(wide, 0), chans)
    gx_all = [ref[...].astype(F32) for ref in (gx_own_ref, *gx_refs)]
    for s in range(parts):
        at = slice(s * chans, (s + 1) * chans)
        k = lax.rem(s - info_ref[ME] + parts, parts)
        mean, inv, first, second = (shard_of([wide[4 * j + i : 4 * j + i + 1] for j in range(parts)], k)[None] for i in range(4))
        xhat = (x_ref[:, :, at].astype(F32) - mean) * inv
        grad_ref[:, :, at] = (inv * (shard_of(gx_all, k) - first - xhat * second)).astype(BF16)


def call(kernel, name, outs, operands, scratch=(), scalars=True, cost=None):
    spec = lambda i: pl.BlockSpec(memory_space=pltpu.SMEM if scalars and i == 0 else pltpu.VMEM)
    return pl.pallas_call(
        kernel,
        out_shape=outs,
        in_specs=[spec(i) for i in range(len(operands))],
        out_specs=[pl.BlockSpec(memory_space=pltpu.VMEM)] * len(outs),
        scratch_shapes=scratch,
        compiler_params=pltpu.CompilerParams(vmem_limit_bytes=28 * 2**20),
        cost_estimate=cost,
        name=name,
    )(*operands)


def tied(value, *others):
    for other in others:
        value = value + 0.0 * other[0, :1, : value.shape[-1]].astype(F32)
    return value


def stats_rounds(axis):
    count = lax.axis_size(axis)
    if count == 4:
        return [near, lambda i: i ^ 2]
    return [functools.partial(lambda step, i: i ^ step, 2**j) for j in range(count.bit_length() - 1)]


def body(latents, norm_gain, norm_shift, conv_weight, conv_bias, cotangent):
    _, rows, cols, cin = latents.shape
    outs = cotangent.shape[3]
    chans = conv_weight.shape[2]
    parts = lax.axis_size("dp")
    me = lax.axis_index("dp")
    groups = GROUPS * chans // cin
    both = chans + outs
    n = rows * cols * (cin // GROUPS)
    count = float(n * lax.axis_size("ha") * lax.axis_size("wa"))
    x, cot = latents[0], cotangent[0]
    sds = jax.ShapeDtypeStruct
    where = [lax.axis_index(a) for a in ("ha", "wa")]
    last = [lax.axis_size(a) - 1 for a in ("ha", "wa")]
    info = jnp.stack(
        [me, where[0] % 2 == 0, where[1] % 2 == 0, where[0] > 0, where[0] < last[0], where[1] > 0, where[1] < last[1]]
    ).astype(jnp.int32)

    peers = [[(i, (i + k) % parts) for i in range(parts)] for k in range(1, parts)]
    from_peers = lambda values: [lax.ppermute(v, "dp", pairs) for v, pairs in zip(values, peers)]
    cot_tiles = [cot, *from_peers([cot] * (parts - 1))]
    first = call(
        functools.partial(first_kernel, parts, groups),
        "first",
        [sds((2 * (rows + cols) + 8, chans), BF16)] * parts,
        [info, x],
        cost=pl.CostEstimate(flops=10**10, bytes_accessed=1, transcendentals=0),
    )
    got = from_peers(first[1:])
    tiles = call(
        functools.partial(tiles_kernel, parts),
        "tiles",
        [sds((rows, cols, chans), BF16)] * parts,
        [info, x, conv_weight],
    )
    x_tiles = [tiles[0], *from_peers(tiles[1:])]
    size = 2 * parts * groups
    pack_near, pack_across, stats = call(
        functools.partial(rows_kernel, parts),
        "rows",
        [sds((parts * cols + 8, both), BF16), sds((parts * cols, both), BF16), sds((1, size), F32)],
        [info, first[0], *got, *cot_tiles],
    )

    def reduced(stats, n, axis, pairings):
        for partner in pairings:
            stats, n = merged(stats, exchange(stats, axis, partner), n), 2 * n
        return stats, n

    rounds_h, rounds_w = stats_rounds("ha"), stats_rounds("wa")
    near_h = exchange(pack_near, "ha", near)
    ends_w = call(
        functools.partial(columns_kernel, parts),
        "columns",
        [sds((2 * rows, both), BF16)] * parts,
        [info, first[0], *got, *cot_tiles, stats],
    )
    stats, n = merged(stats, unpacked(near_h, parts * cols, size), n), 2 * n
    if lax.axis_size("ha") == 4:
        across_h = exchange(packed([pack_across], stats), "ha", across)
        stats, n = merged(stats, unpacked(across_h, parts * cols, size), n), 2 * n
    else:
        across_h = exchange(pack_across, "ha", across)
        stats, n = reduced(stats, n, "ha", rounds_h[1:])
    used = parts * (rows + 2)
    near_w, across_w = call(
        functools.partial(pack_kernel, parts, rows, cols),
        "pack",
        [sds((-(-(used + 3) // 8) * 8, both), BF16), sds((used, both), BF16)],
        [info, near_h, across_h, stats, *ends_w],
    )
    near_w = exchange(near_w, "wa", near)
    across_w = exchange(across_w, "wa", across, ends=False)
    stats, n = merged(stats, unpacked(near_w, used, size), n), 2 * n
    stats, n = reduced(stats, n, "wa", rounds_w[1:])

    strips = [near_h, across_h, near_w, across_w]
    padded = lambda depth: pltpu.VMEM((rows + 2, parts, cols + 8, depth), F32)
    shifted = (3, rows + 2, parts * cols)
    (grad_act,) = call(
        functools.partial(backward_kernel, parts),
        "conv_backward",
        [sds((rows, parts, cols, chans), F32)],
        [info, *cot_tiles, *strips, conv_weight, *x_tiles[1:]],
        [padded(outs), pltpu.VMEM((*shifted, outs), BF16)],
    )
    *small, gx_own, gx_other, act, scales = call(
        functools.partial(terms_kernel, parts, count),
        "terms",
        [
            *[sds((4, groups), F32)] * parts,
            sds((rows, cols, chans), F32),
            sds((parts - 1, rows, cols, chans), BF16),
            sds((rows, parts, cols + 8, chans), F32),
            sds((2 * parts + 2, chans), F32),
        ],
        [info, *x_tiles, stats, norm_gain, norm_shift, grad_act],
    )

    to_owners = lambda values: [lax.ppermute(v, "dp", [(j, i) for i, j in pairs]) for v, pairs in zip(values, peers)]
    small = jnp.stack([small[0], *to_owners(small[1:])], 0)
    gx = to_owners([gx_other[k] for k in range(parts - 1)])
    start = outs * 3 // 5 // 128 * 128
    parts_of = lambda size: [sds((rows, cols, size), F32), sds((parts - 1, rows, cols, size), BF16)]
    conv_own, conv_other, act_windows = call(
        functools.partial(forward_kernel, parts),
        "conv_forward",
        [*parts_of(start), sds((*shifted, chans), BF16)],
        [info, act, scales, *strips, conv_weight],
        [padded(chans)],
    )
    sums = tied(small[:, :2], conv_own)
    sums = sums + exchange(sums, "ha", rounds_h[0])
    conv_own2, conv_other2 = call(
        functools.partial(second_forward_kernel, parts, start),
        "conv_forward2",
        parts_of(outs - start),
        [act_windows, conv_weight, sums],
        scalars=False,
    )
    conv = [conv_own, conv_own2]
    for k in range(parts - 1):
        back = [(j, i) for i, j in peers[k]]
        conv += [lax.ppermute(v[k], "dp", back) for v in (conv_other, conv_other2)]
    for partner in rounds_h[1:]:
        sums = sums + exchange(sums, "ha", partner)
    sums = tied(sums, conv_own2)
    for partner in rounds_w:
        sums = sums + exchange(sums, "wa", partner)
    conv_out, grad = call(
        functools.partial(finish_kernel, parts, count),
        "finish",
        [sds((rows, cols, outs), BF16), sds((rows, cols, cin), BF16)],
        [info, x, small, sums, conv_bias, gx_own, *gx, *conv],
    )
    return conv_out[None], grad[None]


def solution(mesh):
    tile = P("dp", "ha", "wa", None)
    return jax.shard_map(
        body,
        mesh=mesh,
        in_specs=(tile, P(), P(), P(None, None, "dp", None), P(), tile),
        out_specs=(tile, tile),
        check_vma=False,
    )
```
